32 devices in a mesh: rows: 16 (over z, y, core), cols: 2 (over x).
Axes of the slice: x: 2, y: 2, z: 4, core: 2. Of those that a mesh axis runs over, the one named last changes fastest.
Arguments:
- patches: bfloat16 [8, 160, 40, 256], P(None, 'rows', 'cols'), may hold values from -6 to 6
- target: bfloat16 [8, 160, 40, 256], P(None, 'rows', 'cols'), may hold values from -6 to 6
- kept_mask: int32 [8, 160, 40], P(None, 'rows', 'cols'), may hold values from 0 to 1, as said below
- ln1_gain: float32 [256], replicated, may hold values from 0.5 to 1.5
- ln1_bias: float32 [256], replicated, may hold values from -1.75 to 1.75
- qkv_weight: bfloat16 [256, 768], replicated, may hold values from -0.375 to 0.375
- query_bias: float32 [256], replicated, may hold values from -3 to 3
- value_bias: float32 [256], replicated, may hold values from -3 to 3
- rel_table: float32 [8, 361], replicated, may hold values from -4 to 4
- proj_weight: bfloat16 [256, 256], replicated, may hold values from -1.5 to 1.5
- proj_bias: float32 [256], replicated, may hold values from -1.75 to 1.75
- ln2_gain: float32 [256], replicated, may hold values from 0.5 to 1.5
- ln2_bias: float32 [256], replicated, may hold values from -1.75 to 1.75
- fc1_weight: bfloat16 [256, 1024], replicated, may hold values from -0.375 to 0.375
- fc1_bias: float32 [1024], replicated, may hold values from -3 to 3
- fc2_weight: bfloat16 [1024, 256], replicated, may hold values from -0.1875 to 0.1875
- fc2_bias: float32 [256], replicated, may hold values from -1.75 to 1.75
Outputs:
- output: bfloat16 [8, 160, 40, 256], P(None, 'rows', 'cols')
- patches_grad: float32 [8, 160, 40, 256], P(None, 'rows', 'cols')
- ln1_gain_grad: float32 [256], replicated
- ln1_bias_grad: float32 [256], replicated
- qkv_weight_grad: float32 [256, 768], replicated
- query_bias_grad: float32 [256], replicated
- value_bias_grad: float32 [256], replicated
- rel_table_grad: float32 [8, 361], replicated
- proj_weight_grad: float32 [256, 256], replicated
- proj_bias_grad: float32 [256], replicated
- ln2_gain_grad: float32 [256], replicated
- ln2_bias_grad: float32 [256], replicated
- fc1_weight_grad: float32 [256, 1024], replicated
- fc1_bias_grad: float32 [1024], replicated
- fc2_weight_grad: float32 [1024, 256], replicated
- fc2_bias_grad: float32 [256], replicated
The draws below stay inside these ranges and needn't reach their ends.
Inputs may be any that keep to these rules, and one draw needn't show every extreme that they name: `kept_mask`: 1 marks a patch that counts in the loss; at least one patch is kept.
All inputs are finite; a program needn't handle non-finite values.
Results may differ from the reference program's by a relative error of at most 0.012.
Values may be sent and summed in bfloat16 or wider, within the bound.
No kernel may reach another device: no remote copies, remote signals or barrier semaphores. Data moves between devices by JAX's collectives and lax.ppermute only.
A program may use at most 128 MiB of HBM per device.

```python
import jax
import jax.numpy as jnp
from jax import lax

D = 256
HEADS = 8
HEAD_DIM = 32
FF = 1024
WIN = 10
SHIFT = 5
PAGES = 8
REL = 361
NH = 160
NW = 40


def draw_kept_mask(key, part):
    key = jax.random.fold_in(key, 11)
    random_draw = jax.random.randint(key, (PAGES, NH, NW), 0, 4 * (NH - 1))
    row_index = jnp.arange(NH, dtype=jnp.int32)[None, :, None]
    kept_cells = random_draw < NH - 1 + 2 * row_index
    anchor_cell = (row_index == NH - 1) & (jnp.arange(NW, dtype=jnp.int32)[None, None, :] == 0) & (jnp.arange(PAGES, dtype=jnp.int32)[:, None, None] == 0)
    return (kept_cells | anchor_cell).astype(jnp.int32)


def levels(rng, shape, split, least, largest):
    def one(axis_at, parts):
        heights = jax.random.uniform(jax.random.fold_in(jax.random.fold_in(rng, 6), axis_at), (parts,), jnp.float32, least / len(split), largest / len(split))
        return jnp.repeat(jnp.exp(heights), shape[axis_at] // parts).reshape((-1,) + (1,) * (len(shape) - axis_at - 1))

    loudness = one(*split[0])
    for cut in split[1:]:
        loudness = loudness * one(*cut)
    return loudness


def gaussian(stream_key, shape, deviation, most, pieces=(), held_as=jnp.bfloat16):
    drawn = jax.random.normal(stream_key, shape, jnp.float32) * deviation
    if len(pieces) > 0:
        drawn = levels(stream_key, shape, pieces, -0.22, 0.18) * drawn
    return jnp.clip(drawn, min=-most, max=most).astype(held_as)


def setup_inputs(seed: int = 0) -> dict:
    keys = jax.random.split(jax.random.key(seed), 18)
    patches = gaussian(keys[0], (PAGES, NH, NW, D), 1.0, 6.0, ((1, 16), (2, 2)))
    target = gaussian(keys[1], (PAGES, NH, NW, D), 1.0, 6.0, ((1, 16), (2, 2)))
    kept_mask = draw_kept_mask(jax.random.fold_in(keys[17], 71), 0)
    ln1_gain = jnp.clip(1.0 + 0.1 * jax.random.normal(keys[3], (D,), jnp.float32), 0.5, 1.5)
    ln1_bias = gaussian(keys[4], (D,), 0.3, 1.75, (), jnp.float32)
    qkv_weight = gaussian(keys[5], (D, 3 * D), D ** -0.5, 0.375)
    query_bias = gaussian(keys[6], (D,), 0.5, 3.0, (), jnp.float32)
    value_bias = gaussian(keys[7], (D,), 0.5, 3.0, (), jnp.float32)
    rel_table = gaussian(keys[8], (HEADS, REL), 1.0, 4.0, (), jnp.float32)
    proj_weight = gaussian(keys[9], (D, D), (D // 16) ** -0.5, 1.5)
    proj_bias = gaussian(keys[10], (D,), 0.3, 1.75, (), jnp.float32)
    ln2_gain = jnp.clip(1.0 + 0.1 * jax.random.normal(keys[11], (D,), jnp.float32), 0.5, 1.5)
    ln2_bias = gaussian(keys[12], (D,), 0.3, 1.75, (), jnp.float32)
    fc1_weight = gaussian(keys[13], (D, FF), D ** -0.5, 0.375)
    fc1_bias = gaussian(keys[14], (FF,), 0.5, 3.0, (), jnp.float32)
    fc2_weight = gaussian(keys[15], (FF, D), FF ** -0.5, 0.1875)
    fc2_bias = gaussian(keys[16], (D,), 0.3, 1.75, (), jnp.float32)
    return {"patches": patches, "target": target, "kept_mask": kept_mask, "ln1_gain": ln1_gain, "ln1_bias": ln1_bias, "qkv_weight": qkv_weight, "query_bias": query_bias, "value_bias": value_bias, "rel_table": rel_table, "proj_weight": proj_weight, "proj_bias": proj_bias, "ln2_gain": ln2_gain, "ln2_bias": ln2_bias, "fc1_weight": fc1_weight, "fc1_bias": fc1_bias, "fc2_weight": fc2_weight, "fc2_bias": fc2_bias}


EPS = 1e-05
HIGH = lax.Precision.HIGHEST

@jax.custom_vjp
def low(v):
    return lax.optimization_barrier(v.astype(jnp.bfloat16)).astype(jnp.float32)

@jax.custom_vjp
def low_back(v):
    return v

def low_keep(v):
    return (low(v), None)

def low_pass(kept, grad):
    return (grad,)

def back_keep(v):
    return (v, None)

def back_low(kept, grad):
    return (low(grad),)
low.defvjp(low_keep, low_pass)
low_back.defvjp(back_keep, back_low)

def region_labels(extent):
    position = jnp.arange(extent)
    return (position >= extent - WIN).astype(jnp.int32) + (position >= extent - SHIFT).astype(jnp.int32)

def windowed(field):
    height, width, chans = field.shape
    blocks = field.reshape(height // WIN, WIN, width // WIN, WIN, chans)
    return blocks.transpose(0, 2, 1, 3, 4).reshape(-1, WIN * WIN, chans)

def unwindowed(field, height, width):
    chans = field.shape[-1]
    blocks = field.reshape(height // WIN, width // WIN, WIN, WIN, chans)
    return blocks.transpose(0, 2, 1, 3, 4).reshape(height, width, chans)

def relative_index():
    place = jnp.arange(WIN * WIN)
    row_pos = place // WIN
    col_pos = place % WIN
    row_off = row_pos[:, None] - row_pos[None, :] + WIN - 1
    col_off = col_pos[:, None] - col_pos[None, :] + WIN - 1
    return (row_off * (2 * WIN - 1) + col_off).astype(jnp.int32)

def layer_norm(field, gain, bias):
    center = field - lax.optimization_barrier(jnp.mean(field, -1, keepdims=True))
    inv_std = lax.rsqrt(lax.optimization_barrier(jnp.mean(center * center, -1, keepdims=True)) + EPS)
    return center * inv_std * gain + bias

def matmul_high(left, right):
    return jnp.dot(left, right, precision=HIGH, preferred_element_type=jnp.float32)

def page_layer(page, params):
    ln1_gain, ln1_bias, qkv_weight, query_bias, value_bias, rel_table, proj_weight, proj_bias, ln2_gain, ln2_bias, fc1_weight, fc1_bias, fc2_weight, fc2_bias = params
    height, width, _ = page.shape
    shifted = jnp.roll(page, (-SHIFT, -SHIFT), (0, 1))
    inputs = windowed(shifted)
    wins = inputs.shape[0]
    length = WIN * WIN
    attn_in = low(layer_norm(inputs, ln1_gain, ln1_bias))
    projected = matmul_high(attn_in, qkv_weight)
    queries = low_back(low(projected[..., :D] + query_bias)).reshape(wins, length, HEADS, HEAD_DIM)
    keys_all = low_back(low(projected[..., D:2 * D])).reshape(wins, length, HEADS, HEAD_DIM)
    values = low_back(low(projected[..., 2 * D:] + value_bias)).reshape(wins, length, HEADS, HEAD_DIM)
    logits = low_back(jnp.einsum('wihd,wjhd->whij', queries, keys_all, precision=HIGH))
    labels = region_labels(height)[:, None] * 3 + region_labels(width)[None, :]
    label_win = windowed(labels[:, :, None])[..., 0]
    region_mask = jnp.where(label_win[:, :, None] == label_win[:, None, :], 0.0, -100.0).astype(jnp.float32)
    rel_bias = rel_table[:, relative_index()]
    scores = logits * HEAD_DIM ** (-0.5) + rel_bias[None] + region_mask[:, None]
    probs = low(jax.nn.softmax(scores, -1))
    mixed = jnp.einsum('whij,wjhd->wihd', probs, values, precision=HIGH).reshape(wins, length, D)
    mixed = low_back(low(mixed))
    branch = low_back(matmul_high(mixed, proj_weight) + proj_bias)
    resid = inputs + branch
    mlp_in = low(layer_norm(resid, ln2_gain, ln2_bias))
    pre_act = low_back(matmul_high(mlp_in, fc1_weight) + fc1_bias)
    hidden = low(jax.nn.gelu(pre_act, approximate=False))
    result = resid + low_back(matmul_high(hidden, fc2_weight) + fc2_bias)
    return jnp.roll(unwindowed(result, height, width), (SHIFT, SHIFT), (0, 1))

def reference(patches, target, kept_mask, ln1_gain, ln1_bias, qkv_weight, query_bias, value_bias, rel_table, proj_weight, proj_bias, ln2_gain, ln2_bias, fc1_weight, fc1_bias, fc2_weight, fc2_bias):
    params = (ln1_gain.astype(jnp.float32), ln1_bias.astype(jnp.float32), qkv_weight.astype(jnp.float32), query_bias.astype(jnp.float32), value_bias.astype(jnp.float32), rel_table.astype(jnp.float32), proj_weight.astype(jnp.float32), proj_bias.astype(jnp.float32), ln2_gain.astype(jnp.float32), ln2_bias.astype(jnp.float32), fc1_weight.astype(jnp.float32), fc1_bias.astype(jnp.float32), fc2_weight.astype(jnp.float32), fc2_bias.astype(jnp.float32))
    inputs = patches.astype(jnp.float32)

    def forward(field, weights):
        return lax.map(jax.checkpoint(lambda page: page_layer(page, weights)), field)
    result, pull = jax.vjp(forward, inputs, params)
    kept_float = kept_mask.astype(jnp.float32)
    kept_total = jnp.sum(kept_float)
    cotangent = kept_float[..., None] * target.astype(jnp.float32) * (PAGES * NH * NW / kept_total)
    input_grad, grads = pull(cotangent)
    return (result.astype(jnp.bfloat16), input_grad, grads[0], grads[1], grads[2], grads[3], grads[4], grads[5], grads[6], grads[7], grads[8], grads[9], grads[10], grads[11], grads[12], grads[13])
```

```python
import math

import jax
import jax.numpy as jnp
from jax import lax
from jax.experimental import pallas as pl
from jax.experimental.pallas import tpu as pltpu
from jax.sharding import PartitionSpec as P

WIN = 10
SHIFT = 5
EPS = 1e-05
HIGH = lax.Precision.HIGHEST
F32 = jnp.float32
BF16 = jnp.bfloat16

SPAN = 2 * WIN - 1
TOK = WIN * WIN
ROWS = 104
KEYS = 128
GROUP = 4
RELS = 384
NEVER = -1e30
VMEM_LIMIT = 60 * 1024 * 1024


def dot(a, b):
    return lax.dot_general(a, b, (((1,), (0,)), ((), ())), preferred_element_type=F32)


def dot_bt(a, b):
    return lax.dot_general(a, b, (((1,), (1,)), ((), ())), preferred_element_type=F32)


def dot_at(a, b):
    return lax.dot_general(a, b, (((0,), (0,)), ((), ())), preferred_element_type=F32)


def normalize(x):
    center = x - jnp.sum(x, -1, keepdims=True) * (1.0 / x.shape[-1])
    inv = lax.rsqrt(jnp.sum(center * center, -1, keepdims=True) * (1.0 / x.shape[-1]) + EPS)
    return center * inv, inv


def norm_back(up, normed, inv):
    scale = 1.0 / up.shape[-1]
    mean_up = jnp.sum(up, -1, keepdims=True) * scale
    mean_un = jnp.sum(up * normed, -1, keepdims=True) * scale
    return inv * (up - mean_up - normed * mean_un)


def fold(x):
    return jnp.sum(x.reshape(x.shape[0] // 8, 8, x.shape[1]), 0)


def gather_windows(raster, windows, own, low, right, corner):
    for r in range(WIN):
        if r < WIN - SHIFT:
            main, side = own[0, r + SHIFT], right[0, r]
        else:
            main, side = low[0, r - SHIFT], corner[0, r - SHIFT]
        raster[r, 0 : 2 * WIN, :] = main.astype(F32)
        raster[r, 2 * WIN : 2 * WIN + SHIFT, :] = side.astype(F32)
    for r in range(WIN):
        for w in range(2):
            at = SHIFT + w * WIN
            windows[w * ROWS + r * WIN : w * ROWS + (r + 1) * WIN, :] = raster[r, at : at + WIN, :]


def scatter_windows(raster, windows, out):
    for r in range(WIN):
        for w in range(2):
            raster[r, w * WIN : (w + 1) * WIN, :] = windows[
                w * ROWS + r * WIN : w * ROWS + (r + 1) * WIN, :
            ]
    for r in range(WIN):
        out[0, r] = raster[r, 0 : 2 * WIN, :].astype(out.dtype)


def head_masks(rows, dtype):
    lane = lax.broadcasted_iota(jnp.int32, (rows, KEYS), 1)
    width = KEYS // GROUP
    return [
        ((lane >= k * width) & (lane < (k + 1) * width)).astype(F32).astype(dtype)
        for k in range(GROUP)
    ]


def split_rows(x):
    high = x.astype(BF16)
    return high, (x - high.astype(F32)).astype(BF16)


def forward_kernel(
    own, low, right, corner, t_own, t_low, t_right, t_corner, count,
    qkv_w, proj_w, fc1_w, fc2_w, bias,
    g1, b1, qb, vb, pb, g2, b2, f1b, f2b,
    frame_out, xw_out, qkv_out, p_out, dy_out, do_out, sums_out,
    raster, xw, tw, rw, fc1_acc, fc2_acc, proj_acc, fc1_sum, small_sum,
):
    page = pl.program_id(0)

    @pl.when(page == 0)
    def _():
        for buf in (xw, tw, rw, fc1_acc, fc2_acc, proj_acc, fc1_sum, small_sum):
            buf[...] = jnp.zeros_like(buf)

    d = g1.shape[-1]
    heads = d // (KEYS // GROUP)
    scale = (d // heads) ** (-0.5)
    gather_windows(raster, xw, own, low, right, corner)
    gather_windows(raster, tw, t_own, t_low, t_right, t_corner)
    x = xw[...]
    xw_out[0] = x.astype(BF16)
    normed, _ = normalize(x)
    attn_in = (normed * g1[...] + b1[...]).astype(BF16)
    proj = dot(attn_in, qkv_w[...])
    q_all = proj[:, :d] + qb[...]
    k_all = proj[:, d : 2 * d]
    v_all = proj[:, 2 * d :] + vb[...]
    masks = head_masks(KEYS, BF16)
    filler = jnp.zeros((KEYS - ROWS, d), F32)
    mixed = []
    for w in range(2):
        rows = slice(w * ROWS, (w + 1) * ROWS)
        q = jnp.concatenate([q_all[rows], filler], 0).astype(BF16)
        k = jnp.concatenate([k_all[rows], filler], 0).astype(BF16)
        v = jnp.concatenate([v_all[rows], filler], 0).astype(BF16)
        qkv_out[w, :, :d] = q
        qkv_out[w, :, d : 2 * d] = k
        qkv_out[w, :, 2 * d :] = v
        parts = []
        for g in range(heads // GROUP):
            lanes = slice(g * KEYS, (g + 1) * KEYS)
            kg, vg = k[:, lanes], v[:, lanes]
            k_stack = jnp.concatenate([kg * m for m in masks], 0)
            v_stack = jnp.concatenate([vg * m for m in masks], 0)
            wide = slice(g * GROUP * KEYS, (g + 1) * GROUP * KEYS)
            s = dot_bt(q[:ROWS, lanes], k_stack) * scale + bias[w, :, wide]
            probs = []
            for h in range(GROUP):
                sh = s[:, h * KEYS : (h + 1) * KEYS]
                e = jnp.exp(sh - jnp.max(sh, -1, keepdims=True))
                probs.append(e * (1.0 / jnp.sum(e, -1, keepdims=True)))
            p = jnp.concatenate(probs, 1).astype(BF16)
            p_out[w, :, wide] = p
            parts.append(dot(p, v_stack))
        mixed.append(jnp.concatenate(parts, 1))
    o = jnp.concatenate(mixed, 0).astype(BF16)
    y = x + dot(o, proj_w[...]) + pb[...]
    normed2, inv2 = normalize(y)
    c = (normed2 * g2[...] + b2[...]).astype(BF16)
    h = dot(c, fc1_w[...]) + f1b[...]
    e = jnp.exp(h * h * -0.5)
    phi = 0.5 * (1.0 + lax.erf(h * math.sqrt(0.5)))
    gelu = (h * phi).astype(BF16)
    slope = phi + h * e * (1.0 / math.sqrt(2.0 * math.pi))
    rw[...] = y + dot(gelu, fc2_w[...]) + f2b[...]
    scatter_windows(raster, rw, frame_out)

    dr = tw[...]
    drb = dr.astype(BF16)
    dh = (dot_bt(drb, fc2_w[...]) * slope).astype(BF16)
    fc2_acc[...] += dot_at(drb, gelu)
    fc1_acc[...] += dot_at(c, dh)
    dc = dot_bt(dh, fc1_w[...])
    dy = dr + norm_back(dc * g2[...], normed2, inv2)
    dz = dy.astype(BF16)
    proj_acc[...] += dot_at(o, dz)
    do = dot_bt(dz, proj_w[...])
    for w in range(2):
        do_out[w] = do[w * ROWS : (w + 1) * ROWS].astype(BF16)
    dy_out[0] = dy
    fc1_sum[...] += fold(dh.astype(F32))
    small_sum[0] += fold(dc * normed2)
    small_sum[1] += fold(dc)
    small_sum[2] += fold(dr)
    small_sum[3] += fold(dz.astype(F32))

    @pl.when(page == pl.num_programs(0) - 1)
    def _():
        ff = fc1_w.shape[1] // d
        for j in range(ff):
            sums_out[j * d : (j + 1) * d, :] = fc1_acc[:, j * d : (j + 1) * d].astype(BF16)
            sums_out[(ff + j) * d : (ff + j + 1) * d, :] = fc2_acc[:, j * d : (j + 1) * d].T.astype(
                BF16
            )
        at = 2 * ff * d
        sums_out[at : at + d, :] = proj_acc[...].astype(BF16)
        rows = [jnp.sum(fc1_sum[:, j * d : (j + 1) * d], 0, keepdims=True) for j in range(ff)]
        rows += [jnp.sum(small_sum[k], 0, keepdims=True) for k in range(4)]
        rows.append(jnp.full((1, d), count[0], F32))
        rows.append(jnp.zeros((16 - len(rows), d), F32))
        high, low_part = split_rows(jnp.concatenate(rows, 0))
        at += d
        sums_out[at : at + 16, :] = high
        sums_out[at + 16 : at + 32, :] = low_part
        if sums_out.shape[0] > at + 32:
            sums_out[at + 32 :, :] = jnp.zeros((sums_out.shape[0] - at - 32, d), BF16)


def backward_kernel(
    xw, qkv, p_in, dy_in, do_in, qkv_w, g1, b1, hot,
    frame_out, sums_out,
    raster, dxw, qkv_acc, rel_acc, col_sum, small_sum,
):
    page = pl.program_id(0)

    @pl.when(page == 0)
    def _():
        for buf in (qkv_acc, rel_acc, col_sum, small_sum):
            buf[...] = jnp.zeros_like(buf)

    d = g1.shape[-1]
    heads = d // (KEYS // GROUP)
    scale = (d // heads) ** (-0.5)
    masks = head_masks(KEYS, BF16)
    row_masks = head_masks(ROWS, F32)
    dqs, dks, dvs = [], [], []
    for w in range(2):
        q = qkv[w, :, :d]
        k = qkv[w, :, d : 2 * d]
        v = qkv[w, :, 2 * d :]
        do = do_in[w]
        dq, dk, dv = [], [], []
        for g in range(heads // GROUP):
            lanes = slice(g * KEYS, (g + 1) * KEYS)
            kg, vg = k[:, lanes], v[:, lanes]
            k_stack = jnp.concatenate([kg * m for m in masks], 0)
            v_stack = jnp.concatenate([vg * m for m in masks], 0)
            dog = do[:, lanes]
            qf = q[:, lanes].astype(F32)[:ROWS]
            dof = dog.astype(F32)
            q_stack = jnp.concatenate([qf * m for m in row_masks], 0).astype(BF16)
            do_stack = jnp.concatenate([dof * m for m in row_masks], 0).astype(BF16)
            wide = slice(g * GROUP * KEYS, (g + 1) * GROUP * KEYS)
            dp = dot_bt(dog, v_stack)
            p = p_in[w, :, wide].astype(F32)
            t = p * dp
            ds = []
            for h in range(GROUP):
                at = slice(h * KEYS, (h + 1) * KEYS)
                th = t[:, at]
                ds.append(th - p[:, at] * jnp.sum(th, -1, keepdims=True))
            for h in range(GROUP):
                at = (g * GROUP + h) * KEYS
                rel_acc[:, at : at + KEYS] += ds[h]
            dts = [x * scale for x in ds]
            dt = jnp.concatenate(dts, 1).astype(BF16)
            dt_stack = jnp.concatenate(dts, 0).astype(BF16)
            p_stack = jnp.concatenate(
                [p[:, h * KEYS : (h + 1) * KEYS] for h in range(GROUP)], 0
            ).astype(BF16)
            dq.append(dot(dt, k_stack))
            dk.append(dot_at(dt_stack, q_stack)[:ROWS])
            dv.append(dot_at(p_stack, do_stack)[:ROWS])
        dqs.append(jnp.concatenate(dq, 1))
        dks.append(jnp.concatenate(dk, 1))
        dvs.append(jnp.concatenate(dv, 1))
    joined = jnp.concatenate(
        [jnp.concatenate(dqs, 0), jnp.concatenate(dks, 0), jnp.concatenate(dvs, 0)], 1
    ).astype(BF16)
    normed, inv = normalize(xw[0].astype(F32))
    attn_in = (normed * g1[...] + b1[...]).astype(BF16)
    qkv_acc[...] += dot_at(attn_in, joined)
    col_sum[...] += fold(joined.astype(F32))
    da = dot_bt(joined, qkv_w[...])
    small_sum[0] += fold(da * normed)
    small_sum[1] += fold(da)
    dxw[...] = dy_in[0] + norm_back(da * g1[...], normed, inv)
    scatter_windows(raster, dxw, frame_out)

    @pl.when(page == pl.num_programs(0) - 1)
    def _():
        for j in range(3):
            sums_out[j * d : (j + 1) * d, :] = qkv_acc[:, j * d : (j + 1) * d].astype(BF16)
        stack = jnp.concatenate([rel_acc[:, h * KEYS : (h + 1) * KEYS] for h in range(heads)], 0)
        high, rest = split_rows(stack)
        u = dot(high, hot[...]) + dot(rest, hot[...])
        row = lax.broadcasted_iota(jnp.int32, (ROWS, RELS), 0)
        place = row
        for k in range(1, WIN):
            place = place + jnp.where(row >= k * WIN, WIN - 1, 0)
        place = jnp.concatenate([place] * heads, 0)
        for bit in range(8):
            moved = pltpu.roll(u, 1 << bit, 1)
            u = jnp.where((place & (1 << bit)) != 0, moved, u)
        rel = jnp.concatenate(
            [jnp.sum(u[h * ROWS : (h + 1) * ROWS], 0, keepdims=True) for h in range(heads)], 0
        )
        rows = [jnp.sum(small_sum[k], 0, keepdims=True) for k in range(2)]
        rows.append(jnp.sum(col_sum[:, :d], 0, keepdims=True))
        rows.append(jnp.sum(col_sum[:, 2 * d :], 0, keepdims=True))
        rows.append(jnp.zeros((4, d), F32))
        rows.append(rel[:, :d])
        rows.append(jnp.concatenate([rel[:, d:], jnp.zeros((heads, 2 * d - RELS), F32)], 1))
        rows.append(jnp.zeros((8, d), F32))
        high, rest = split_rows(jnp.concatenate(rows, 0))
        at = 3 * d
        sums_out[at : at + 32, :] = high
        sums_out[at + 32 : at + 64, :] = rest
        if sums_out.shape[0] > at + 64:
            sums_out[at + 64 :, :] = jnp.zeros((sums_out.shape[0] - at - 64, d), BF16)


def finish_forward_kernel(total, sums, fc1, fc2, proj, smalls, scale_out):
    d = proj.shape[0]
    ff = fc1.shape[1] // d
    at = (2 * ff + 1) * d
    rows = sums[at : at + 16, :].astype(F32) + sums[at + 16 : at + 32, :].astype(F32)
    scale = total / rows[ff + 4 : ff + 5, :]
    smalls[...] = rows * scale
    scale_out[...] = scale
    for j in range(ff):
        fc1[:, j * d : (j + 1) * d] = sums[j * d : (j + 1) * d, :].astype(F32) * scale
        fc2[j * d : (j + 1) * d, :] = sums[(ff + j) * d : (ff + j + 1) * d, :].astype(F32) * scale
    proj[...] = sums[2 * ff * d : (2 * ff + 1) * d, :].astype(F32) * scale


def finish_backward_kernel(sums, scale_in, qkv, smalls):
    d = scale_in.shape[1]
    scale = scale_in[...]
    for j in range(3):
        qkv[:, j * d : (j + 1) * d] = sums[j * d : (j + 1) * d, :].astype(F32) * scale
    at = 3 * d
    rows = sums[at : at + 32, :].astype(F32) + sums[at + 32 : at + 64, :].astype(F32)
    smalls[...] = rows * scale


def permute(block, target):
    rows, cols = lax.axis_size("rows"), lax.axis_size("cols")
    route = []
    for r in range(rows):
        for c in range(cols):
            tr, tc = target(r, c)
            route.append((r * cols + c, (tr % rows) * cols + tc % cols))
    return lax.ppermute(block, ("rows", "cols"), route)


def flip_by(parts, index):
    stack = jnp.stack(parts, 0)
    n = len(parts)
    bit = 1
    while bit < n:
        view = stack.reshape((n // (2 * bit), 2, bit) + stack.shape[1:])
        view = jnp.where((index & bit) != 0, view[:, ::-1], view)
        stack = view.reshape(stack.shape)
        bit *= 2
    return stack


def tree_sum(parts):
    parts = [p.astype(F32) for p in parts]
    while len(parts) > 1:
        parts = [parts[i] + parts[i + 1] for i in range(0, len(parts), 2)]
    return parts[0].astype(BF16)


def sum_over_devices(x):
    rows, cols = lax.axis_size("rows"), lax.axis_size("cols")
    r, c = lax.axis_index("rows"), lax.axis_index("cols")
    planes = 2 * cols
    depth = rows // 4
    n, d = x.shape
    core = r & 1
    spot = ((r >> 1) & 1) * cols + c
    halves = x.reshape(2, n // 2, d)
    mine = lax.dynamic_index_in_dim(halves, core, 0, False)
    other = permute(
        lax.dynamic_index_in_dim(halves, 1 - core, 0, False), lambda r, c: (r ^ 1, c)
    )
    half = tree_sum([mine, other]).reshape(planes, n // (2 * planes), d)

    def plane_hop(k):
        return lambda r, c: (r ^ (2 * (k // cols)), c ^ (k % cols))

    got = [lax.dynamic_index_in_dim(half, spot, 0, False)]
    for k in range(1, planes):
        got.append(permute(lax.dynamic_index_in_dim(half, spot ^ k, 0, False), plane_hop(k)))
    piece = tree_sum(got)
    got = [piece]
    for k in range(1, depth):
        got.append(permute(piece, lambda r, c, k=k: (r ^ (4 * k), c)))
    piece = tree_sum(got)
    got = [piece]
    for k in range(1, planes):
        got.append(permute(piece, plane_hop(k)))
    half = flip_by(got, spot).reshape(n // 2, d)
    other = permute(half, lambda r, c: (r ^ 1, c))
    return flip_by([half, other], core).reshape(n, d)


def strips(field):
    low = permute(field[:, :SHIFT], lambda r, c: (r - 1, c))
    right = permute(field[:, SHIFT:, :SHIFT], lambda r, c: (r, c - 1))
    corner = permute(field[:, :SHIFT, :SHIFT], lambda r, c: (r - 1, c - 1))
    return low, right, corner


def leave(field, scale=None):
    upper = permute(field[:, SHIFT:, :-SHIFT].astype(BF16), lambda r, c: (r + 1, c))
    left = permute(field[:, :SHIFT, -SHIFT:].astype(BF16), lambda r, c: (r, c + 1))
    corner = permute(field[:, SHIFT:, -SHIFT:].astype(BF16), lambda r, c: (r + 1, c + 1))
    dtype = field.dtype
    top = jnp.concatenate([corner.astype(dtype), upper.astype(dtype)], 2)
    low = jnp.concatenate([left.astype(dtype), field[:, :SHIFT, :-SHIFT]], 2)
    whole = jnp.concatenate([top, low], 1)
    return whole if scale is None else whole * scale


def region_labels(height, width):
    rows_all = height * lax.axis_size("rows")
    cols_all = width * lax.axis_size("cols")
    row = lax.axis_index("rows") * height + jnp.arange(height, dtype=jnp.int32)
    col = lax.axis_index("cols") * width + jnp.arange(width, dtype=jnp.int32)
    row_region = (row >= rows_all - WIN).astype(jnp.int32) + (row >= rows_all - SHIFT).astype(
        jnp.int32
    )
    col_region = (col >= cols_all - WIN).astype(jnp.int32) + (col >= cols_all - SHIFT).astype(
        jnp.int32
    )
    return row_region[:, None] * 3 + col_region[None, :]


def attention_bias(rel_table, height, width):
    heads = rel_table.shape[0]
    offsets = jnp.arange(WIN)[:, None] - jnp.arange(WIN)[None, :] + WIN - 1
    hots = (offsets[:, :, None] == jnp.arange(SPAN)[None, None, :]).astype(F32)
    grid = rel_table.reshape(heads, SPAN, SPAN)
    rel = jnp.einsum("hab,ija,klb->ikhjl", grid, hots, hots, precision=HIGH).reshape(
        TOK, heads, TOK
    )
    labels = region_labels(height, width).reshape(WIN, width // WIN, WIN)
    labels = labels.transpose(1, 0, 2).reshape(width // WIN, TOK)
    mask = jnp.where(labels[:, :, None] == labels[:, None, :], 0.0, -100.0).astype(F32)
    full = rel[None] + mask[:, :, None, :]
    full = jnp.pad(
        full, ((0, 0), (0, ROWS - TOK), (0, 0), (0, KEYS - TOK)), constant_values=NEVER
    )
    return full.reshape(width // WIN, ROWS, heads * KEYS)


def whole(a):
    return pl.BlockSpec(a.shape, lambda i: (0,) * len(a.shape), pipeline_mode=pl.Buffered(1))


def paged(shape, count=1):
    return pl.BlockSpec((count,) + shape[1:], lambda i: (i,) + (0,) * (len(shape) - 1))


def held(shape):
    return pl.BlockSpec(shape, lambda i: (0,) * len(shape))


def shards(
    patches, target, kept_mask, ln1_gain, ln1_bias, qkv_weight, query_bias, value_bias, rel_table,
    proj_weight, proj_bias, ln2_gain, ln2_bias, fc1_weight, fc1_bias, fc2_weight, fc2_bias,
):
    pages, height, width, d = patches.shape
    heads = rel_table.shape[0]
    ff = fc1_weight.shape[1]
    rows, cols = lax.axis_size("rows"), lax.axis_size("cols")
    step = 64 * cols
    params = pltpu.CompilerParams(
        dimension_semantics=("arbitrary",), vmem_limit_bytes=VMEM_LIMIT
    )

    p_strips = strips(patches)
    masked = target * kept_mask.astype(BF16)[..., None]
    t_strips = strips(masked)
    count = jnp.sum(kept_mask.astype(F32)).reshape(1)
    bias = attention_bias(rel_table, height, width)
    vec = lambda a: a.reshape(1, -1)

    paged_in = [patches, *p_strips, masked, *t_strips]
    weights = [qkv_weight, proj_weight, fc1_weight, fc2_weight, bias]
    vectors = [
        vec(a)
        for a in (
            ln1_gain, ln1_bias, query_bias, value_bias, proj_bias, ln2_gain, ln2_bias, fc1_bias,
            fc2_bias,
        )
    ]
    n1 = -(-(2 * ff + d + 32) // step) * step
    n2 = -(-(3 * d + 64) // step) * step
    outs = [
        jax.ShapeDtypeStruct((pages, height, width, d), BF16),
        jax.ShapeDtypeStruct((pages, 2 * ROWS, d), BF16),
        jax.ShapeDtypeStruct((2 * pages, KEYS, 3 * d), BF16),
        jax.ShapeDtypeStruct((2 * pages, ROWS, heads * KEYS), BF16),
        jax.ShapeDtypeStruct((pages, 2 * ROWS, d), F32),
        jax.ShapeDtypeStruct((2 * pages, ROWS, d), BF16),
        jax.ShapeDtypeStruct((n1, d), BF16),
    ]
    frame, xw, qkv, probs, dy, do, sums1 = pl.pallas_call(
        forward_kernel,
        grid=(pages,),
        in_specs=[paged(a.shape) for a in paged_in]
        + [pl.BlockSpec(memory_space=pltpu.SMEM)]
        + [whole(a) for a in weights + vectors],
        out_specs=[
            paged(outs[0].shape), paged(outs[1].shape), paged(outs[2].shape, 2),
            paged(outs[3].shape, 2), paged(outs[4].shape), paged(outs[5].shape, 2),
            held(outs[6].shape),
        ],
        out_shape=outs,
        scratch_shapes=[
            pltpu.VMEM((WIN, 32, d), F32),
            pltpu.VMEM((2 * ROWS, d), F32),
            pltpu.VMEM((2 * ROWS, d), F32),
            pltpu.VMEM((2 * ROWS, d), F32),
            pltpu.VMEM((d, ff), F32),
            pltpu.VMEM((d, ff), F32),
            pltpu.VMEM((d, d), F32),
            pltpu.VMEM((8, ff), F32),
            pltpu.VMEM((4, 8, d), F32),
        ],
        compiler_params=params,
        name="forward_and_mlp_backward",
    )(*paged_in, count, *weights, *vectors)

    total1 = sum_over_devices(sums1)
    output = leave(frame)

    place = jnp.arange(KEYS)
    spot = (SPAN * (WIN - 1) + WIN - 1) - (place // WIN * SPAN + place % WIN)
    hot = ((spot[:, None] == jnp.arange(RELS)[None, :]) & (place < TOK)[:, None]).astype(BF16)
    outs = [
        jax.ShapeDtypeStruct((pages, height, width, d), F32),
        jax.ShapeDtypeStruct((n2, d), BF16),
    ]
    grad_frame, sums2 = pl.pallas_call(
        backward_kernel,
        grid=(pages,),
        in_specs=[
            paged(xw.shape), paged(qkv.shape, 2), paged(probs.shape, 2), paged(dy.shape),
            paged(do.shape, 2),
        ]
        + [whole(a) for a in (qkv_weight, vectors[0], vectors[1], hot)],
        out_specs=[paged(outs[0].shape), held(outs[1].shape)],
        out_shape=outs,
        scratch_shapes=[
            pltpu.VMEM((WIN, 32, d), F32),
            pltpu.VMEM((2 * ROWS, d), F32),
            pltpu.VMEM((d, 3 * d), F32),
            pltpu.VMEM((ROWS, heads * KEYS), F32),
            pltpu.VMEM((8, 3 * d), F32),
            pltpu.VMEM((2, 8, d), F32),
        ],
        compiler_params=params,
        name="attention_backward",
    )(xw, qkv, probs, dy, do, qkv_weight, vectors[0], vectors[1], hot)

    total2 = sum_over_devices(sums2)
    total = float(pages * height * rows * width * cols)
    outs = [
        jax.ShapeDtypeStruct(s, F32) for s in ((d, ff), (ff, d), (d, d), (16, d), (1, d))
    ]
    fc1_grad, fc2_grad, proj_grad, smalls1, scale = pl.pallas_call(
        lambda *refs: finish_forward_kernel(total, *refs),
        out_shape=outs,
        compiler_params=pltpu.CompilerParams(vmem_limit_bytes=VMEM_LIMIT),
        name="finish_mlp_sums",
    )(total1)
    outs = [jax.ShapeDtypeStruct(s, F32) for s in ((d, 3 * d), (32, d))]
    qkv_grad, smalls2 = pl.pallas_call(
        finish_backward_kernel,
        out_shape=outs,
        compiler_params=pltpu.CompilerParams(vmem_limit_bytes=VMEM_LIMIT),
        name="finish_attention_sums",
    )(total2, scale)
    patches_grad = leave(grad_frame, scale[0, 0])
    k = ff // d
    rel = jnp.concatenate([smalls2[8 : 8 + heads], smalls2[16 : 16 + heads]], 1)
    rel_grad = rel[:, : SPAN * SPAN]
    return (
        output,
        patches_grad,
        smalls2[0],
        smalls2[1],
        qkv_grad,
        smalls2[2],
        smalls2[3],
        rel_grad,
        proj_grad,
        smalls1[k + 3],
        smalls1[k],
        smalls1[k + 1],
        fc1_grad,
        smalls1[:k].reshape(ff),
        fc2_grad,
        smalls1[k + 2],
    )


def solution(mesh):
    field = P(None, "rows", "cols", None)
    return jax.shard_map(
        shards,
        mesh=mesh,
        in_specs=(field, field, P(None, "rows", "cols")) + (P(),) * 14,
        out_specs=(field, field) + (P(),) * 14,
        check_vma=False,
    )
```

```python
import math

import jax
import jax.numpy as jnp
from jax import lax
from jax.experimental import pallas as pl
from jax.experimental.pallas import tpu as pltpu
from jax.sharding import PartitionSpec as P

WIN = 10
SHIFT = 5
EPS = 1e-05
F32 = jnp.float32
BF16 = jnp.bfloat16

SPAN = 2 * WIN - 1
TOK = WIN * WIN
ROWS = 104
KEYS = 128
GROUP = 4
RELS = 384
NEVER = -1e30
PAGES = 8
VMEM_LIMIT = 60 * 1024 * 1024


def dot(a, b):
    return lax.dot_general(a, b, (((1,), (0,)), ((), ())), preferred_element_type=F32)


def dot_bt(a, b):
    return lax.dot_general(a, b, (((1,), (1,)), ((), ())), preferred_element_type=F32)


def dot_at(a, b):
    return lax.dot_general(a, b, (((0,), (0,)), ((), ())), preferred_element_type=F32)


def normalize(x):
    center = x - jnp.sum(x, -1, keepdims=True) * (1.0 / x.shape[-1])
    inv = lax.rsqrt(jnp.sum(center * center, -1, keepdims=True) * (1.0 / x.shape[-1]) + EPS)
    return center * inv, inv


def norm_back(up, normed, inv):
    scale = 1.0 / up.shape[-1]
    mean_up = jnp.sum(up, -1, keepdims=True) * scale
    mean_un = jnp.sum(up * normed, -1, keepdims=True) * scale
    return inv * (up - mean_up - normed * mean_un)


def fold(x):
    return jnp.sum(x.reshape(x.shape[0] // 8, 8, x.shape[1]), 0)


def head_masks(rows, dtype):
    lane = lax.broadcasted_iota(jnp.int32, (rows, KEYS), 1)
    width = KEYS // GROUP
    return [
        ((lane >= k * width) & (lane < (k + 1) * width)).astype(F32).astype(dtype)
        for k in range(GROUP)
    ]


def split_rows(x):
    high = x.astype(BF16)
    return high, (x - high.astype(F32)).astype(BF16)


def page_rows(page, count):
    return pl.ds(page, count, stride=PAGES)


def load_rows(ref, w, rows):
    return jnp.concatenate([ref[t, w, rows, :] for t in range(ref.shape[0])], 1)


def store_rows(ref, w, rows, value):
    for t in range(ref.shape[0]):
        ref[t, w, rows, :] = value[:, t * KEYS : (t + 1) * KEYS]


def only_tokens(x):
    return jnp.where(lax.broadcasted_iota(jnp.int32, x.shape, 0) < TOK, x, 0.0)


def gather_frame(out, own, low, right, corner):
    for w in range(2):
        for r in range(WIN):
            if r < WIN - SHIFT:
                main, side, mr, sr = own, right, r + SHIFT, r
            else:
                main, side, mr, sr = low, corner, r - SHIFT, r - SHIFT
            if w == 0:
                block = main[mr, SHIFT : SHIFT + WIN].astype(F32)
            else:
                block = jnp.concatenate(
                    [main[mr, SHIFT + WIN :].astype(F32), side[sr].astype(F32)], 0
                )
            at = r * WIN * PAGES
            store_rows(
                out, w, slice(at, at + WIN * PAGES), block.reshape(WIN * PAGES, block.shape[-1])
            )


def tenth(n):
    return (n * 205) >> 11


def squeeze_matrix():
    at = lax.broadcasted_iota(jnp.int32, (RELS, 2 * KEYS), 0)
    to = lax.broadcasted_iota(jnp.int32, (RELS, 2 * KEYS), 1)
    hit = (at == to + (SPAN - WIN) * tenth(to)) & (to < SPAN * WIN)
    return hit.astype(F32).astype(BF16)


def bias_kernel(edge, table, out):
    heads = table.shape[0]
    reversed_table = table[...]
    moved = []
    for c in range(WIN):
        shift = WIN - 1 - c
        moved.append(pltpu.roll(reversed_table, RELS - shift, 1) if shift else reversed_table)
    stack = jnp.concatenate(moved, 0)
    high = stack.astype(BF16)
    rest = stack - high.astype(F32)
    middle = rest.astype(BF16)
    least = (rest - middle.astype(F32)).astype(BF16)
    squeeze = squeeze_matrix()
    wide = dot(high, squeeze) + dot(middle, squeeze) + dot(least, squeeze)
    count = WIN * heads
    for r in range(WIN):
        shift = (WIN - 1 - r) * WIN
        rel = pltpu.roll(wide, 2 * KEYS - shift, 1) if shift else wide
        rel = rel[:, :KEYS]
        key = lax.broadcasted_iota(jnp.int32, (count, KEYS), 1)
        row = lax.broadcasted_iota(jnp.int32, (count, KEYS), 0)
        across = (key < TOK // 2) if r >= SHIFT else (key >= TOK // 2)
        key_left = key - WIN * tenth(key) < SHIFT
        own_left = row < SHIFT * heads
        beside = key_left != own_left
        for w in range(2):
            cut_off = across & (edge[0] != 0)
            if w == 1:
                cut_off = cut_off | (beside & (edge[1] != 0))
            value = rel + jnp.where(cut_off, -100.0, 0.0)
            out[w, r * count : (r + 1) * count, :] = jnp.where(key < TOK, value, NEVER)
    for w in range(2):
        out[w, TOK * heads :, :] = jnp.zeros((out.shape[1] - TOK * heads, KEYS), F32)


def attention_kernel(
    own, low, right, corner, qkv_w, bias, g1, b1, qb, vb,
    x_out, xw_out, qkv_out, p_out, o_out,
    xf,
):
    page = pl.program_id(0)

    @pl.when(page == 0)
    def _():
        gather_frame(xf, own, low, right, corner)
        for t in range(xf.shape[0]):
            for w in range(2):
                xf[t, w, TOK * PAGES :, :] = jnp.zeros((xf.shape[2] - TOK * PAGES, KEYS), F32)
                x_out[w * TOK * PAGES : (w + 1) * TOK * PAGES, t * KEYS : (t + 1) * KEYS] = xf[
                    t, w, : TOK * PAGES, :
                ].astype(BF16)

    d = g1.shape[-1]
    heads = d // (KEYS // GROUP)
    scale = (d // heads) ** (-0.5)
    x = jnp.concatenate([only_tokens(load_rows(xf, w, page_rows(page, ROWS))) for w in range(2)], 0)
    for w in range(2):
        xw_out[w, 0] = x[w * ROWS : (w + 1) * ROWS].astype(BF16)
    normed, _ = normalize(x)
    attn_in = (normed * g1[...] + b1[...]).astype(BF16)
    proj = dot(attn_in, qkv_w[...])
    q_all = proj[:, :d] + qb[...]
    k_all = proj[:, d : 2 * d]
    v_all = proj[:, 2 * d :] + vb[...]
    masks = head_masks(KEYS, BF16)
    filler = jnp.zeros((KEYS - ROWS, d), F32)
    for w in range(2):
        rows = slice(w * ROWS, (w + 1) * ROWS)
        q = jnp.concatenate([q_all[rows], filler], 0).astype(BF16)
        k = jnp.concatenate([k_all[rows], filler], 0).astype(BF16)
        v = jnp.concatenate([v_all[rows], filler], 0).astype(BF16)
        qkv_out[w, 0, :, :d] = q
        qkv_out[w, 0, :, d : 2 * d] = k
        qkv_out[w, 0, :, 2 * d :] = v
        parts = []
        for g in range(heads // GROUP):
            lanes = slice(g * KEYS, (g + 1) * KEYS)
            kg, vg = k[:, lanes], v[:, lanes]
            k_stack = jnp.concatenate([kg * m for m in masks], 0)
            v_stack = jnp.concatenate([vg * m for m in masks], 0)
            wide = slice(g * GROUP * KEYS, (g + 1) * GROUP * KEYS)
            s = dot_bt(q[:ROWS, lanes], k_stack)
            probs = []
            for h in range(GROUP):
                rel = bias[w, pl.ds(g * GROUP + h, ROWS, stride=heads), :]
                sh = s[:, h * KEYS : (h + 1) * KEYS] * scale + rel
                e = jnp.exp(sh - jnp.max(sh, -1, keepdims=True))
                probs.append(e * (1.0 / jnp.sum(e, -1, keepdims=True)))
            p = jnp.concatenate(probs, 1).astype(BF16)
            p_out[w, 0, :, wide] = p
            parts.append(dot(p, v_stack))
        store_rows(o_out, w, page_rows(page, TOK), jnp.concatenate(parts, 1)[:TOK])


def mlp_kernel(
    x_in, o_in, t_own, t_low, t_right, t_corner, count,
    proj_w, fc1_w, fc2_w, pb, g2, b2, f1b, f2b,
    frame_out, dy_out, do_out, sums_out,
    tf, fc1_acc, fc2_acc, proj_acc, fc1_sum, small_sum,
):
    step = pl.program_id(0)

    @pl.when(step == 0)
    def _():
        for buf in (fc1_acc, fc2_acc, proj_acc, fc1_sum, small_sum):
            buf[...] = jnp.zeros_like(buf)
        gather_frame(tf, t_own, t_low, t_right, t_corner)

    size, d = x_in.shape
    ff = fc1_w.shape[1] // d
    o = load_rows(o_in, 0, slice(None)).astype(BF16)
    y = x_in[...].astype(F32) + dot(o, proj_w[...]) + pb[...]
    normed2, inv2 = normalize(y)
    c = (normed2 * g2[...] + b2[...]).astype(BF16)
    dr = load_rows(tf, step // 2, pl.ds(pl.multiple_of(step % 2 * size, size), size))
    drb = dr.astype(BF16)
    r = y + f2b[...]
    dc = None
    for j in range(ff):
        at = slice(j * d, (j + 1) * d)
        h = dot(c, fc1_w[:, at]) + f1b[:, at]
        phi = 0.5 * (1.0 + lax.erf(h * math.sqrt(0.5)))
        slope = phi + h * (jnp.exp(h * h * -0.5) * (1.0 / math.sqrt(2.0 * math.pi)))
        gelu = (h * phi).astype(BF16)
        dh_wide = dot_bt(drb, fc2_w[at, :]) * slope
        dh = dh_wide.astype(BF16)
        r = r + dot(gelu, fc2_w[at, :])
        fc2_acc[:, at] += dot_at(drb, gelu)
        fc1_acc[:, at] += dot_at(c, dh)
        fc1_sum[:, at] += fold(dh.astype(F32))
        more = dot_bt(dh, fc1_w[:, at])
        dc = more if dc is None else dc + more
    frame_out[...] = r.reshape(frame_out.shape).astype(BF16)
    dy = dr + norm_back(dc * g2[...], normed2, inv2)
    dz = dy.astype(BF16)
    proj_acc[...] += dot_at(o, dz)
    store_rows(do_out, 0, slice(None), dot_bt(dz, proj_w[...]))
    store_rows(dy_out, 0, slice(None), dy)
    small_sum[0] += fold(dc * normed2)
    small_sum[1] += fold(dc)
    small_sum[2] += fold(dr)
    small_sum[3] += fold(dz.astype(F32))

    @pl.when(step == pl.num_programs(0) - 1)
    def _():
        for j in range(ff):
            sums_out[j * d : (j + 1) * d, :] = fc1_acc[:, j * d : (j + 1) * d].astype(BF16)
            sums_out[(ff + j) * d : (ff + j + 1) * d, :] = fc2_acc[:, j * d : (j + 1) * d].T.astype(
                BF16
            )
        at = 2 * ff * d
        sums_out[at : at + d, :] = proj_acc[...].astype(BF16)
        rows = [jnp.sum(fc1_sum[:, j * d : (j + 1) * d], 0, keepdims=True) for j in range(ff)]
        rows += [jnp.sum(small_sum[k], 0, keepdims=True) for k in range(4)]
        rows.append(jnp.full((1, d), count[0], F32))
        rows.append(jnp.zeros((16 - len(rows), d), F32))
        high, low_part = split_rows(jnp.concatenate(rows, 0))
        at += d
        sums_out[at : at + 16, :] = high
        sums_out[at + 16 : at + 32, :] = low_part
        if sums_out.shape[0] > at + 32:
            sums_out[at + 32 :, :] = jnp.zeros((sums_out.shape[0] - at - 32, d), BF16)


def backward_kernel(last, *refs):
    xw, qkv, p_in, dy_in, do_in, qkv_w, g1, b1 = refs[:8]
    if last:
        before, outs, (dx, qkv_acc, rel_acc, col_sum, small_sum) = refs[8:12], refs[12:17], refs[17:22]
        mixed = refs[22]
    else:
        before, outs, (dx,) = None, refs[8:14], refs[14:]
        qkv_acc, rel_acc, col_sum, small_sum = outs[2:]
    step = pl.program_id(0)

    @pl.when(step == 0)
    def _():
        for k, buf in enumerate((qkv_acc, rel_acc, col_sum, small_sum)):
            buf[...] = before[k][...] if last else jnp.zeros_like(buf)

    d = g1.shape[-1]
    heads = d // (KEYS // GROUP)
    scale = (d // heads) ** (-0.5)
    masks = head_masks(KEYS, BF16)
    row_masks = head_masks(ROWS, F32)
    count = xw.shape[1]
    dqs, dks, dvs = [], [], []
    rel_sum = [None] * heads
    for n in range(count):
        page = step * count + n
        q = qkv[0, n, :, :d]
        k = qkv[0, n, :, d : 2 * d]
        v = qkv[0, n, :, 2 * d :]
        do = only_tokens(load_rows(do_in, 0, page_rows(page, ROWS)))
        dq, dk, dv = [], [], []
        for g in range(heads // GROUP):
            lanes = slice(g * KEYS, (g + 1) * KEYS)
            kg, vg = k[:, lanes], v[:, lanes]
            k_stack = jnp.concatenate([kg * m for m in masks], 0)
            v_stack = jnp.concatenate([vg * m for m in masks], 0)
            dof = do[:, lanes]
            dog = dof.astype(BF16)
            qf = q[:, lanes].astype(F32)[:ROWS]
            q_stack = jnp.concatenate([qf * m for m in row_masks], 0).astype(BF16)
            do_stack = jnp.concatenate([dof * m for m in row_masks], 0).astype(BF16)
            wide = slice(g * GROUP * KEYS, (g + 1) * GROUP * KEYS)
            dp = dot_bt(dog, v_stack)
            p = p_in[0, n, :, wide].astype(F32)
            t = p * dp
            ds = []
            for h in range(GROUP):
                at = slice(h * KEYS, (h + 1) * KEYS)
                th = t[:, at]
                ds.append(th - p[:, at] * jnp.sum(th, -1, keepdims=True))
            for h in range(GROUP):
                at = g * GROUP + h
                rel_sum[at] = ds[h] if n == 0 else rel_sum[at] + ds[h]
            dts = [x * scale for x in ds]
            dt = jnp.concatenate(dts, 1).astype(BF16)
            dt_stack = jnp.concatenate(dts, 0).astype(BF16)
            p_stack = jnp.concatenate(
                [p[:, h * KEYS : (h + 1) * KEYS] for h in range(GROUP)], 0
            ).astype(BF16)
            dq.append(dot(dt, k_stack))
            dk.append(dot_at(dt_stack, q_stack)[:ROWS])
            dv.append(dot_at(p_stack, do_stack)[:ROWS])
        dqs.append(jnp.concatenate(dq, 1))
        dks.append(jnp.concatenate(dk, 1))
        dvs.append(jnp.concatenate(dv, 1))
    for h in range(heads):
        rel_acc[:, h * KEYS : (h + 1) * KEYS] += rel_sum[h]
    joined = jnp.concatenate(
        [jnp.concatenate(dqs, 0), jnp.concatenate(dks, 0), jnp.concatenate(dvs, 0)], 1
    ).astype(BF16)
    x = jnp.concatenate([xw[0, n].astype(F32) for n in range(count)], 0)
    normed, inv = normalize(x)
    attn_in = (normed * g1[...] + b1[...]).astype(BF16)
    qkv_acc[...] += dot_at(attn_in, joined)
    col_sum[...] += fold(joined.astype(F32))
    da = dot_bt(joined, qkv_w[...])
    small_sum[0] += fold(da * normed)
    small_sum[1] += fold(da)
    back = norm_back(da * g1[...], normed, inv)
    for n in range(count):
        rows = page_rows(step * count + n, TOK)
        store_rows(dx, 0, rows, load_rows(dy_in, 0, rows) + back[n * ROWS : n * ROWS + TOK])

    @pl.when(step == pl.num_programs(0) - 1)
    def _():
        frame = load_rows(dx, 0, slice(None)).reshape(WIN, WIN, PAGES, d)
        if not last:
            outs[0][...] = frame[:SHIFT]
            outs[1][...] = frame[SHIFT:].astype(BF16)
            return
        stays, up, left, corner, sums_out = outs
        stays[...] = frame[:SHIFT, :SHIFT]
        up[...] = frame[SHIFT:, :SHIFT].astype(BF16)
        left[...] = frame[:SHIFT, SHIFT:].astype(BF16)
        corner[...] = frame[SHIFT:, SHIFT:].astype(BF16)
        for j in range(3):
            sums_out[j * d : (j + 1) * d, :] = qkv_acc[:, j * d : (j + 1) * d].astype(BF16)
        rel = table_gradient(
            [rel_acc[:, h * KEYS : (h + 1) * KEYS] for h in range(heads)], mixed
        )
        rows = [jnp.sum(small_sum[k], 0, keepdims=True) for k in range(2)]
        rows.append(jnp.sum(col_sum[:, :d], 0, keepdims=True))
        rows.append(jnp.sum(col_sum[:, 2 * d :], 0, keepdims=True))
        rows.append(jnp.zeros((4, d), F32))
        rows.append(rel[:, :d])
        rows.append(jnp.concatenate([rel[:, d:], jnp.zeros((heads, 2 * d - RELS), F32)], 1))
        rows.append(jnp.zeros((8, d), F32))
        high, rest = split_rows(jnp.concatenate(rows, 0))
        at = 3 * d
        sums_out[at : at + 32, :] = high
        sums_out[at + 32 : at + 64, :] = rest
        if sums_out.shape[0] > at + 64:
            sums_out[at + 64 :, :] = jnp.zeros((sums_out.shape[0] - at - 64, d), BF16)


def table_gradient(by_head, mixed):
    heads = len(by_head)
    for h in range(heads):
        mixed[pl.ds(h, ROWS, stride=heads), :] = by_head[h]
    wide = None
    for r in range(WIN):
        part = mixed[r * WIN * heads : (r + 1) * WIN * heads, :]
        part = jnp.concatenate([part, jnp.zeros_like(part)], 1)
        shift = (WIN - 1 - r) * WIN
        part = pltpu.roll(part, shift, 1) if shift else part
        wide = part if wide is None else wide + part
    high, rest = split_rows(wide)
    squeeze = squeeze_matrix()
    moved = dot_bt(high, squeeze) + dot_bt(rest, squeeze)
    total = None
    for c in range(WIN):
        part = moved[c * heads : (c + 1) * heads]
        shift = WIN - 1 - c
        part = pltpu.roll(part, shift, 1) if shift else part
        total = part if total is None else total + part
    at = lax.broadcasted_iota(jnp.int32, (RELS, RELS), 0)
    to = lax.broadcasted_iota(jnp.int32, (RELS, RELS), 1)
    turn = (at + to == SPAN * SPAN - 1).astype(F32).astype(BF16)
    high, rest = split_rows(total)
    return dot(high, turn) + dot(rest, turn)


def collect(places, buf, mine, other, planes):
    core, spot = places[0], places[1]
    size = mine.shape[0] // planes
    for first, pieces in ((core, mine), (1 - core, other)):
        for k in range(planes):
            at = pl.multiple_of((first * planes + (spot ^ k)) * size, 16)
            buf[pl.ds(at, size), :] = pieces[k * size : (k + 1) * size, :].astype(F32)


def finish_mlp_kernel(
    total, planes, places, mine, other,
    fc1, fc2, proj, fc1_b, g2, b2, fc2_b, proj_b, scale_out, buf,
):
    collect(places, buf, mine, other, planes)
    d = proj.shape[0]
    ff = fc1.shape[1] // d
    at = (2 * ff + 1) * d
    rows = buf[at : at + 16, :] + buf[at + 16 : at + 32, :]
    scale = total / rows[ff + 4 : ff + 5, :]
    rows = rows * scale
    scale_out[...] = scale
    for j in range(ff):
        fc1[:, j * d : (j + 1) * d] = buf[j * d : (j + 1) * d, :] * scale
        fc2[j * d : (j + 1) * d, :] = buf[(ff + j) * d : (ff + j + 1) * d, :] * scale
        fc1_b[:, j * d : (j + 1) * d] = rows[j : j + 1]
    proj[...] = buf[2 * ff * d : (2 * ff + 1) * d, :] * scale
    for k, ref in enumerate((g2, b2, fc2_b, proj_b)):
        ref[...] = rows[ff + k : ff + k + 1]


def finish_attention_kernel(
    planes, places, mine, other, scale_in, qkv, g1, b1, q_b, v_b, rel, buf
):
    collect(places, buf, mine, other, planes)
    d = scale_in.shape[1]
    scale = scale_in[...]
    for j in range(3):
        qkv[:, j * d : (j + 1) * d] = buf[j * d : (j + 1) * d, :] * scale
    at = 3 * d
    rows = (buf[at : at + 32, :] + buf[at + 32 : at + 64, :]) * scale
    for k, ref in enumerate((g1, b1, q_b, v_b)):
        ref[...] = rows[k : k + 1]
    heads = rel.shape[0]
    rel[:, :d] = rows[8 : 8 + heads]
    rel[:, d:] = rows[16 : 16 + heads, : rel.shape[1] - d]


def permute(block, target):
    rows, cols = lax.axis_size("rows"), lax.axis_size("cols")
    route = []
    for r in range(rows):
        for c in range(cols):
            tr, tc = target(r, c)
            route.append((r * cols + c, (tr % rows) * cols + tc % cols))
    return lax.ppermute(block, ("rows", "cols"), route)


def tree_sum(parts):
    parts = [p.astype(F32) for p in parts]
    while len(parts) > 1:
        parts = [parts[i] + parts[i + 1] for i in range(0, len(parts), 2)]
    return parts[0].astype(BF16)


def after(values, done):
    return lax.optimization_barrier((values, done))[0]


def spot_index():
    r, c = lax.axis_index("rows"), lax.axis_index("cols")
    return r & 1, ((r >> 1) & 1) * lax.axis_size("cols") + c


def core_hop(r, c):
    return r ^ 1, c


def plane_hop(k):
    cols = lax.axis_size("cols")
    return lambda r, c: (r ^ (2 * (k // cols)), c ^ (k % cols))


def core_scatter(x):
    core, _ = spot_index()
    halves = x.reshape(2, x.shape[0] // 2, x.shape[1])
    mine = lax.dynamic_index_in_dim(halves, core, 0, False)
    other = permute(lax.dynamic_index_in_dim(halves, 1 - core, 0, False), core_hop)
    return tree_sum([mine, other])


def plane_scatter(half):
    planes = 2 * lax.axis_size("cols")
    _, spot = spot_index()
    pieces = half.reshape(planes, half.shape[0] // planes, half.shape[1])
    got = [lax.dynamic_index_in_dim(pieces, spot, 0, False)]
    for k in range(1, planes):
        got.append(
            permute(lax.dynamic_index_in_dim(pieces, spot ^ k, 0, False), plane_hop(k))
        )
    return got


def depth_share(piece):
    got = [piece]
    for k in range(1, lax.axis_size("rows") // 4):
        got.append(permute(piece, lambda r, c, k=k: (r ^ (4 * k), c)))
    return got


def plane_gather(piece):
    got = [piece]
    for k in range(1, 2 * lax.axis_size("cols")):
        got.append(permute(piece, plane_hop(k)))
    return got


def strips(field):
    low = permute(field[:SHIFT], lambda r, c: (r - 1, c))
    right = permute(field[SHIFT:, :SHIFT], lambda r, c: (r, c - 1))
    corner = permute(field[:SHIFT, :SHIFT], lambda r, c: (r - 1, c - 1))
    return low, right, corner


def leave(field):
    upper = permute(field[SHIFT:, :-SHIFT].astype(BF16), lambda r, c: (r + 1, c))
    left = permute(field[:SHIFT, -SHIFT:].astype(BF16), lambda r, c: (r, c + 1))
    corner = permute(field[SHIFT:, -SHIFT:].astype(BF16), lambda r, c: (r + 1, c + 1))
    return corner, upper, left, field[:SHIFT, :-SHIFT]


def whole(a):
    return pl.BlockSpec(a.shape, lambda i: (0,) * len(a.shape), pipeline_mode=pl.Buffered(1))


def held(a):
    return pl.BlockSpec(a.shape, lambda i: (0,) * len(a.shape))


def bias_call(edge, rel_table):
    heads = rel_table.shape[0]
    table = jnp.pad(rel_table[:, ::-1], ((0, 0), (0, RELS - SPAN * SPAN)))
    return pl.pallas_call(
        bias_kernel,
        in_specs=[pl.BlockSpec(memory_space=pltpu.SMEM), pl.BlockSpec(memory_space=pltpu.VMEM)],
        out_shape=jax.ShapeDtypeStruct((2, ROWS * heads, KEYS), F32),
        compiler_params=pltpu.CompilerParams(vmem_limit_bytes=VMEM_LIMIT),
        name="attention_bias",
    )(edge, table)


def loop_params():
    return pltpu.CompilerParams(
        dimension_semantics=("arbitrary",), vmem_limit_bytes=VMEM_LIMIT
    )


def cost(flops):
    return pl.CostEstimate(flops=flops, bytes_accessed=10**7, transcendentals=10**6)


def attention_call(patches, p_strips, qkv_w, bias, g1, b1, q_b, v_b):
    pages, d = patches.shape[2:]
    heads = bias.shape[1] // ROWS
    tokens = 2 * TOK * pages
    shape = jax.ShapeDtypeStruct
    inputs = [patches, *p_strips, qkv_w, bias, g1, b1, q_b, v_b]
    outs = [
        shape((tokens, d), BF16),
        shape((2, pages, ROWS, d), BF16),
        shape((2, pages, KEYS, 3 * d), BF16),
        shape((2, pages, ROWS, heads * KEYS), BF16),
        shape((d // KEYS, 2, TOK * pages, KEYS), F32),
    ]
    paged = lambda a: pl.BlockSpec((2, 1) + a.shape[2:], lambda i: (0, i, 0, 0))
    return pl.pallas_call(
        attention_kernel,
        grid=(pages,),
        in_specs=[whole(a) for a in inputs],
        out_specs=[held(outs[0]), paged(outs[1]), paged(outs[2]), paged(outs[3]), held(outs[4])],
        out_shape=outs,
        scratch_shapes=[pltpu.VMEM((d // KEYS, 2, ROWS * pages, KEYS), F32)],
        compiler_params=loop_params(),
        cost_estimate=cost(10**10),
        name="attention_forward",
    )(*inputs)


def mlp_call(size, x, mixed, masked, t_strips, count, *weights):
    height, width, pages, d = masked.shape
    ff = weights[1].shape[1]
    tokens, chunk = x.shape[0], x.shape[0] // 4
    shape = jax.ShapeDtypeStruct
    blocks = [masked, *t_strips]
    outs = [
        shape((height, width, pages, d), BF16),
        shape((d // KEYS, 2, ROWS * pages, KEYS), F32),
        shape((d // KEYS, 2, ROWS * pages, KEYS), F32),
        shape((size, d), BF16),
    ]
    part = pl.BlockSpec((d // KEYS, 1, chunk, KEYS), lambda i: (0, i // 2, i % 2, 0))
    return pl.pallas_call(
        mlp_kernel,
        grid=(4,),
        in_specs=[pl.BlockSpec((chunk, d), lambda i: (i, 0)), part]
        + [whole(a) for a in blocks]
        + [pl.BlockSpec(memory_space=pltpu.SMEM)]
        + [whole(a) for a in weights],
        out_specs=[
            pl.BlockSpec((SHIFT, WIN, pages, d), lambda i: (i % 2, i // 2, 0, 0)),
            part, part, held(outs[3]),
        ],
        out_shape=outs,
        scratch_shapes=[
            pltpu.VMEM((d // KEYS, 2, TOK * pages, KEYS), F32),
            pltpu.VMEM((d, ff), F32),
            pltpu.VMEM((d, ff), F32),
            pltpu.VMEM((d, d), F32),
            pltpu.VMEM((8, ff), F32),
            pltpu.VMEM((4, 8, d), F32),
        ],
        compiler_params=loop_params(),
        cost_estimate=cost(10**10),
        name="mlp_forward_backward",
    )(x, mixed, *blocks, count, *weights)


def backward_call(w, size, xw, qkv, probs, dy, do, qkv_w, g1, b1, before=()):
    last = w == 1
    pages, d = xw.shape[1], xw.shape[3]
    heads = probs.shape[3] // KEYS
    batch = 2
    shape = jax.ShapeDtypeStruct
    sums = [
        shape((d, 3 * d), F32), shape((ROWS, heads * KEYS), F32), shape((8, 3 * d), F32),
        shape((2, 8, d), F32),
    ]
    dx = pltpu.VMEM((d // KEYS, 1, TOK * pages, KEYS), F32)
    rest = WIN - SHIFT
    if last:
        outs = [
            shape((SHIFT, SHIFT, pages, d), F32), shape((rest, SHIFT, pages, d), BF16),
            shape((SHIFT, rest, pages, d), BF16), shape((rest, rest, pages, d), BF16),
            shape((size, d), BF16),
        ]
        scratch = [dx] + [pltpu.VMEM(a.shape, F32) for a in sums]
        scratch.append(pltpu.VMEM((ROWS * heads, KEYS), F32))
    else:
        outs = [shape((SHIFT, WIN, pages, d), F32), shape((rest, WIN, pages, d), BF16)] + sums
        scratch = [dx]
    paged = lambda a: pl.BlockSpec((1, batch) + a.shape[2:], lambda i: (w, i, 0, 0))
    rows = pl.BlockSpec((d // KEYS, 1, ROWS * pages, KEYS), lambda i: (0, w, 0, 0))
    return pl.pallas_call(
        lambda *refs: backward_kernel(last, *refs),
        grid=(pages // batch,),
        in_specs=[paged(xw), paged(qkv), paged(probs), rows, rows]
        + [whole(a) for a in (qkv_w, g1, b1, *before)],
        out_specs=[held(a) for a in outs],
        out_shape=outs,
        scratch_shapes=scratch,
        compiler_params=loop_params(),
        cost_estimate=cost(10**10),
        name="attention_backward",
    )(xw, qkv, probs, dy, do, qkv_w, g1, b1, *before)


def finish_call(kernel, shapes, places, size, *inputs):
    return pl.pallas_call(
        kernel,
        in_specs=[pl.BlockSpec(memory_space=pltpu.SMEM)]
        + [pl.BlockSpec(memory_space=pltpu.VMEM)] * len(inputs),
        out_shape=[jax.ShapeDtypeStruct(s, F32) for s in shapes],
        scratch_shapes=[pltpu.VMEM((size, inputs[0].shape[1]), F32)],
        compiler_params=pltpu.CompilerParams(vmem_limit_bytes=VMEM_LIMIT),
        name="finish_sums",
    )(places, *inputs)


def shards(
    patches, target, kept_mask, ln1_gain, ln1_bias, qkv_weight, query_bias, value_bias, rel_table,
    proj_weight, proj_bias, ln2_gain, ln2_bias, fc1_weight, fc1_bias, fc2_weight, fc2_bias,
):
    pages, height, width, d = patches.shape
    ff = fc1_weight.shape[1]
    rows, cols = lax.axis_size("rows"), lax.axis_size("cols")
    planes = 2 * cols
    step = 32 * planes
    tokens = pages * height * width
    vec = lambda a: a.reshape(1, -1)

    patches = patches.transpose(1, 2, 0, 3)
    p_strips = strips(patches)
    edge = jnp.stack(
        [lax.axis_index("rows") == rows - 1, lax.axis_index("cols") == cols - 1]
    ).astype(jnp.int32)
    bias = bias_call(edge, rel_table)
    kept = kept_mask.transpose(1, 2, 0)
    masked = target.transpose(1, 2, 0, 3) * kept.astype(BF16)[..., None]
    t_strips = strips(masked)
    count = jnp.sum(kept_mask.astype(F32)).reshape(1)

    g1, b1 = vec(ln1_gain), vec(ln1_bias)
    x, xw, qkv, probs, mixed = attention_call(
        patches, p_strips, qkv_weight, bias, g1, b1, vec(query_bias), vec(value_bias)
    )
    n1 = -(-(2 * ff + d + 32) // step) * step
    n2 = -(-(3 * d + 64) // step) * step
    frame, dy, do, sums = mlp_call(
        n1, x, mixed, masked, t_strips, count, proj_weight, fc1_weight, fc2_weight,
        vec(proj_bias), vec(ln2_gain), vec(ln2_bias), vec(fc1_bias), vec(fc2_bias),
    )

    half = core_scatter(sums)
    got = plane_scatter(half)
    do = after(do, half)
    first = backward_call(0, n2, xw, qkv, probs, dy, do, qkv_weight, g1, b1)
    stays_a, up_a = first[:2]
    got = after(got, first[2])
    piece = tree_sum(got)
    got = depth_share(piece)
    do = after(do, piece)
    stays_b, up_b, left, corner, sums2 = backward_call(
        1, n2, xw, qkv, probs, dy, do, qkv_weight, g1, b1, first[2:]
    )
    got = after(got, sums2)
    half2 = core_scatter(sums2)
    piece = tree_sum(got)
    got2 = plane_scatter(half2)
    mine = jnp.concatenate(plane_gather(piece), 0)
    piece2 = tree_sum(got2)
    got2 = depth_share(piece2)
    other = permute(mine, core_hop)
    piece2 = tree_sum(got2)
    mine2 = jnp.concatenate(plane_gather(piece2), 0)
    other2 = permute(mine2, core_hop)

    places = jnp.stack(spot_index()).astype(jnp.int32)
    total = float(tokens * rows * cols)
    row = (1, d)
    fc1_g, fc2_g, proj_g, fc1_bg, g2_g, b2_g, fc2_bg, proj_bg, scale = finish_call(
        lambda *refs: finish_mlp_kernel(total, planes, *refs),
        [(d, ff), (ff, d), (d, d), (1, ff), row, row, row, row, row],
        places, n1, mine, other,
    )
    qkv_g, g1_g, b1_g, q_bg, v_bg, rel_g = finish_call(
        lambda *refs: finish_attention_kernel(planes, *refs),
        [(d, 3 * d), row, row, row, row, rel_table.shape],
        places, n2, mine2, other2, scale,
    )

    down = lambda r, c: (r + 1, c)
    side = lambda r, c: (r, c + 1)
    across = lambda r, c: (r + 1, c + 1)
    out_up = permute(frame[SHIFT:, :-SHIFT], down)
    out_left = permute(frame[:SHIFT, -SHIFT:], side)
    out_corner = permute(frame[SHIFT:, -SHIFT:], across)
    top = jnp.concatenate([out_corner, out_up], 1)
    bottom = jnp.concatenate([out_left, frame[:SHIFT, :-SHIFT]], 1)
    output = jnp.concatenate([top, bottom], 0)
    up_a, up_b = permute(up_a, down), permute(up_b, down)
    left, corner = permute(left, side), permute(corner, across)
    top = jnp.concatenate([corner, up_a, up_b], 1).astype(F32)
    bottom = jnp.concatenate([left.astype(F32), stays_a, stays_b], 1)
    grad = jnp.concatenate([top, bottom], 0) * scale[0]
    flat = lambda a: a.reshape(-1)
    return (
        output.transpose(2, 0, 1, 3),
        grad.transpose(2, 0, 1, 3),
        flat(g1_g),
        flat(b1_g),
        qkv_g,
        flat(q_bg),
        flat(v_bg),
        rel_g,
        proj_g,
        flat(proj_bg),
        flat(g2_g),
        flat(b2_g),
        fc1_g,
        flat(fc1_bg),
        fc2_g,
        flat(fc2_bg),
    )


def solution(mesh):
    field = P(None, "rows", "cols", None)
    return jax.shard_map(
        shards,
        mesh=mesh,
        in_specs=(field, field, P(None, "rows", "cols")) + (P(),) * 14,
        out_specs=(field, field) + (P(),) * 14,
        check_vma=False,
    )
```

```python
import math

import jax
import jax.numpy as jnp
from jax import lax
from jax.experimental import pallas as pl
from jax.experimental.pallas import tpu as pltpu
from jax.sharding import PartitionSpec as P

WIN = 10
SHIFT = 5
EPS = 1e-05
F32 = jnp.float32
BF16 = jnp.bfloat16

SPAN = 2 * WIN - 1
TOK = WIN * WIN
ROWS = 104
KEYS = 128
GROUP = 4
RELS = 384
NEVER = -1e30
PAGES = 8
VMEM_LIMIT = 20


def dot(a, b):
    return lax.dot_general(a, b, (((1,), (0,)), ((), ())), preferred_element_type=F32)


def dot_bt(a, b):
    return lax.dot_general(a, b, (((1,), (1,)), ((), ())), preferred_element_type=F32)


def dot_at(a, b):
    return lax.dot_general(a, b, (((0,), (0,)), ((), ())), preferred_element_type=F32)


def normalize(x):
    center = x - jnp.sum(x, -1, keepdims=True) * (1.0 / x.shape[-1])
    inv = lax.rsqrt(jnp.sum(center * center, -1, keepdims=True) * (1.0 / x.shape[-1]) + EPS)
    return center * inv, inv


def norm_back(up, normed, inv):
    scale = 1.0 / up.shape[-1]
    mean_up = jnp.sum(up, -1, keepdims=True) * scale
    mean_un = jnp.sum(up * normed, -1, keepdims=True) * scale
    return inv * (up - mean_up - normed * mean_un)


def fold(x):
    return jnp.sum(x.reshape(x.shape[0] // 8, 8, x.shape[1]), 0)


def head_masks(rows, dtype):
    lane = lax.broadcasted_iota(jnp.int32, (rows, KEYS), 1)
    width = KEYS // GROUP
    return [
        ((lane >= k * width) & (lane < (k + 1) * width)).astype(F32).astype(dtype)
        for k in range(GROUP)
    ]


def head_rows(x, masks):
    return jnp.concatenate([x * m for m in masks], 0).astype(BF16)


def own_lanes(stacked):
    lane = lax.broadcasted_iota(jnp.int32, (ROWS, KEYS), 1)
    out = stacked[(GROUP - 1) * ROWS :]
    for h in reversed(range(GROUP - 1)):
        out = jnp.where(lane < (h + 1) * (KEYS // GROUP), stacked[h * ROWS : (h + 1) * ROWS], out)
    return out


def split_rows(x):
    high = x.astype(BF16)
    return high, (x - high.astype(F32)).astype(BF16)


def page_rows(page, count):
    return pl.ds(page, count, stride=PAGES)


def load_rows(ref, w, rows):
    return jnp.concatenate([ref[t, w, rows, :] for t in range(ref.shape[0])], 1)


def store_rows(ref, w, rows, value):
    for t in range(ref.shape[0]):
        ref[t, w, rows, :] = value[:, t * KEYS : (t + 1) * KEYS]


def only_tokens(x):
    return jnp.where(lax.broadcasted_iota(jnp.int32, x.shape, 0) < TOK, x, 0.0)


def gather_frame(out, own, low, right, corner):
    for w in range(2):
        for r in range(WIN):
            if r < WIN - SHIFT:
                main, side, mr, sr = own, right, r + SHIFT, r
            else:
                main, side, mr, sr = low, corner, r - SHIFT, r - SHIFT
            if w == 0:
                block = main[mr, SHIFT : SHIFT + WIN].astype(F32)
            else:
                block = jnp.concatenate(
                    [main[mr, SHIFT + WIN :].astype(F32), side[sr].astype(F32)], 0
                )
            at = r * WIN * PAGES
            store_rows(
                out, w, slice(at, at + WIN * PAGES), block.reshape(WIN * PAGES, block.shape[-1])
            )


def tenth(n):
    return (n * 205) >> 11


def squeeze_matrix():
    at = lax.broadcasted_iota(jnp.int32, (RELS, 2 * KEYS), 0)
    to = lax.broadcasted_iota(jnp.int32, (RELS, 2 * KEYS), 1)
    hit = (at == to + (SPAN - WIN) * tenth(to)) & (to < SPAN * WIN)
    return hit.astype(F32).astype(BF16)


def copy_all(pairs, sems):
    copies = [pltpu.make_async_copy(a, b, sems.at[k]) for k, (a, b) in enumerate(pairs)]
    for copy in copies:
        copy.start()
    for copy in copies:
        copy.wait()


def strips_kernel(field, low, right, corner, sems):
    copy_all(
        (
            (field.at[:SHIFT], low), (field.at[SHIFT:, :SHIFT], right),
            (field.at[:SHIFT, :SHIFT], corner),
        ),
        sems,
    )


def target_kernel(
    target_in, kept_in, table_in, masked, low, right, corner, count, table, target, kept, sems
):
    copy_all(((target_in, target), (kept_in, kept), (table_in, table)), sems)
    rows, cols = target.shape[:2]
    total = jnp.zeros(kept.shape[1:], F32)
    for r in range(rows):
        kept_row = kept[r].astype(F32)
        total = total + kept_row
        for c in range(cols):
            masked[r, c] = (target[r, c].astype(F32) * kept_row[:, c : c + 1]).astype(BF16)
    low[...] = masked[:SHIFT]
    right[...] = masked[SHIFT:, :SHIFT]
    corner[...] = masked[:SHIFT, :SHIFT]
    total = jnp.sum(jnp.sum(total, 1, keepdims=True), 0, keepdims=True)
    count[...] = jnp.broadcast_to(total, count.shape)


def split_halves(places, sums, mine, other):
    size = mine.shape[0]
    core = places[2]
    mine[...] = sums[pl.ds(pl.multiple_of(core * size, 16), size), :]
    other[...] = sums[pl.ds(pl.multiple_of((1 - core) * size, 16), size), :]


def split_kernel(places, mine, other, *outs):
    size = outs[0].shape[0]
    for k, out in enumerate(outs):
        at = pl.ds(pl.multiple_of((places[3] ^ k) * size, 16), size)
        out[...] = (mine[at, :].astype(F32) + other[at, :].astype(F32)).astype(BF16)


def tree_sum(parts):
    while len(parts) > 1:
        parts = [parts[i] + parts[i + 1] for i in range(0, len(parts), 2)]
    return parts[0]


def sum_kernel(*refs):
    refs[-1][...] = tree_sum([ref[...].astype(F32) for ref in refs[:-1]]).astype(BF16)


def join_kernel(*refs):
    out, at = refs[-1], 0
    for ref in refs[:-1]:
        out[at : at + ref.shape[0]] = ref[...]
        at += ref.shape[0]


def side_kernel(out_up, out_side, grad_up, grad_side, out):
    at = 0
    for ref in (out_up, out_side, grad_up, grad_side):
        out[at : at + ref.shape[0]] = ref[:, -SHIFT:]
        at += ref.shape[0]


def turn_matrix():
    at = lax.broadcasted_iota(jnp.int32, (RELS, RELS), 0)
    to = lax.broadcasted_iota(jnp.int32, (RELS, RELS), 1)
    return (at + to == SPAN * SPAN - 1).astype(F32).astype(BF16)


def split_three(x):
    high = x.astype(BF16)
    rest = x - high.astype(F32)
    middle = rest.astype(BF16)
    return high, middle, (rest - middle.astype(F32)).astype(BF16)


def bias_kernel(edge, table, out, padded):
    heads = table.shape[0]
    padded[...] = jnp.zeros_like(padded)
    padded[:, : table.shape[1]] = table[...]
    turn = turn_matrix()
    high, middle, least = split_three(padded[...])
    reversed_table = dot(high, turn) + dot(middle, turn) + dot(least, turn)
    moved = []
    for c in range(WIN):
        shift = WIN - 1 - c
        moved.append(pltpu.roll(reversed_table, RELS - shift, 1) if shift else reversed_table)
    stack = jnp.concatenate(moved, 0)
    high, middle, least = split_three(stack)
    squeeze = squeeze_matrix()
    wide = dot(high, squeeze) + dot(middle, squeeze) + dot(least, squeeze)
    count = WIN * heads
    for r in range(WIN):
        shift = (WIN - 1 - r) * WIN
        rel = pltpu.roll(wide, 2 * KEYS - shift, 1) if shift else wide
        rel = rel[:, :KEYS]
        key = lax.broadcasted_iota(jnp.int32, (count, KEYS), 1)
        row = lax.broadcasted_iota(jnp.int32, (count, KEYS), 0)
        across = (key < TOK // 2) if r >= SHIFT else (key >= TOK // 2)
        key_left = key - WIN * tenth(key) < SHIFT
        own_left = row < SHIFT * heads
        beside = key_left != own_left
        for w in range(2):
            cut_off = across & (edge[0] != 0)
            if w == 1:
                cut_off = cut_off | (beside & (edge[1] != 0))
            value = rel + jnp.where(cut_off, -100.0, 0.0)
            out[w, r * count : (r + 1) * count, :] = jnp.where(key < TOK, value, NEVER)
    for w in range(2):
        out[w, TOK * heads :, :] = jnp.zeros((out.shape[1] - TOK * heads, KEYS), F32)


def attention_kernel(
    own, low, right, corner, qkv_w, bias, g1, b1, qb, vb,
    x_out, xw_out, qkv_out, p_out, o_out,
    xf,
):
    gather_frame(xf, own, low, right, corner)
    for t in range(xf.shape[0]):
        for w in range(2):
            xf[t, w, TOK * PAGES :, :] = jnp.zeros((xf.shape[2] - TOK * PAGES, KEYS), F32)
            x_out[w * TOK * PAGES : (w + 1) * TOK * PAGES, t * KEYS : (t + 1) * KEYS] = xf[
                t, w, : TOK * PAGES, :
            ].astype(BF16)

    @pl.loop(0, PAGES)
    def _(page):
        attention_page(
            page, xf, qkv_w, bias, g1, b1, qb, vb, xw_out, qkv_out, p_out, o_out
        )


def attention_page(page, xf, qkv_w, bias, g1, b1, qb, vb, xw_out, qkv_out, p_out, o_out):
    d = g1.shape[-1]
    heads = d // (KEYS // GROUP)
    scale = (d // heads) ** (-0.5)
    x = jnp.concatenate([only_tokens(load_rows(xf, w, page_rows(page, ROWS))) for w in range(2)], 0)
    for w in range(2):
        xw_out[w, page] = x[w * ROWS : (w + 1) * ROWS].astype(BF16)
    normed, _ = normalize(x)
    attn_in = (normed * g1[...] + b1[...]).astype(BF16)
    proj = dot(attn_in, qkv_w[...])
    q_all = proj[:, :d] + qb[...]
    k_all = proj[:, d : 2 * d]
    v_all = proj[:, 2 * d :] + vb[...]
    masks = head_masks(ROWS, F32)
    filler = jnp.zeros((KEYS - ROWS, d), F32)
    groups = heads // GROUP
    scores, values = [], []
    for w in range(2):
        rows = slice(w * ROWS, (w + 1) * ROWS)
        q = jnp.concatenate([q_all[rows], filler], 0).astype(BF16)
        k = jnp.concatenate([k_all[rows], filler], 0).astype(BF16)
        v = jnp.concatenate([v_all[rows], filler], 0).astype(BF16)
        qkv_out[w, page, :, :d] = q
        qkv_out[w, page, :, d : 2 * d] = k
        qkv_out[w, page, :, 2 * d :] = v
        for g in range(groups):
            lanes = slice(g * KEYS, (g + 1) * KEYS)
            scores.append(dot_bt(head_rows(q_all[rows, lanes], masks), k[:, lanes]))
            values.append(v[:, lanes])
    probs = []
    for n, s in enumerate(scores):
        w, g = divmod(n, groups)
        es = []
        for h in range(GROUP):
            rel = bias[w, pl.ds(g * GROUP + h, ROWS, stride=heads), :]
            sh = s[h * ROWS : (h + 1) * ROWS] * scale + rel
            e = jnp.exp(sh - jnp.max(sh, -1, keepdims=True))
            es.append(e * (1.0 / jnp.sum(e, -1, keepdims=True)))
        p = jnp.concatenate(es, 0).astype(BF16)
        p_out[w, page, g * GROUP * ROWS : (g + 1) * GROUP * ROWS, :] = p
        probs.append(p)
    parts = [own_lanes(dot(p, v)) for p, v in zip(probs, values)]
    for w in range(2):
        joined = jnp.concatenate(parts[w * groups : (w + 1) * groups], 1)
        store_rows(o_out, w, page_rows(page, TOK), joined[:TOK])


def mlp_kernel(
    places, x_in, o_in, t_own, t_low, t_right, t_corner, count,
    proj_w, fc1_w, fc2_w, pb, g2, b2, f1b, f2b,
    stays, up, side, dy_out, do_out, mine, other,
    frame_out, sums_out, tf, fc1_acc, fc2_acc, proj_acc, fc1_sum, small_sum,
):
    for buf in (fc1_acc, fc2_acc, proj_acc, fc1_sum, small_sum):
        buf[...] = jnp.zeros_like(buf)
    gather_frame(tf, t_own, t_low, t_right, t_corner)

    @pl.loop(0, 4)
    def _(step):
        mlp_chunk(
            step, x_in, o_in, proj_w, fc1_w, fc2_w, pb, g2, b2, f1b, f2b, frame_out, dy_out, do_out,
            tf, fc1_acc, fc2_acc, proj_acc, fc1_sum, small_sum,
        )

    d = proj_w.shape[0]
    ff = fc1_w.shape[1] // d
    for j in range(ff):
        sums_out[j * d : (j + 1) * d, :] = fc1_acc[:, j * d : (j + 1) * d].astype(BF16)
        sums_out[(ff + j) * d : (ff + j + 1) * d, :] = fc2_acc[:, j * d : (j + 1) * d].T.astype(
            BF16
        )
    at = 2 * ff * d
    sums_out[at : at + d, :] = proj_acc[...].astype(BF16)
    rows = [jnp.sum(fc1_sum[:, j * d : (j + 1) * d], 0, keepdims=True) for j in range(ff)]
    rows += [jnp.sum(small_sum[k], 0, keepdims=True) for k in range(4)]
    rows.append(count[...])
    rows.append(jnp.zeros((16 - len(rows), d), F32))
    high, low_part = split_rows(jnp.concatenate(rows, 0))
    at += d
    sums_out[at : at + 16, :] = high
    sums_out[at + 16 : at + 32, :] = low_part
    if sums_out.shape[0] > at + 32:
        sums_out[at + 32 :, :] = jnp.zeros((sums_out.shape[0] - at - 32, d), BF16)
    split_halves(places, sums_out, mine, other)
    stays[...] = frame_out[:SHIFT, :-SHIFT]
    up[...] = frame_out[SHIFT:]
    side[...] = frame_out[:SHIFT, -SHIFT:]


def mlp_chunk(
    step, x_in, o_in, proj_w, fc1_w, fc2_w, pb, g2, b2, f1b, f2b, frame_out, dy_out, do_out,
    tf, fc1_acc, fc2_acc, proj_acc, fc1_sum, small_sum,
):
    size, d = x_in.shape[0] // 4, x_in.shape[1]
    ff = fc1_w.shape[1] // d
    w, half = step // 2, step % 2
    rows = pl.ds(pl.multiple_of(half * size, 16), size)
    o = load_rows(o_in, w, rows).astype(BF16)
    y = x_in[pl.ds(pl.multiple_of(step * size, 16), size), :].astype(F32) + dot(o, proj_w[...]) + pb[...]
    normed2, inv2 = normalize(y)
    c = (normed2 * g2[...] + b2[...]).astype(BF16)
    dr = load_rows(tf, w, rows)
    drb = dr.astype(BF16)
    r = y + f2b[...]
    dc = None
    for j in range(ff):
        at = slice(j * d, (j + 1) * d)
        h = dot(c, fc1_w[:, at]) + f1b[:, at]
        phi = 0.5 * (1.0 + lax.erf(h * math.sqrt(0.5)))
        slope = phi + h * (jnp.exp(h * h * -0.5) * (1.0 / math.sqrt(2.0 * math.pi)))
        gelu = (h * phi).astype(BF16)
        dh_wide = dot_bt(drb, fc2_w[at, :]) * slope
        dh = dh_wide.astype(BF16)
        r = r + dot(gelu, fc2_w[at, :])
        fc2_acc[:, at] += dot_at(drb, gelu)
        fc1_acc[:, at] += dot_at(c, dh)
        fc1_sum[:, at] += fold(dh.astype(F32))
        more = dot_bt(dh, fc1_w[:, at])
        dc = more if dc is None else dc + more
    frame_out[pl.ds(half * SHIFT, SHIFT), pl.ds(w * WIN, WIN)] = r.reshape(
        SHIFT, WIN, PAGES, d
    ).astype(BF16)
    dy = dr + norm_back(dc * g2[...], normed2, inv2)
    dz = dy.astype(BF16)
    proj_acc[...] += dot_at(o, dz)
    store_rows(do_out, w, rows, dot_bt(dz, proj_w[...]))
    store_rows(dy_out, w, rows, dy)
    small_sum[0] += fold(dc * normed2)
    small_sum[1] += fold(dc)
    small_sum[2] += fold(dr)
    small_sum[3] += fold(dz.astype(F32))


def backward_kernel(
    places, xw, qkv, p_in, dy_in, do_in, qkv_w, g1, b1,
    stays, side, up, mine, other,
    dx, qkv_acc, rel_acc, col_sum, small_sum, mixed, sums_out,
):
    for buf in (qkv_acc, rel_acc, col_sum, small_sum):
        buf[...] = jnp.zeros_like(buf)

    @pl.loop(0, PAGES)
    def _(page):
        backward_page(
            page, xw, qkv, p_in, dy_in, do_in, qkv_w, g1, b1, dx, qkv_acc, rel_acc, col_sum,
            small_sum,
        )

    d = g1.shape[-1]
    heads = d // (KEYS // GROUP)
    right = load_rows(dx, 1, slice(None)).reshape(WIN, WIN, PAGES, d)
    left = load_rows(dx, 0, slice(None)).reshape(WIN, WIN, PAGES, d)
    stays[:, :WIN] = left[:SHIFT]
    stays[:, WIN:] = right[:SHIFT, :SHIFT]
    side[...] = right[:SHIFT, SHIFT:].astype(BF16)
    up[:, :WIN] = left[SHIFT:].astype(BF16)
    up[:, WIN:] = right[SHIFT:].astype(BF16)
    for j in range(3):
        sums_out[j * d : (j + 1) * d, :] = qkv_acc[:, j * d : (j + 1) * d].astype(BF16)
    rel = table_gradient(
        [rel_acc[:, h * KEYS : (h + 1) * KEYS] for h in range(heads)], mixed
    )
    rows = [jnp.sum(small_sum[k], 0, keepdims=True) for k in range(2)]
    rows.append(jnp.sum(col_sum[:, :d], 0, keepdims=True))
    rows.append(jnp.sum(col_sum[:, 2 * d :], 0, keepdims=True))
    rows.append(jnp.zeros((4, d), F32))
    rows.append(rel[:, :d])
    rows.append(jnp.concatenate([rel[:, d:], jnp.zeros((heads, 2 * d - RELS), F32)], 1))
    rows.append(jnp.zeros((8, d), F32))
    high, rest = split_rows(jnp.concatenate(rows, 0))
    at = 3 * d
    sums_out[at : at + 32, :] = high
    sums_out[at + 32 : at + 64, :] = rest
    if sums_out.shape[0] > at + 64:
        sums_out[at + 64 :, :] = jnp.zeros((sums_out.shape[0] - at - 64, d), BF16)
    split_halves(places, sums_out, mine, other)


def backward_page(
    page, xw, qkv, p_in, dy_in, do_in, qkv_w, g1, b1, dx, qkv_acc, rel_acc, col_sum, small_sum
):
    d = g1.shape[-1]
    heads = d // (KEYS // GROUP)
    scale = (d // heads) ** (-0.5)
    masks = head_masks(ROWS, F32)
    count = 2
    groups = heads // GROUP
    chains = [(n, g) for n in range(count) for g in range(groups)]
    qs, ks, dos, dps = [], [], [], []
    for n, g in chains:
        lanes = slice(g * KEYS, (g + 1) * KEYS)
        qs.append(head_rows(qkv[n, page, :, lanes].astype(F32)[:ROWS], masks))
        ks.append(qkv[n, page, :, d + g * KEYS : d + (g + 1) * KEYS])
        v = qkv[n, page, :, 2 * d + g * KEYS : 2 * d + (g + 1) * KEYS]
        do = only_tokens(do_in[g, n, page_rows(page, ROWS), :])
        dos.append(head_rows(do, masks))
        dps.append(dot_bt(dos[-1], v))
    dts = []
    rel_sum = [None] * heads
    for c, (n, g) in enumerate(chains):
        p = p_in[n, page, g * GROUP * ROWS : (g + 1) * GROUP * ROWS, :].astype(F32)
        t = p * dps[c]
        ds = t - p * jnp.sum(t, -1, keepdims=True)
        for h in range(GROUP):
            at = g * GROUP + h
            part = ds[h * ROWS : (h + 1) * ROWS]
            rel_sum[at] = part if n == 0 else rel_sum[at] + part
        dts.append((ds * scale).astype(BF16))
    dqs, dks, dvs = [], [], []
    for c, (n, g) in enumerate(chains):
        p = p_in[n, page, g * GROUP * ROWS : (g + 1) * GROUP * ROWS, :]
        dqs.append(own_lanes(dot(dts[c], ks[c])))
        dks.append(dot_at(dts[c], qs[c])[:ROWS])
        dvs.append(dot_at(p, dos[c])[:ROWS])
    for h in range(heads):
        rel_acc[:, h * KEYS : (h + 1) * KEYS] += rel_sum[h]
    joined = jnp.concatenate(
        [
            jnp.concatenate([part[n * groups + g] for n in range(count)], 0)
            for part in (dqs, dks, dvs)
            for g in range(groups)
        ],
        1,
    ).astype(BF16)
    x = jnp.concatenate([xw[n, page].astype(F32) for n in range(count)], 0)
    normed, inv = normalize(x)
    attn_in = (normed * g1[...] + b1[...]).astype(BF16)
    qkv_acc[...] += dot_at(attn_in, joined)
    col_sum[...] += fold(joined.astype(F32))
    da = dot_bt(joined, qkv_w[...])
    small_sum[0] += fold(da * normed)
    small_sum[1] += fold(da)
    back = norm_back(da * g1[...], normed, inv)
    for n in range(count):
        rows = page_rows(page, TOK)
        store_rows(dx, n, rows, load_rows(dy_in, n, rows) + back[n * ROWS : n * ROWS + TOK])


def table_gradient(by_head, mixed):
    heads = len(by_head)
    for h in range(heads):
        mixed[pl.ds(h, ROWS, stride=heads), :] = by_head[h]
    wide = None
    for r in range(WIN):
        part = mixed[r * WIN * heads : (r + 1) * WIN * heads, :]
        part = jnp.concatenate([part, jnp.zeros_like(part)], 1)
        shift = (WIN - 1 - r) * WIN
        part = pltpu.roll(part, shift, 1) if shift else part
        wide = part if wide is None else wide + part
    high, rest = split_rows(wide)
    squeeze = squeeze_matrix()
    moved = dot_bt(high, squeeze) + dot_bt(rest, squeeze)
    total = None
    for c in range(WIN):
        part = moved[c * heads : (c + 1) * heads]
        shift = WIN - 1 - c
        part = pltpu.roll(part, shift, 1) if shift else part
        total = part if total is None else total + part
    turn = turn_matrix()
    high, rest = split_rows(total)
    return dot(high, turn) + dot(rest, turn)


def collect(places, buf, mine, other, planes, first, size):
    core, spot = places[2], places[3]
    stride = mine.shape[0] // planes
    for c, pieces in ((core, mine), (1 - core, other)):
        for k in range(planes):
            at = pl.multiple_of((c * planes + (spot ^ k)) * size, 16)
            buf[pl.ds(at, size), :] = pieces[k * stride + first : k * stride + first + size, :].astype(
                F32
            )


def finish_kernel(
    total, planes, sizes, places, mine, other, up, side, stays,
    grad, fc1, fc2, proj, fc1_b, g2, b2, fc2_b, proj_b, qkv, g1, b1, q_b, v_b, rel, buf1, buf2,
):
    collect(places, buf1, mine, other, planes, 0, sizes[0])
    collect(places, buf2, mine, other, planes, sizes[0], sizes[1])
    d = proj.shape[0]
    ff = fc1.shape[1] // d
    at = (2 * ff + 1) * d
    rows = buf1[at : at + 16, :] + buf1[at + 16 : at + 32, :]
    scale = total / rows[ff + 4 : ff + 5, :]
    rows = rows * scale
    wide = scale.reshape(1, 1, 1, d)
    rest = up.shape[0]
    grad[:rest, :SHIFT] = side[: rest].astype(F32) * wide
    grad[:rest, SHIFT:] = up[:, :-SHIFT].astype(F32) * wide
    grad[rest:, :SHIFT] = side[rest:].astype(F32) * wide
    grad[rest:, SHIFT:] = stays[...] * wide
    for j in range(ff):
        fc1[:, j * d : (j + 1) * d] = buf1[j * d : (j + 1) * d, :] * scale
        fc2[j * d : (j + 1) * d, :] = buf1[(ff + j) * d : (ff + j + 1) * d, :] * scale
        fc1_b[:, j * d : (j + 1) * d] = rows[j : j + 1]
    proj[...] = buf1[2 * ff * d : (2 * ff + 1) * d, :] * scale
    for k, ref in enumerate((g2, b2, fc2_b, proj_b)):
        ref[...] = rows[ff + k : ff + k + 1]
    for j in range(3):
        qkv[:, j * d : (j + 1) * d] = buf2[j * d : (j + 1) * d, :] * scale
    at = 3 * d
    rows = (buf2[at : at + 32, :] + buf2[at + 32 : at + 64, :]) * scale
    for k, ref in enumerate((g1, b1, q_b, v_b)):
        ref[...] = rows[k : k + 1]
    heads = rel.shape[0]
    rel[:, :d] = rows[8 : 8 + heads]
    rel[:, d:] = rows[16 : 16 + heads, : rel.shape[1] - d]


def permute(block, target):
    rows, cols = lax.axis_size("rows"), lax.axis_size("cols")
    route = []
    for r in range(rows):
        for c in range(cols):
            tr, tc = target(r, c)
            route.append((r * cols + c, (tr % rows) * cols + tc % cols))
    return lax.ppermute(block, ("rows", "cols"), route)


def after(values, done):
    return lax.optimization_barrier((values, done))[0]


def core_hop(r, c):
    return r ^ 1, c


def plane_hop(k):
    cols = lax.axis_size("cols")
    return lambda r, c: (r ^ (2 * (k // cols)), c ^ (k % cols))


def plane_share(pieces):
    return [pieces[0]] + [permute(p, plane_hop(k)) for k, p in enumerate(pieces) if k]


def depth_share(piece):
    got = [piece]
    for k in range(1, lax.axis_size("rows") // 4):
        got.append(permute(piece, lambda r, c, k=k: (r ^ (4 * k), c)))
    return got


def strip_hops():
    return [lambda r, c: (r - 1, c), lambda r, c: (r, c - 1), lambda r, c: (r - 1, c - 1)]


def in_vmem():
    return pl.BlockSpec(memory_space=pltpu.VMEM)


def in_smem():
    return pl.BlockSpec(memory_space=pltpu.SMEM)


def to_vmem(a):
    return pltpu.with_memory_space_constraint(a, pltpu.VMEM)


def limit(mib):
    return pltpu.CompilerParams(vmem_limit_bytes=mib * 1024 * 1024)


def strip_shapes(field):
    rows, cols, pages, d = field.shape
    return [
        pltpu.VMEM(s, BF16)
        for s in (
            (SHIFT, cols, pages, d), (rows - SHIFT, SHIFT, pages, d), (SHIFT, SHIFT, pages, d)
        )
    ]


def in_hbm():
    return pl.BlockSpec(memory_space=pltpu.HBM)


def to_hbm(a):
    return pltpu.with_memory_space_constraint(a, pltpu.HBM)


def strips_call(field):
    return pl.pallas_call(
        strips_kernel,
        in_specs=[in_hbm()],
        out_specs=[in_vmem()] * 3,
        out_shape=strip_shapes(field),
        scratch_shapes=[pltpu.SemaphoreType.DMA((3,))],
        compiler_params=limit(4),
        name="input_strips",
    )(to_hbm(field))


def target_call(target, kept, table):
    return pl.pallas_call(
        target_kernel,
        in_specs=[in_hbm()] * 3,
        out_specs=[in_vmem()] * 6,
        out_shape=[
            pltpu.VMEM(target.shape, BF16), *strip_shapes(target),
            pltpu.VMEM((1, target.shape[-1]), F32), pltpu.VMEM(table.shape, F32),
        ],
        scratch_shapes=[
            pltpu.VMEM(target.shape, BF16), pltpu.VMEM(kept.shape, kept.dtype),
            pltpu.SemaphoreType.DMA((3,)),
        ],
        compiler_params=limit(8),
        name="masked_target",
    )(*map(to_hbm, (target, kept, table)))


def split_call(places, mine, other):
    planes = 2 * lax.axis_size("cols")
    n, d = mine.shape
    return pl.pallas_call(
        split_kernel,
        in_specs=[in_smem()] + [in_vmem()] * 2,
        out_specs=[in_vmem()] * planes,
        out_shape=[pltpu.VMEM((n // planes, d), BF16)] * planes,
        compiler_params=limit(4),
        name="split_sums",
    )(places, *map(to_vmem, (mine, other)))


def local_call(kernel, rows, parts, name):
    return pl.pallas_call(
        kernel,
        in_specs=[in_vmem()] * len(parts),
        out_specs=in_vmem(),
        out_shape=pltpu.VMEM((rows,) + parts[-1].shape[1:], BF16),
        compiler_params=limit(4),
        name=name,
    )(*map(to_vmem, parts))


def sum_call(parts):
    return local_call(sum_kernel, parts[0].shape[0], parts, "add_pieces")


def join_call(parts):
    return local_call(join_kernel, sum(a.shape[0] for a in parts), parts, "join_pieces")


def side_call(*parts):
    return local_call(side_kernel, sum(a.shape[0] for a in parts), parts, "side_strip")


def bias_call(places, rel_table):
    heads = rel_table.shape[0]
    return pl.pallas_call(
        bias_kernel,
        in_specs=[in_smem(), in_vmem()],
        out_specs=in_vmem(),
        out_shape=pltpu.VMEM((2, ROWS * heads, KEYS), F32),
        scratch_shapes=[pltpu.VMEM((heads, RELS), F32)],
        compiler_params=limit(VMEM_LIMIT),
        name="attention_bias",
    )(places, to_vmem(rel_table))


def cost(flops):
    return pl.CostEstimate(flops=flops, bytes_accessed=10**7, transcendentals=10**6)


def attention_call(patches, p_strips, qkv_w, bias, g1, b1, q_b, v_b):
    pages, d = patches.shape[2:]
    heads = bias.shape[1] // ROWS
    tokens = 2 * TOK * pages
    shape = pltpu.VMEM
    inputs = [patches, *p_strips, qkv_w, bias, g1, b1, q_b, v_b]
    outs = [
        shape((tokens, d), BF16),
        shape((2, pages, ROWS, d), BF16),
        shape((2, pages, KEYS, 3 * d), BF16),
        shape((2, pages, heads * ROWS, KEYS), BF16),
        shape((d // KEYS, 2, TOK * pages, KEYS), F32),
    ]
    return pl.pallas_call(
        attention_kernel,
        in_specs=[in_vmem()] * len(inputs),
        out_specs=[in_vmem()] * len(outs),
        out_shape=outs,
        scratch_shapes=[pltpu.VMEM((d // KEYS, 2, ROWS * pages, KEYS), F32)],
        compiler_params=limit(VMEM_LIMIT),
        cost_estimate=cost(10**10),
        name="attention_forward",
    )(*map(to_vmem, inputs))


def mlp_call(size, places, x, mixed, masked, t_strips, count, *weights):
    height, width, pages, d = masked.shape
    ff = weights[1].shape[1]
    shape = pltpu.VMEM
    inputs = [x, mixed, masked, *t_strips, count, *weights]
    rest = WIN - SHIFT
    outs = [
        shape((SHIFT, width - SHIFT, pages, d), BF16), shape((rest, width, pages, d), BF16),
        shape((SHIFT, SHIFT, pages, d), BF16),
        shape((d // KEYS, 2, ROWS * pages, KEYS), F32),
        shape((d // KEYS, 2, ROWS * pages, KEYS), F32),
        shape((size // 2, d), BF16), shape((size // 2, d), BF16),
    ]
    return pl.pallas_call(
        mlp_kernel,
        in_specs=[in_smem()] + [in_vmem()] * len(inputs),
        out_specs=[in_vmem()] * len(outs),
        out_shape=outs,
        scratch_shapes=[
            pltpu.VMEM((height, width, pages, d), BF16),
            pltpu.VMEM((size, d), BF16),
            pltpu.VMEM((d // KEYS, 2, TOK * pages, KEYS), F32),
            pltpu.VMEM((d, ff), F32),
            pltpu.VMEM((d, ff), F32),
            pltpu.VMEM((d, d), F32),
            pltpu.VMEM((8, ff), F32),
            pltpu.VMEM((4, 8, d), F32),
        ],
        compiler_params=limit(VMEM_LIMIT),
        cost_estimate=cost(10**10),
        name="mlp_forward_backward",
    )(places, *map(to_vmem, inputs))


def backward_call(size, places, xw, qkv, probs, dy, do, qkv_w, g1, b1):
    pages, d = xw.shape[1], xw.shape[3]
    heads = probs.shape[2] // ROWS
    shape = pltpu.VMEM
    inputs = [xw, qkv, probs, dy, do, qkv_w, g1, b1]
    rest = WIN - SHIFT
    outs = [
        shape((SHIFT, 2 * WIN - SHIFT, pages, d), F32), shape((SHIFT, SHIFT, pages, d), BF16),
        shape((rest, 2 * WIN, pages, d), BF16), shape((size // 2, d), BF16),
        shape((size // 2, d), BF16),
    ]
    return pl.pallas_call(
        backward_kernel,
        in_specs=[in_smem()] + [in_vmem()] * len(inputs),
        out_specs=[in_vmem()] * len(outs),
        out_shape=outs,
        scratch_shapes=[
            shape((d // KEYS, 2, TOK * pages, KEYS), F32),
            shape((d, 3 * d), F32),
            shape((ROWS, heads * KEYS), F32),
            shape((8, 3 * d), F32),
            shape((2, 8, d), F32),
            shape((ROWS * heads, KEYS), F32),
            shape((size, d), BF16),
        ],
        compiler_params=limit(VMEM_LIMIT),
        cost_estimate=cost(10**10),
        name="attention_backward",
    )(places, *map(to_vmem, inputs))


def finish_call(total, planes, ff, n1, n2, rel_shape, places, *inputs):
    d = inputs[0].shape[1]
    row = (1, d)
    field = (WIN,) + inputs[2].shape[1:]
    shapes = [field, (d, ff), (ff, d), (d, d), (1, ff), row, row, row, row, (d, 3 * d)]
    shapes += [row, row, row, row, rel_shape]
    sizes = (n1 // (2 * planes), n2 // (2 * planes))
    return pl.pallas_call(
        lambda *refs: finish_kernel(total, planes, sizes, *refs),
        in_specs=[in_smem()] + [in_vmem()] * len(inputs),
        out_shape=[jax.ShapeDtypeStruct(s, F32) for s in shapes],
        scratch_shapes=[pltpu.VMEM((n1, d), F32), pltpu.VMEM((n2, d), F32)],
        compiler_params=limit(VMEM_LIMIT),
        name="finish_sums",
    )(places, *map(to_vmem, inputs))


def shards(
    patches, target, kept_mask, ln1_gain, ln1_bias, qkv_weight, query_bias, value_bias, rel_table,
    proj_weight, proj_bias, ln2_gain, ln2_bias, fc1_weight, fc1_bias, fc2_weight, fc2_bias,
):
    pages, height, width, d = patches.shape
    ff = fc1_weight.shape[1]
    rows, cols = lax.axis_size("rows"), lax.axis_size("cols")
    r, c = lax.axis_index("rows"), lax.axis_index("cols")
    planes = 2 * cols
    step = 32 * planes
    tokens = pages * height * width
    vec = lambda a: a.reshape(1, -1)
    n1 = -(-(2 * ff + d + 32) // step) * step
    n2 = -(-(3 * d + 64) // step) * step

    places = jnp.stack([r == rows - 1, c == cols - 1, r & 1, ((r >> 1) & 1) * cols + c])
    places = places.astype(jnp.int32)
    patches = patches.transpose(1, 2, 0, 3)
    p_strips = [permute(a, hop) for a, hop in zip(strips_call(patches), strip_hops())]
    masked, *t_strips, count, table = target_call(
        target.transpose(1, 2, 0, 3), kept_mask.transpose(1, 0, 2), rel_table
    )
    t_strips = [permute(a, hop) for a, hop in zip(t_strips, strip_hops())]
    bias = bias_call(places, table)

    g1, b1 = vec(ln1_gain), vec(ln1_bias)
    x, xw, qkv, probs, mixed = attention_call(
        patches, p_strips, qkv_weight, bias, g1, b1, vec(query_bias), vec(value_bias)
    )
    out_stays, out_up, out_side, dy, do, mine, other = mlp_call(
        n1, places, x, mixed, masked, t_strips, count, proj_weight, fc1_weight, fc2_weight,
        vec(proj_bias), vec(ln2_gain), vec(ln2_bias), vec(fc1_bias), vec(fc2_bias),
    )

    to_right, to_below = (lambda r, c: (r, c + 1)), (lambda r, c: (r + 1, c))
    out_up = permute(out_up, to_below)

    pieces = split_call(places, mine, permute(other, core_hop))
    got = plane_share(pieces)
    do = after(do, pieces)
    stays, side, up, mine2, other2 = backward_call(
        n2, places, xw, qkv, probs, dy, do, qkv_weight, g1, b1
    )
    got, out_up = after((got, out_up), mine2)
    piece = sum_call(got)
    mine2, other2, up, out_up = after((mine2, other2, up, out_up), piece)
    up = permute(up, to_below)
    pieces2 = split_call(places, mine2, permute(other2, core_hop))
    got = depth_share(piece)
    got2 = plane_share(pieces2)
    piece2 = sum_call(got2)
    side, up = after((side, up), piece2)
    side = permute(side_call(out_up, out_side, up, side), to_right)
    got2 = depth_share(piece2)
    piece = sum_call(got)
    piece2 = sum_call(got2)

    piece = join_call([piece, piece2])
    piece, side = after((piece, side), side)
    mine = join_call(plane_share([piece] * planes))
    other = permute(mine, core_hop)
    rest = WIN - SHIFT
    top = jnp.concatenate([side[:rest], out_up[:, :-SHIFT]], 1)
    bottom = jnp.concatenate([side[rest:WIN], out_stays], 1)
    output = jnp.concatenate([top, bottom], 0)
    mine, output = after((mine, output), output)
    total = float(tokens * rows * cols)
    (
        grad, fc1_g, fc2_g, proj_g, fc1_bg, g2_g, b2_g, fc2_bg, proj_bg, qkv_g, g1_g, b1_g, q_bg,
        v_bg, rel_g,
    ) = finish_call(
        total, planes, ff, n1, n2, rel_table.shape, places, mine, other, up, side[WIN:], stays
    )
    flat = lambda a: a.reshape(-1)
    return (
        output.transpose(2, 0, 1, 3),
        grad.transpose(2, 0, 1, 3),
        flat(g1_g),
        flat(b1_g),
        qkv_g,
        flat(q_bg),
        flat(v_bg),
        rel_g,
        proj_g,
        flat(proj_bg),
        flat(g2_g),
        flat(b2_g),
        fc1_g,
        flat(fc1_bg),
        fc2_g,
        flat(fc2_bg),
    )


def solution(mesh):
    field = P(None, "rows", "cols", None)
    return jax.shard_map(
        shards,
        mesh=mesh,
        in_specs=(field, field, P(None, "rows", "cols")) + (P(),) * 14,
        out_specs=(field, field) + (P(),) * 14,
        check_vma=False,
    )
```

```python
import math

import jax
import jax.numpy as jnp
from jax import lax
from jax.experimental import pallas as pl
from jax.experimental.pallas import tpu as pltpu
from jax.sharding import PartitionSpec as P

WIN = 10
SHIFT = 5
EPS = 1e-05
F32 = jnp.float32
BF16 = jnp.bfloat16

SPAN = 2 * WIN - 1
TOK = WIN * WIN
ROWS = 104
KEYS = 128
GROUP = 4
RELS = 384
NEVER = -1e30
PAGES = 8
BACK_AT_ONCE = 1
AT_ONCE = 4
VMEM_LIMIT = 20


def dot(a, b):
    return lax.dot_general(a, b, (((1,), (0,)), ((), ())), preferred_element_type=F32)


def dot_bt(a, b):
    return lax.dot_general(a, b, (((1,), (1,)), ((), ())), preferred_element_type=F32)


def dot_at(a, b):
    return lax.dot_general(a, b, (((0,), (0,)), ((), ())), preferred_element_type=F32)


def normalize(x):
    center = x - jnp.sum(x, -1, keepdims=True) * (1.0 / x.shape[-1])
    inv = lax.rsqrt(jnp.sum(center * center, -1, keepdims=True) * (1.0 / x.shape[-1]) + EPS)
    return center * inv, inv


def norm_back(up, normed, inv):
    scale = 1.0 / up.shape[-1]
    mean_up = jnp.sum(up, -1, keepdims=True) * scale
    mean_un = jnp.sum(up * normed, -1, keepdims=True) * scale
    return inv * (up - mean_up - normed * mean_un)


def fold(x):
    return jnp.sum(x.reshape(x.shape[0] // 8, 8, x.shape[1]), 0)


def head_masks(rows, dtype):
    lane = lax.broadcasted_iota(jnp.int32, (rows, KEYS), 1)
    width = KEYS // GROUP
    return [
        ((lane >= k * width) & (lane < (k + 1) * width)).astype(F32).astype(dtype)
        for k in range(GROUP)
    ]


def head_rows(x, masks):
    return jnp.concatenate([x * m for m in masks], 0).astype(BF16)


def own_lanes(stacked):
    lane = lax.broadcasted_iota(jnp.int32, (ROWS, KEYS), 1)
    out = stacked[(GROUP - 1) * ROWS :]
    for h in reversed(range(GROUP - 1)):
        out = jnp.where(lane < (h + 1) * (KEYS // GROUP), stacked[h * ROWS : (h + 1) * ROWS], out)
    return out


def split_rows(x):
    high = x.astype(BF16)
    return high, (x - high.astype(F32)).astype(BF16)


def page_rows(page, count):
    return pl.ds(page, count, stride=PAGES)


def load_rows(ref, w, rows):
    return jnp.concatenate([ref[t, w, rows, :] for t in range(ref.shape[0])], 1)


def store_rows(ref, w, rows, value):
    for t in range(ref.shape[0]):
        ref[t, w, rows, :] = value[:, t * KEYS : (t + 1) * KEYS]


def only_tokens(x):
    return jnp.where(lax.broadcasted_iota(jnp.int32, x.shape, 0) < TOK, x, 0.0)


def gather_frame(out, own, low, right, corner):
    for w in range(2):
        for r in range(WIN):
            if r < WIN - SHIFT:
                main, side, mr, sr = own, right, r + SHIFT, r
            else:
                main, side, mr, sr = low, corner, r - SHIFT, r - SHIFT
            if w == 0:
                block = main[mr, SHIFT : SHIFT + WIN].astype(F32)
            else:
                block = jnp.concatenate(
                    [main[mr, SHIFT + WIN :].astype(F32), side[sr].astype(F32)], 0
                )
            at = r * WIN * PAGES
            store_rows(
                out, w, slice(at, at + WIN * PAGES), block.reshape(WIN * PAGES, block.shape[-1])
            )


def tenth(n):
    return (n * 205) >> 11


def squeeze_matrix():
    at = lax.broadcasted_iota(jnp.int32, (RELS, 2 * KEYS), 0)
    to = lax.broadcasted_iota(jnp.int32, (RELS, 2 * KEYS), 1)
    hit = (at == to + (SPAN - WIN) * tenth(to)) & (to < SPAN * WIN)
    return hit.astype(F32).astype(BF16)


def copy_all(pairs, sems):
    copies = [pltpu.make_async_copy(a, b, sems.at[k]) for k, (a, b) in enumerate(pairs)]
    for copy in copies:
        copy.start()
    for copy in copies:
        copy.wait()


def strips_kernel(field, low, right, corner, sems):
    copy_all(
        (
            (field.at[:SHIFT], low), (field.at[SHIFT:, :SHIFT], right),
            (field.at[:SHIFT, :SHIFT], corner),
        ),
        sems,
    )


def target_kernel(
    target_in, kept_in, table_in, masked, low, right, corner, count, table, target, kept, sems
):
    copy_all(((target_in, target), (kept_in, kept), (table_in, table)), sems)
    rows, cols = target.shape[:2]
    total = jnp.zeros(kept.shape[1:], F32)
    for r in range(rows):
        kept_row = kept[r].astype(F32)
        total = total + kept_row
        for c in range(cols):
            masked[r, c] = (target[r, c].astype(F32) * kept_row[:, c : c + 1]).astype(BF16)
    low[...] = masked[:SHIFT]
    right[...] = masked[SHIFT:, :SHIFT]
    corner[...] = masked[:SHIFT, :SHIFT]
    total = jnp.sum(jnp.sum(total, 1, keepdims=True), 0, keepdims=True)
    count[...] = jnp.broadcast_to(total, count.shape)


def split_halves(places, sums, mine, other):
    size = mine.shape[0]
    core = places[2]
    mine[...] = sums[pl.ds(pl.multiple_of(core * size, 16), size), :]
    other[...] = sums[pl.ds(pl.multiple_of((1 - core) * size, 16), size), :]


def split_kernel(places, mine, other, *outs):
    size = outs[0].shape[0]
    for k, out in enumerate(outs):
        at = pl.ds(pl.multiple_of((places[3] ^ k) * size, 16), size)
        out[...] = (mine[at, :].astype(F32) + other[at, :].astype(F32)).astype(BF16)


def tree_sum(parts):
    while len(parts) > 1:
        parts = [parts[i] + parts[i + 1] for i in range(0, len(parts), 2)]
    return parts[0]


def sum_kernel(*refs):
    refs[-1][...] = tree_sum([ref[...].astype(F32) for ref in refs[:-1]]).astype(BF16)


def join_kernel(*refs):
    out, at = refs[-1], 0
    for ref in refs[:-1]:
        out[at : at + ref.shape[0]] = ref[...]
        at += ref.shape[0]


def split_three(x):
    high = x.astype(BF16)
    rest = x - high.astype(F32)
    middle = rest.astype(BF16)
    return high, middle, (rest - middle.astype(F32)).astype(BF16)


def bias_kernel(edge, table, out, padded):
    heads = table.shape[0]
    padded[...] = jnp.zeros_like(padded)
    padded[:, : table.shape[1]] = table[...]
    offsets = padded[...]
    moved = []
    for c in range(WIN):
        shift = WIN - 1 - c
        moved.append(pltpu.roll(offsets, RELS - shift, 1) if shift else offsets)
    stack = jnp.concatenate(moved, 0)
    high, middle, least = split_three(stack)
    squeeze = squeeze_matrix()
    wide = dot(high, squeeze) + dot(middle, squeeze) + dot(least, squeeze)
    count = WIN * heads
    for r in range(WIN):
        shift = (WIN - 1 - r) * WIN
        rel = pltpu.roll(wide, 2 * KEYS - shift, 1) if shift else wide
        rel = rel[:, :KEYS]
        query = lax.broadcasted_iota(jnp.int32, (count, KEYS), 1)
        row = lax.broadcasted_iota(jnp.int32, (count, KEYS), 0)
        across = (query < TOK // 2) if r >= SHIFT else (query >= TOK // 2)
        query_left = query - WIN * tenth(query) < SHIFT
        own_left = row < SHIFT * heads
        beside = query_left != own_left
        for w in range(2):
            cut_off = across & (edge[0] != 0)
            if w == 1:
                cut_off = cut_off | (beside & (edge[1] != 0))
            value = rel + jnp.where(cut_off, -100.0, 0.0)
            out[w, r * count : (r + 1) * count, :] = value
    for w in range(2):
        out[w, TOK * heads :, :] = jnp.full((out.shape[1] - TOK * heads, KEYS), NEVER, F32)


def attention_kernel(
    own, low, right, corner, qkv_w, bias, g1, b1, qb, vb,
    x_out, xw_out, qkv_out, p_out, o_out,
    xf,
):
    gather_frame(xf, own, low, right, corner)
    for t in range(xf.shape[0]):
        for w in range(2):
            xf[t, w, TOK * PAGES :, :] = jnp.zeros((xf.shape[2] - TOK * PAGES, KEYS), F32)
            x_out[w * TOK * PAGES : (w + 1) * TOK * PAGES, t * KEYS : (t + 1) * KEYS] = xf[
                t, w, : TOK * PAGES, :
            ].astype(BF16)

    d = g1.shape[-1]
    heads = d // (KEYS // GROUP)
    scale = (d // heads) ** (-0.5)
    windows = [(page, w) for page in range(PAGES) for w in range(2)]
    x = jnp.concatenate(
        [only_tokens(load_rows(xf, w, page_rows(page, ROWS))) for page, w in windows], 0
    )
    xw_out[...] = x.astype(BF16)
    normed, _ = normalize(x)
    attn_in = (normed * g1[...] + b1[...]).astype(BF16)
    proj = dot(attn_in, qkv_w[...])
    q_all = proj[:, :d] + qb[...]
    k_all = proj[:, d : 2 * d]
    v_all = proj[:, 2 * d :] + vb[...]
    masks = head_masks(ROWS, F32)
    filler = jnp.zeros((KEYS - ROWS, d), F32)
    groups = heads // GROUP
    for start in range(0, len(windows), AT_ONCE):
        scores, values = [], []
        some = windows[start : start + AT_ONCE]
        for n, (page, w) in enumerate(some):
            rows = slice((start + n) * ROWS, (start + n + 1) * ROWS)
            q = jnp.concatenate([q_all[rows], filler], 0).astype(BF16)
            k = jnp.concatenate([k_all[rows], filler], 0).astype(BF16)
            v = jnp.concatenate([v_all[rows], filler], 0).astype(BF16)
            qkv_out[w, page, :, :d] = q
            qkv_out[w, page, :, d : 2 * d] = k
            qkv_out[w, page, :, 2 * d :] = v
            for g in range(groups):
                lanes = slice(g * KEYS, (g + 1) * KEYS)
                scores.append(dot_bt(head_rows(k_all[rows, lanes], masks), q[:, lanes]))
                values.append(head_rows(v_all[rows, lanes], masks))
        probs = []
        for n, s in enumerate(scores):
            page, w = some[n // groups]
            g = n % groups
            es = []
            for h in range(GROUP):
                rel = bias[w, pl.ds(g * GROUP + h, ROWS, stride=heads), :]
                sh = s[h * ROWS : (h + 1) * ROWS] * scale + rel
                e = jnp.exp(sh - jnp.max(sh, 0, keepdims=True))
                es.append(e * (1.0 / jnp.sum(e, 0, keepdims=True)))
            p = jnp.concatenate(es, 0).astype(BF16)
            p_out[w, page, g * GROUP * ROWS : (g + 1) * GROUP * ROWS, :] = p
            probs.append(p)
        parts = [dot_at(p, v)[:ROWS] for p, v in zip(probs, values)]
        for n, (page, w) in enumerate(some):
            joined = jnp.concatenate(parts[n * groups : (n + 1) * groups], 1)
            store_rows(o_out, w, page_rows(page, TOK), joined[:TOK])


def mlp_kernel(
    places, x_in, o_in, t_own, t_low, t_right, t_corner, count,
    proj_w, fc1_w, fc2_w, pb, g2, b2, f1b, f2b,
    stays, up, side, corner, dy_out, do_out, mine, other,
    frame_out, sums_out, tf, fc1_acc, fc2_acc, proj_acc, fc1_sum, small_sum,
):
    gather_frame(tf, t_own, t_low, t_right, t_corner)

    mlp_step(
        x_in, o_in, proj_w, fc1_w, fc2_w, pb, g2, b2, f1b, f2b, frame_out, dy_out, do_out,
        tf, fc1_acc, fc2_acc, proj_acc, fc1_sum, small_sum,
    )

    d = proj_w.shape[0]
    ff = fc1_w.shape[1] // d
    for j in range(ff):
        sums_out[j * d : (j + 1) * d, :] = fc1_acc[:, j * d : (j + 1) * d].astype(BF16)
        sums_out[(ff + j) * d : (ff + j + 1) * d, :] = fc2_acc[:, j * d : (j + 1) * d].T.astype(
            BF16
        )
    at = 2 * ff * d
    sums_out[at : at + d, :] = proj_acc[...].astype(BF16)
    rows = [jnp.sum(fc1_sum[:, j * d : (j + 1) * d], 0, keepdims=True) for j in range(ff)]
    rows += [jnp.sum(small_sum[k], 0, keepdims=True) for k in range(4)]
    rows.append(count[...])
    rows.append(jnp.zeros((16 - len(rows), d), F32))
    high, low_part = split_rows(jnp.concatenate(rows, 0))
    at += d
    sums_out[at : at + 16, :] = high
    sums_out[at + 16 : at + 32, :] = low_part
    if sums_out.shape[0] > at + 32:
        sums_out[at + 32 :, :] = jnp.zeros((sums_out.shape[0] - at - 32, d), BF16)
    split_halves(places, sums_out, mine, other)
    stays[...] = frame_out[:SHIFT, :-SHIFT]
    up[...] = frame_out[SHIFT:, :-SHIFT]
    side[...] = frame_out[:SHIFT, -SHIFT:]
    corner[...] = frame_out[SHIFT:, -SHIFT:]


def both_windows(ref):
    return jnp.concatenate([load_rows(ref, w, slice(0, TOK * PAGES)) for w in range(2)], 0)


def mlp_step(
    x_in, o_in, proj_w, fc1_w, fc2_w, pb, g2, b2, f1b, f2b, frame_out, dy_out, do_out,
    tf, fc1_acc, fc2_acc, proj_acc, fc1_sum, small_sum,
):
    d = x_in.shape[1]
    ff = fc1_w.shape[1] // d
    tokens = TOK * PAGES
    o = both_windows(o_in).astype(BF16)
    y = x_in[...].astype(F32) + dot(o, proj_w[...]) + pb[...]
    normed2, inv2 = normalize(y)
    c = (normed2 * g2[...] + b2[...]).astype(BF16)
    dr = both_windows(tf)
    drb = dr.astype(BF16)
    r = y + f2b[...]
    dc = None
    for j in range(ff):
        at = slice(j * d, (j + 1) * d)
        h = dot(c, fc1_w[:, at]) + f1b[:, at]
        phi = 0.5 * (1.0 + lax.erf(h * math.sqrt(0.5)))
        slope = phi + h * (jnp.exp(h * h * -0.5) * (1.0 / math.sqrt(2.0 * math.pi)))
        gelu = (h * phi).astype(BF16)
        dh_wide = dot_bt(drb, fc2_w[at, :]) * slope
        dh = dh_wide.astype(BF16)
        r = r + dot(gelu, fc2_w[at, :])
        fc2_acc[:, at] = dot_at(drb, gelu)
        fc1_acc[:, at] = dot_at(c, dh)
        fc1_sum[:, at] = fold(dh.astype(F32))
        more = dot_bt(dh, fc1_w[:, at])
        dc = more if dc is None else dc + more
    for w in range(2):
        frame_out[:, w * WIN : (w + 1) * WIN] = (
            r[w * tokens : (w + 1) * tokens].reshape(WIN, WIN, PAGES, d).astype(BF16)
        )
    dy = dr + norm_back(dc * g2[...], normed2, inv2)
    dz = dy.astype(BF16)
    proj_acc[...] = dot_at(o, dz)
    do = dot_bt(dz, proj_w[...])
    for w in range(2):
        rows = slice(w * tokens, (w + 1) * tokens)
        store_rows(do_out, w, slice(0, tokens), do[rows])
        store_rows(dy_out, w, slice(0, tokens), dy[rows])
    small_sum[0] = fold(dc * normed2)
    small_sum[1] = fold(dc)
    small_sum[2] = fold(dr)
    small_sum[3] = fold(dz.astype(F32))


def backward_kernel(
    places, xw, qkv, p_in, dy_in, do_in, qkv_w, g1, b1, out_side, out_corner,
    stays, side, corner, up, mine, other,
    dx, qkv_acc, rel_acc, col_sum, small_sum, mixed, sums_out, joined_all,
):
    rel_acc[...] = jnp.zeros_like(rel_acc)
    for page in range(0, PAGES, BACK_AT_ONCE):
        backward_pages(range(page, page + BACK_AT_ONCE), qkv, p_in, do_in, joined_all, rel_acc)

    d = g1.shape[-1]
    heads = d // (KEYS // GROUP)
    joined = joined_all[...]
    normed, inv = normalize(xw[...].astype(F32))
    attn_in = (normed * g1[...] + b1[...]).astype(BF16)
    qkv_acc[...] = dot_at(attn_in, joined)
    col_sum[...] = fold(joined.astype(F32))
    da = dot_bt(joined, qkv_w[...])
    small_sum[0] = fold(da * normed)
    small_sum[1] = fold(da)
    back = norm_back(da * g1[...], normed, inv)
    for page in range(PAGES):
        rows = page_rows(page, TOK)
        for w in range(2):
            at = (2 * page + w) * ROWS
            store_rows(dx, w, rows, load_rows(dy_in, w, rows) + back[at : at + TOK])
    right = load_rows(dx, 1, slice(None)).reshape(WIN, WIN, PAGES, d)
    left = load_rows(dx, 0, slice(None)).reshape(WIN, WIN, PAGES, d)
    stays[:, :WIN] = left[:SHIFT]
    stays[:, WIN:] = right[:SHIFT, :SHIFT]
    side[:SHIFT] = out_side[...]
    side[SHIFT:] = right[:SHIFT, SHIFT:].astype(BF16)
    corner[: WIN - SHIFT] = out_corner[...]
    corner[WIN - SHIFT :] = right[SHIFT:, SHIFT:].astype(BF16)
    up[:, :WIN] = left[SHIFT:].astype(BF16)
    up[:, WIN:] = right[SHIFT:, :SHIFT].astype(BF16)
    for j in range(3):
        sums_out[j * d : (j + 1) * d, :] = qkv_acc[:, j * d : (j + 1) * d].astype(BF16)
    rel = table_gradient(
        [rel_acc[:, h * KEYS : (h + 1) * KEYS] for h in range(heads)], mixed
    )
    rows = [jnp.sum(small_sum[k], 0, keepdims=True) for k in range(2)]
    rows.append(jnp.sum(col_sum[:, :d], 0, keepdims=True))
    rows.append(jnp.sum(col_sum[:, 2 * d :], 0, keepdims=True))
    rows.append(jnp.zeros((4, d), F32))
    rows.append(rel[:, :d])
    rows.append(jnp.concatenate([rel[:, d:], jnp.zeros((heads, 2 * d - RELS), F32)], 1))
    rows.append(jnp.zeros((8, d), F32))
    high, rest = split_rows(jnp.concatenate(rows, 0))
    at = 3 * d
    sums_out[at : at + 32, :] = high
    sums_out[at + 32 : at + 64, :] = rest
    if sums_out.shape[0] > at + 64:
        sums_out[at + 64 :, :] = jnp.zeros((sums_out.shape[0] - at - 64, d), BF16)
    split_halves(places, sums_out, mine, other)


def backward_pages(pages, qkv, p_in, do_in, joined_all, rel_acc):
    d = qkv.shape[-1] // 3
    heads = d // (KEYS // GROUP)
    groups = heads // GROUP
    scale = (d // heads) ** (-0.5)
    masks = head_masks(ROWS, F32)
    chains = [(page, w, g) for page in pages for w in range(2) for g in range(groups)]
    queries, keys, dos, dps = [], [], [], []
    filler = jnp.zeros((KEYS - ROWS, KEYS), F32)
    for page, w, g in chains:
        lanes = slice(g * KEYS, (g + 1) * KEYS)
        queries.append(qkv[w, page, :, lanes])
        k = qkv[w, page, :, d + g * KEYS : d + (g + 1) * KEYS]
        v = qkv[w, page, :, 2 * d + g * KEYS : 2 * d + (g + 1) * KEYS]
        keys.append(head_rows(k.astype(F32)[:ROWS], masks))
        do = only_tokens(do_in[g, w, page_rows(page, ROWS), :])
        dos.append(jnp.concatenate([do, filler], 0).astype(BF16))
        dps.append(dot_bt(head_rows(v.astype(F32)[:ROWS], masks), dos[-1]))
    dts = []
    rel_sum = [None] * heads
    for c, (page, w, g) in enumerate(chains):
        p = p_in[w, page, g * GROUP * ROWS : (g + 1) * GROUP * ROWS, :].astype(F32)
        t = p * dps[c]
        ds = []
        for h in range(GROUP):
            at = slice(h * ROWS, (h + 1) * ROWS)
            part = t[at] - p[at] * jnp.sum(t[at], 0, keepdims=True)
            head = g * GROUP + h
            rel_sum[head] = part if rel_sum[head] is None else rel_sum[head] + part
            ds.append(part * scale)
        dts.append(jnp.concatenate(ds, 0).astype(BF16))
    for h in range(heads):
        rel_acc[:, h * KEYS : (h + 1) * KEYS] += rel_sum[h]
    parts = {}
    for c, (page, w, g) in enumerate(chains):
        p = p_in[w, page, g * GROUP * ROWS : (g + 1) * GROUP * ROWS, :]
        parts[0, page, w, g] = dot_at(dts[c], keys[c])[:ROWS]
        parts[1, page, w, g] = own_lanes(dot(dts[c], queries[c]))
        parts[2, page, w, g] = own_lanes(dot(p, dos[c]))
    for page in pages:
        for k in range(3):
            for g in range(groups):
                joined = jnp.concatenate([parts[k, page, w, g] for w in range(2)], 0)
                at = k * d + g * KEYS
                joined_all[2 * page * ROWS : 2 * (page + 1) * ROWS, at : at + KEYS] = joined.astype(
                    BF16
                )


def table_gradient(by_head, mixed):
    heads = len(by_head)
    for h in range(heads):
        mixed[pl.ds(h, ROWS, stride=heads), :] = by_head[h]
    wide = None
    for r in range(WIN):
        part = mixed[r * WIN * heads : (r + 1) * WIN * heads, :]
        part = jnp.concatenate([part, jnp.zeros_like(part)], 1)
        shift = (WIN - 1 - r) * WIN
        part = pltpu.roll(part, shift, 1) if shift else part
        wide = part if wide is None else wide + part
    high, rest = split_rows(wide)
    squeeze = squeeze_matrix()
    moved = dot_bt(high, squeeze) + dot_bt(rest, squeeze)
    total = None
    for c in range(WIN):
        part = moved[c * heads : (c + 1) * heads]
        shift = WIN - 1 - c
        part = pltpu.roll(part, shift, 1) if shift else part
        total = part if total is None else total + part
    return total


def collect(places, buf, mine, other, planes, first, size):
    core, spot = places[2], places[3]
    stride = mine.shape[0] // planes
    for c, pieces in ((core, mine), (1 - core, other)):
        for k in range(planes):
            at = pl.multiple_of((c * planes + (spot ^ k)) * size, 16)
            buf[pl.ds(at, size), :] = pieces[k * stride + first : k * stride + first + size, :].astype(
                F32
            )


def finish_kernel(
    total, planes, sizes, places, mine, other, up, side, corner, stays,
    grad, fc1, fc2, proj, fc1_b, g2, b2, fc2_b, proj_b, qkv, g1, b1, q_b, v_b, rel, buf1, buf2,
):
    collect(places, buf1, mine, other, planes, 0, sizes[0])
    collect(places, buf2, mine, other, planes, sizes[0], sizes[1])
    d = proj.shape[0]
    ff = fc1.shape[1] // d
    at = (2 * ff + 1) * d
    rows = buf1[at : at + 16, :] + buf1[at + 16 : at + 32, :]
    scale = total / rows[ff + 4 : ff + 5, :]
    rows = rows * scale
    wide = scale.reshape(1, 1, 1, d)
    rest = up.shape[0]
    grad[:rest, :SHIFT] = corner[rest:].astype(F32) * wide
    grad[:rest, SHIFT:] = up[...].astype(F32) * wide
    grad[rest:, :SHIFT] = side[SHIFT:].astype(F32) * wide
    grad[rest:, SHIFT:] = stays[...] * wide
    for j in range(ff):
        fc1[:, j * d : (j + 1) * d] = buf1[j * d : (j + 1) * d, :] * scale
        fc2[j * d : (j + 1) * d, :] = buf1[(ff + j) * d : (ff + j + 1) * d, :] * scale
        fc1_b[:, j * d : (j + 1) * d] = rows[j : j + 1]
    proj[...] = buf1[2 * ff * d : (2 * ff + 1) * d, :] * scale
    for k, ref in enumerate((g2, b2, fc2_b, proj_b)):
        ref[...] = rows[ff + k : ff + k + 1]
    for j in range(3):
        qkv[:, j * d : (j + 1) * d] = buf2[j * d : (j + 1) * d, :] * scale
    at = 3 * d
    rows = (buf2[at : at + 32, :] + buf2[at + 32 : at + 64, :]) * scale
    for k, ref in enumerate((g1, b1, q_b, v_b)):
        ref[...] = rows[k : k + 1]
    heads = rel.shape[0]
    rel[:, :d] = rows[8 : 8 + heads]
    rel[:, d:] = rows[16 : 16 + heads, : rel.shape[1] - d]


def permute(block, target):
    rows, cols = lax.axis_size("rows"), lax.axis_size("cols")
    route = []
    for r in range(rows):
        for c in range(cols):
            tr, tc = target(r, c)
            route.append((r * cols + c, (tr % rows) * cols + tc % cols))
    return lax.ppermute(block, ("rows", "cols"), route)


def after(values, done):
    return lax.optimization_barrier((values, done))[0]


def core_hop(r, c):
    return r ^ 1, c


def plane_hop(k):
    cols = lax.axis_size("cols")
    return lambda r, c: (r ^ (2 * (k // cols)), c ^ (k % cols))


def plane_share(pieces):
    return [pieces[0]] + [permute(p, plane_hop(k)) for k, p in enumerate(pieces) if k]


def depth_sum(piece):
    hop = 4
    while hop < lax.axis_size("rows"):
        piece = sum_call([piece, permute(piece, lambda r, c, hop=hop: (r ^ hop, c))])
        hop *= 2
    return piece


def strip_hops():
    return [lambda r, c: (r - 1, c), lambda r, c: (r, c - 1), lambda r, c: (r - 1, c - 1)]


def in_vmem():
    return pl.BlockSpec(memory_space=pltpu.VMEM)


def in_smem():
    return pl.BlockSpec(memory_space=pltpu.SMEM)


def to_vmem(a):
    return pltpu.with_memory_space_constraint(a, pltpu.VMEM)


def limit(mib):
    return pltpu.CompilerParams(vmem_limit_bytes=mib * 1024 * 1024)


def strip_shapes(field):
    rows, cols, pages, d = field.shape
    return [
        pltpu.VMEM(s, BF16)
        for s in (
            (SHIFT, cols, pages, d), (rows - SHIFT, SHIFT, pages, d), (SHIFT, SHIFT, pages, d)
        )
    ]


def in_hbm():
    return pl.BlockSpec(memory_space=pltpu.HBM)


def to_hbm(a):
    return pltpu.with_memory_space_constraint(a, pltpu.HBM)


def strips_call(field):
    return pl.pallas_call(
        strips_kernel,
        in_specs=[in_hbm()],
        out_specs=[in_vmem()] * 3,
        out_shape=strip_shapes(field),
        scratch_shapes=[pltpu.SemaphoreType.DMA((3,))],
        compiler_params=limit(4),
        name="input_strips",
    )(to_hbm(field))


def target_call(target, kept, table):
    return pl.pallas_call(
        target_kernel,
        in_specs=[in_hbm()] * 3,
        out_specs=[in_vmem()] * 6,
        out_shape=[
            pltpu.VMEM(target.shape, BF16), *strip_shapes(target),
            pltpu.VMEM((1, target.shape[-1]), F32), pltpu.VMEM(table.shape, F32),
        ],
        scratch_shapes=[
            pltpu.VMEM(target.shape, BF16), pltpu.VMEM(kept.shape, kept.dtype),
            pltpu.SemaphoreType.DMA((3,)),
        ],
        compiler_params=limit(8),
        name="masked_target",
    )(*map(to_hbm, (target, kept, table)))


def split_call(places, mine, other):
    planes = 2 * lax.axis_size("cols")
    n, d = mine.shape
    return pl.pallas_call(
        split_kernel,
        in_specs=[in_smem()] + [in_vmem()] * 2,
        out_specs=[in_vmem()] * planes,
        out_shape=[pltpu.VMEM((n // planes, d), BF16)] * planes,
        compiler_params=limit(4),
        name="split_sums",
    )(places, *map(to_vmem, (mine, other)))


def local_call(kernel, rows, parts, name):
    return pl.pallas_call(
        kernel,
        in_specs=[in_vmem()] * len(parts),
        out_specs=in_vmem(),
        out_shape=pltpu.VMEM((rows,) + parts[-1].shape[1:], BF16),
        compiler_params=limit(4),
        name=name,
    )(*map(to_vmem, parts))


def sum_call(parts):
    return local_call(sum_kernel, parts[0].shape[0], parts, "add_pieces")


def join_call(parts):
    return local_call(join_kernel, sum(a.shape[0] for a in parts), parts, "join_pieces")


def bias_call(places, rel_table):
    heads = rel_table.shape[0]
    return pl.pallas_call(
        bias_kernel,
        in_specs=[in_smem(), in_vmem()],
        out_specs=in_vmem(),
        out_shape=pltpu.VMEM((2, ROWS * heads, KEYS), F32),
        scratch_shapes=[pltpu.VMEM((heads, RELS), F32)],
        compiler_params=limit(VMEM_LIMIT),
        name="attention_bias",
    )(places, to_vmem(rel_table))


def cost(flops):
    return pl.CostEstimate(flops=flops, bytes_accessed=10**7, transcendentals=10**6)


def attention_call(patches, p_strips, qkv_w, bias, g1, b1, q_b, v_b):
    pages, d = patches.shape[2:]
    heads = bias.shape[1] // ROWS
    tokens = 2 * TOK * pages
    shape = pltpu.VMEM
    inputs = [patches, *p_strips, qkv_w, bias, g1, b1, q_b, v_b]
    outs = [
        shape((tokens, d), BF16),
        shape((2 * pages * ROWS, d), BF16),
        shape((2, pages, KEYS, 3 * d), BF16),
        shape((2, pages, heads * ROWS, KEYS), BF16),
        shape((d // KEYS, 2, TOK * pages, KEYS), F32),
    ]
    return pl.pallas_call(
        attention_kernel,
        in_specs=[in_vmem()] * len(inputs),
        out_specs=[in_vmem()] * len(outs),
        out_shape=outs,
        scratch_shapes=[pltpu.VMEM((d // KEYS, 2, ROWS * pages, KEYS), F32)],
        compiler_params=limit(VMEM_LIMIT),
        cost_estimate=cost(10**10),
        name="attention_forward",
    )(*map(to_vmem, inputs))


def mlp_call(size, places, x, mixed, masked, t_strips, count, *weights):
    height, width, pages, d = masked.shape
    ff = weights[1].shape[1]
    shape = pltpu.VMEM
    inputs = [x, mixed, masked, *t_strips, count, *weights]
    rest = WIN - SHIFT
    outs = [
        shape((SHIFT, width - SHIFT, pages, d), BF16), shape((rest, width - SHIFT, pages, d), BF16),
        shape((SHIFT, SHIFT, pages, d), BF16), shape((rest, SHIFT, pages, d), BF16),
        shape((d // KEYS, 2, ROWS * pages, KEYS), F32),
        shape((d // KEYS, 2, ROWS * pages, KEYS), F32),
        shape((size // 2, d), BF16), shape((size // 2, d), BF16),
    ]
    return pl.pallas_call(
        mlp_kernel,
        in_specs=[in_smem()] + [in_vmem()] * len(inputs),
        out_specs=[in_vmem()] * len(outs),
        out_shape=outs,
        scratch_shapes=[
            pltpu.VMEM((height, width, pages, d), BF16),
            pltpu.VMEM((size, d), BF16),
            pltpu.VMEM((d // KEYS, 2, TOK * pages, KEYS), F32),
            pltpu.VMEM((d, ff), F32),
            pltpu.VMEM((d, ff), F32),
            pltpu.VMEM((d, d), F32),
            pltpu.VMEM((8, ff), F32),
            pltpu.VMEM((4, 8, d), F32),
        ],
        compiler_params=limit(VMEM_LIMIT),
        cost_estimate=cost(10**10),
        name="mlp_forward_backward",
    )(places, *map(to_vmem, inputs))


def backward_call(size, places, xw, qkv, probs, dy, do, *more):
    pages, d = probs.shape[1], xw.shape[1]
    heads = probs.shape[2] // ROWS
    shape = pltpu.VMEM
    inputs = [xw, qkv, probs, dy, do, *more]
    rest = WIN - SHIFT
    outs = [
        shape((SHIFT, 2 * WIN - SHIFT, pages, d), F32), shape((2 * SHIFT, SHIFT, pages, d), BF16),
        shape((2 * rest, SHIFT, pages, d), BF16),
        shape((rest, 2 * WIN - SHIFT, pages, d), BF16), shape((size // 2, d), BF16),
        shape((size // 2, d), BF16),
    ]
    return pl.pallas_call(
        backward_kernel,
        in_specs=[in_smem()] + [in_vmem()] * len(inputs),
        out_specs=[in_vmem()] * len(outs),
        out_shape=outs,
        scratch_shapes=[
            shape((d // KEYS, 2, TOK * pages, KEYS), F32),
            shape((d, 3 * d), F32),
            shape((ROWS, heads * KEYS), F32),
            shape((8, 3 * d), F32),
            shape((2, 8, d), F32),
            shape((ROWS * heads, KEYS), F32),
            shape((size, d), BF16),
            shape((2 * pages * ROWS, 3 * d), BF16),
        ],
        compiler_params=limit(VMEM_LIMIT),
        cost_estimate=cost(10**10),
        name="attention_backward",
    )(places, *map(to_vmem, inputs))


def finish_call(total, planes, ff, n1, n2, rel_shape, places, *inputs):
    d = inputs[0].shape[1]
    row = (1, d)
    field = (WIN, 2 * WIN) + inputs[2].shape[2:]
    shapes = [field, (d, ff), (ff, d), (d, d), (1, ff), row, row, row, row, (d, 3 * d)]
    shapes += [row, row, row, row, rel_shape]
    sizes = (n1 // (2 * planes), n2 // (2 * planes))
    return pl.pallas_call(
        lambda *refs: finish_kernel(total, planes, sizes, *refs),
        in_specs=[in_smem()] + [in_vmem()] * len(inputs),
        out_shape=[jax.ShapeDtypeStruct(s, F32) for s in shapes],
        scratch_shapes=[pltpu.VMEM((n1, d), F32), pltpu.VMEM((n2, d), F32)],
        compiler_params=limit(VMEM_LIMIT),
        name="finish_sums",
    )(places, *map(to_vmem, inputs))


def shards(
    patches, target, kept_mask, ln1_gain, ln1_bias, qkv_weight, query_bias, value_bias, rel_table,
    proj_weight, proj_bias, ln2_gain, ln2_bias, fc1_weight, fc1_bias, fc2_weight, fc2_bias,
):
    pages, height, width, d = patches.shape
    ff = fc1_weight.shape[1]
    rows, cols = lax.axis_size("rows"), lax.axis_size("cols")
    r, c = lax.axis_index("rows"), lax.axis_index("cols")
    planes = 2 * cols
    step = 32 * planes
    tokens = pages * height * width
    vec = lambda a: a.reshape(1, -1)
    n1 = -(-(2 * ff + d + 32) // step) * step
    n2 = -(-(3 * d + 64) // step) * step

    places = jnp.stack([r == rows - 1, c == cols - 1, r & 1, ((r >> 1) & 1) * cols + c])
    places = places.astype(jnp.int32)
    patches = patches.transpose(1, 2, 0, 3)
    p_strips = [permute(a, hop) for a, hop in zip(strips_call(patches), strip_hops())]
    masked, *t_strips, count, table = target_call(
        target.transpose(1, 2, 0, 3), kept_mask.transpose(1, 0, 2), rel_table
    )
    t_strips = [permute(a, hop) for a, hop in zip(t_strips, strip_hops())]
    bias = bias_call(places, table)

    g1, b1 = vec(ln1_gain), vec(ln1_bias)
    x, xw, qkv, probs, mixed = attention_call(
        patches, p_strips, qkv_weight, bias, g1, b1, vec(query_bias), vec(value_bias)
    )
    out_stays, out_up, out_side, out_corner, dy, do, mine, other = mlp_call(
        n1, places, x, mixed, masked, t_strips, count, proj_weight, fc1_weight, fc2_weight,
        vec(proj_bias), vec(ln2_gain), vec(ln2_bias), vec(fc1_bias), vec(fc2_bias),
    )

    to_right, to_below = (lambda r, c: (r, c + 1)), (lambda r, c: (r + 1, c))
    across = lambda r, c: (r + 1, c + 1)
    out_up = permute(out_up, to_below)

    pieces = split_call(places, mine, permute(other, core_hop))
    got = plane_share(pieces)
    do = after(do, pieces)
    stays, side, corner, up, mine2, other2 = backward_call(
        n2, places, xw, qkv, probs, dy, do, qkv_weight, g1, b1, out_side, out_corner
    )
    got, out_up = after((got, out_up), mine2)
    piece = sum_call(got)
    mine2, other2, up, out_up = after((mine2, other2, up, out_up), piece)

    pieces2 = split_call(places, mine2, permute(other2, core_hop))
    piece2 = sum_call(plane_share(pieces2))
    up, side, corner = after((up, side, corner), piece2)
    piece = join_call([piece, piece2])
    up, side, corner = permute(up, to_below), permute(side, to_right), permute(corner, across)
    piece = depth_sum(piece)
    piece, up, side, corner = after((piece, up, side, corner), up)
    mine = join_call(plane_share([piece] * planes))
    other = permute(mine, core_hop)
    top = jnp.concatenate([corner[: WIN - SHIFT], out_up], 1)
    bottom = jnp.concatenate([side[:SHIFT], out_stays], 1)
    output = jnp.concatenate([top, bottom], 0)
    mine, output = after((mine, output), output)
    total = float(tokens * rows * cols)
    (
        grad, fc1_g, fc2_g, proj_g, fc1_bg, g2_g, b2_g, fc2_bg, proj_bg, qkv_g, g1_g, b1_g, q_bg,
        v_bg, rel_g,
    ) = finish_call(
        total, planes, ff, n1, n2, rel_table.shape, places, mine, other, up, side, corner, stays
    )
    flat = lambda a: a.reshape(-1)
    return (
        output.transpose(2, 0, 1, 3),
        grad.transpose(2, 0, 1, 3),
        flat(g1_g),
        flat(b1_g),
        qkv_g,
        flat(q_bg),
        flat(v_bg),
        rel_g,
        proj_g,
        flat(proj_bg),
        flat(g2_g),
        flat(b2_g),
        fc1_g,
        flat(fc1_bg),
        fc2_g,
        flat(fc2_bg),
    )


def solution(mesh):
    field = P(None, "rows", "cols", None)
    return jax.shard_map(
        shards,
        mesh=mesh,
        in_specs=(field, field, P(None, "rows", "cols")) + (P(),) * 14,
        out_specs=(field, field) + (P(),) * 14,
        check_vma=False,
    )
```

```python
import math

import jax
import jax.numpy as jnp
from jax import lax
from jax.experimental import pallas as pl
from jax.experimental.pallas import tpu as pltpu
from jax.sharding import PartitionSpec as P

WIN = 10
SHIFT = 5
EPS = 1e-05
F32 = jnp.float32
BF16 = jnp.bfloat16

SPAN = 2 * WIN - 1
TOK = WIN * WIN
ROWS = 104
KEYS = 128
GROUP = 4
RELS = 384
NEVER = -1e30
PAGES = 8
BACK_AT_ONCE = 1
AT_ONCE = 4
VMEM_LIMIT = 20


def dot(a, b):
    return lax.dot_general(a, b, (((1,), (0,)), ((), ())), preferred_element_type=F32)


def dot_bt(a, b):
    return lax.dot_general(a, b, (((1,), (1,)), ((), ())), preferred_element_type=F32)


def dot_at(a, b):
    return lax.dot_general(a, b, (((0,), (0,)), ((), ())), preferred_element_type=F32)


def normalize(x):
    center = x - jnp.sum(x, -1, keepdims=True) * (1.0 / x.shape[-1])
    inv = lax.rsqrt(jnp.sum(center * center, -1, keepdims=True) * (1.0 / x.shape[-1]) + EPS)
    return center * inv, inv


def norm_back(up, normed, inv):
    scale = 1.0 / up.shape[-1]
    mean_up = jnp.sum(up, -1, keepdims=True) * scale
    mean_un = jnp.sum(up * normed, -1, keepdims=True) * scale
    return inv * (up - mean_up - normed * mean_un)


def fold(x):
    return jnp.sum(x.reshape(x.shape[0] // 8, 8, x.shape[1]), 0)


def head_masks(rows, dtype):
    lane = lax.broadcasted_iota(jnp.int32, (rows, KEYS), 1)
    width = KEYS // GROUP
    return [
        ((lane >= k * width) & (lane < (k + 1) * width)).astype(F32).astype(dtype)
        for k in range(GROUP)
    ]


def head_rows(x, masks):
    return jnp.concatenate([x * m for m in masks], 0).astype(BF16)


def own_lanes(stacked):
    lane = lax.broadcasted_iota(jnp.int32, (ROWS, KEYS), 1)
    out = stacked[(GROUP - 1) * ROWS :]
    for h in reversed(range(GROUP - 1)):
        out = jnp.where(lane < (h + 1) * (KEYS // GROUP), stacked[h * ROWS : (h + 1) * ROWS], out)
    return out


def split_rows(x):
    high = x.astype(BF16)
    return high, (x - high.astype(F32)).astype(BF16)


def page_rows(page, count):
    return pl.ds(page, count, stride=PAGES)


def load_rows(ref, w, rows):
    return jnp.concatenate([ref[t, w, rows, :] for t in range(ref.shape[0])], 1)


def store_rows(ref, w, rows, value):
    for t in range(ref.shape[0]):
        ref[t, w, rows, :] = value[:, t * KEYS : (t + 1) * KEYS]


def only_tokens(x):
    return jnp.where(lax.broadcasted_iota(jnp.int32, x.shape, 0) < TOK, x, 0.0)


def gather_frame(out, own, low, right, corner):
    for w in range(2):
        for r in range(WIN):
            if r < WIN - SHIFT:
                main, side, mr, sr = own, right, r + SHIFT, r
            else:
                main, side, mr, sr = low, corner, r - SHIFT, r - SHIFT
            if w == 0:
                block = main[mr, SHIFT : SHIFT + WIN].astype(F32)
            else:
                block = jnp.concatenate(
                    [main[mr, SHIFT + WIN :].astype(F32), side[sr].astype(F32)], 0
                )
            at = r * WIN * PAGES
            store_rows(
                out, w, slice(at, at + WIN * PAGES), block.reshape(WIN * PAGES, block.shape[-1])
            )


def tenth(n):
    return (n * 205) >> 11


def squeeze_matrix():
    at = lax.broadcasted_iota(jnp.int32, (RELS, 2 * KEYS), 0)
    to = lax.broadcasted_iota(jnp.int32, (RELS, 2 * KEYS), 1)
    hit = (at == to + (SPAN - WIN) * tenth(to)) & (to < SPAN * WIN)
    return hit.astype(F32).astype(BF16)


def copy_all(pairs, sems):
    copies = [pltpu.make_async_copy(a, b, sems.at[k]) for k, (a, b) in enumerate(pairs)]
    for copy in copies:
        copy.start()
    for copy in copies:
        copy.wait()


def strips_kernel(field, low, right, corner, sems):
    copy_all(
        (
            (field.at[:SHIFT], low), (field.at[SHIFT:, :SHIFT], right),
            (field.at[:SHIFT, :SHIFT], corner),
        ),
        sems,
    )


def target_kernel(
    target_in, kept_in, table_in, masked, low, right, corner, count, table, target, kept, sems
):
    copy_all(((target_in, target), (kept_in, kept), (table_in, table)), sems)
    rows, cols = target.shape[:2]
    total = jnp.zeros(kept.shape[1:], F32)
    for r in range(rows):
        kept_row = kept[r].astype(F32)
        total = total + kept_row
        for c in range(cols):
            masked[r, c] = (target[r, c].astype(F32) * kept_row[:, c : c + 1]).astype(BF16)
    low[...] = masked[:SHIFT]
    right[...] = masked[SHIFT:, :SHIFT]
    corner[...] = masked[:SHIFT, :SHIFT]
    total = jnp.sum(jnp.sum(total, 1, keepdims=True), 0, keepdims=True)
    count[...] = jnp.broadcast_to(total, count.shape)


def core_and_spot():
    r, c = lax.axis_index("rows"), lax.axis_index("cols")
    return r & 1, ((r >> 1) & 1) * lax.axis_size("cols") + c


def split_halves(sums, mine, other):
    size = mine.shape[0]
    core, _ = core_and_spot()
    mine[...] = sums[pl.ds(pl.multiple_of(core * size, 16), size), :]
    other[...] = sums[pl.ds(pl.multiple_of((1 - core) * size, 16), size), :]


def split_kernel(mine, other, *outs):
    size = outs[0].shape[0]
    _, spot = core_and_spot()
    for k, out in enumerate(outs):
        at = pl.ds(pl.multiple_of((spot ^ k) * size, 16), size)
        out[...] = (mine[at, :].astype(F32) + other[at, :].astype(F32)).astype(BF16)


def tree_sum(parts):
    while len(parts) > 1:
        parts = [parts[i] + parts[i + 1] for i in range(0, len(parts), 2)]
    return parts[0]


def sum_kernel(*refs):
    refs[-1][...] = tree_sum([ref[...].astype(F32) for ref in refs[:-1]]).astype(BF16)


def join_kernel(*refs):
    out, at = refs[-1], 0
    for ref in refs[:-1]:
        out[at : at + ref.shape[0]] = ref[...]
        at += ref.shape[0]


def split_three(x):
    high = x.astype(BF16)
    rest = x - high.astype(F32)
    middle = rest.astype(BF16)
    return high, middle, (rest - middle.astype(F32)).astype(BF16)


def bias_kernel(table, out, padded):
    heads = table.shape[0]
    last_row = lax.axis_index("rows") == lax.axis_size("rows") - 1
    last_col = lax.axis_index("cols") == lax.axis_size("cols") - 1
    padded[...] = jnp.zeros_like(padded)
    padded[:, : table.shape[1]] = table[...]
    offsets = padded[...]
    moved = []
    for c in range(WIN):
        shift = WIN - 1 - c
        moved.append(pltpu.roll(offsets, RELS - shift, 1) if shift else offsets)
    stack = jnp.concatenate(moved, 0)
    high, middle, least = split_three(stack)
    squeeze = squeeze_matrix()
    wide = dot(high, squeeze) + dot(middle, squeeze) + dot(least, squeeze)
    count = WIN * heads
    for r in range(WIN):
        shift = (WIN - 1 - r) * WIN
        rel = pltpu.roll(wide, 2 * KEYS - shift, 1) if shift else wide
        rel = rel[:, :KEYS]
        query = lax.broadcasted_iota(jnp.int32, (count, KEYS), 1)
        row = lax.broadcasted_iota(jnp.int32, (count, KEYS), 0)
        across = (query < TOK // 2) if r >= SHIFT else (query >= TOK // 2)
        query_left = query - WIN * tenth(query) < SHIFT
        own_left = row < SHIFT * heads
        beside = query_left != own_left
        for w in range(2):
            cut_off = across & last_row
            if w == 1:
                cut_off = cut_off | (beside & last_col)
            value = rel + jnp.where(cut_off, -100.0, 0.0)
            out[w, r * count : (r + 1) * count, :] = value
    for w in range(2):
        out[w, TOK * heads :, :] = jnp.full((out.shape[1] - TOK * heads, KEYS), NEVER, F32)


def attention_kernel(
    own, low, right, corner, qkv_w, bias, g1, b1, qb, vb,
    x_out, xw_out, qkv_out, p_out, o_out,
    xf,
):
    gather_frame(xf, own, low, right, corner)
    for t in range(xf.shape[0]):
        for w in range(2):
            xf[t, w, TOK * PAGES :, :] = jnp.zeros((xf.shape[2] - TOK * PAGES, KEYS), F32)
            x_out[w * TOK * PAGES : (w + 1) * TOK * PAGES, t * KEYS : (t + 1) * KEYS] = xf[
                t, w, : TOK * PAGES, :
            ].astype(BF16)

    d = g1.shape[-1]
    heads = d // (KEYS // GROUP)
    scale = (d // heads) ** (-0.5)
    windows = [(page, w) for page in range(PAGES) for w in range(2)]
    x = jnp.concatenate(
        [only_tokens(load_rows(xf, w, page_rows(page, ROWS))) for page, w in windows], 0
    )
    xw_out[...] = x.astype(BF16)
    normed, _ = normalize(x)
    attn_in = (normed * g1[...] + b1[...]).astype(BF16)
    proj = dot(attn_in, qkv_w[...])
    q_all = proj[:, :d] + qb[...]
    k_all = proj[:, d : 2 * d]
    v_all = proj[:, 2 * d :] + vb[...]
    masks = head_masks(ROWS, F32)
    filler = jnp.zeros((KEYS - ROWS, d), F32)
    groups = heads // GROUP
    for start in range(0, len(windows), AT_ONCE):
        scores, values = [], []
        some = windows[start : start + AT_ONCE]
        for n, (page, w) in enumerate(some):
            rows = slice((start + n) * ROWS, (start + n + 1) * ROWS)
            q = jnp.concatenate([q_all[rows], filler], 0).astype(BF16)
            k = jnp.concatenate([k_all[rows], filler], 0).astype(BF16)
            v = jnp.concatenate([v_all[rows], filler], 0).astype(BF16)
            qkv_out[w, page, :, :d] = q
            qkv_out[w, page, :, d : 2 * d] = k
            qkv_out[w, page, :, 2 * d :] = v
            for g in range(groups):
                lanes = slice(g * KEYS, (g + 1) * KEYS)
                scores.append(dot_bt(head_rows(k_all[rows, lanes], masks), q[:, lanes]))
                values.append(head_rows(v_all[rows, lanes], masks))
        probs = []
        for n, s in enumerate(scores):
            page, w = some[n // groups]
            g = n % groups
            es = []
            for h in range(GROUP):
                rel = bias[w, pl.ds(g * GROUP + h, ROWS, stride=heads), :]
                sh = s[h * ROWS : (h + 1) * ROWS] * scale + rel
                e = jnp.exp(sh - jnp.max(sh, 0, keepdims=True))
                es.append(e * (1.0 / jnp.sum(e, 0, keepdims=True)))
            p = jnp.concatenate(es, 0).astype(BF16)
            p_out[w, page, g * GROUP * ROWS : (g + 1) * GROUP * ROWS, :] = p
            probs.append(p)
        parts = [dot_at(p, v)[:ROWS] for p, v in zip(probs, values)]
        for n, (page, w) in enumerate(some):
            joined = jnp.concatenate(parts[n * groups : (n + 1) * groups], 1)
            store_rows(o_out, w, page_rows(page, TOK), joined[:TOK])


def mlp_kernel(
    x_in, o_in, t_own, t_low, t_right, t_corner, count,
    proj_w, fc1_w, fc2_w, pb, g2, b2, f1b, f2b,
    stays, up, side, corner, dy_out, do_out, rows_out, mine, other,
    frame_out, sums_out, tf, fc1_acc, fc2_acc, proj_acc, fc1_sum, small_sum,
):
    gather_frame(tf, t_own, t_low, t_right, t_corner)

    mlp_step(
        x_in, o_in, proj_w, fc1_w, fc2_w, pb, g2, b2, f1b, f2b, frame_out, dy_out, do_out,
        tf, fc1_acc, fc2_acc, proj_acc, fc1_sum, small_sum,
    )

    d = proj_w.shape[0]
    ff = fc1_w.shape[1] // d
    for j in range(ff):
        sums_out[j * d : (j + 1) * d, :] = fc1_acc[:, j * d : (j + 1) * d].astype(BF16)
        sums_out[(ff + j) * d : (ff + j + 1) * d, :] = fc2_acc[j * d : (j + 1) * d, :].astype(BF16)
    at = 2 * ff * d
    sums_out[at : at + d, :] = proj_acc[...].astype(BF16)
    rows = [jnp.sum(fc1_sum[:, j * d : (j + 1) * d], 0, keepdims=True) for j in range(ff)]
    rows += [jnp.sum(small_sum[k], 0, keepdims=True) for k in range(4)]
    rows.append(count[...])
    rows.append(jnp.zeros((16 - len(rows), d), F32))
    rows_out[...] = jnp.concatenate(rows, 0)
    at += d
    if sums_out.shape[0] > at:
        sums_out[at:, :] = jnp.zeros((sums_out.shape[0] - at, d), BF16)
    split_halves(sums_out, mine, other)
    stays[...] = frame_out[:SHIFT, :-SHIFT]
    up[...] = frame_out[SHIFT:, :-SHIFT]
    side[...] = frame_out[:SHIFT, -SHIFT:]
    corner[...] = frame_out[SHIFT:, -SHIFT:]


def both_windows(ref):
    return jnp.concatenate([load_rows(ref, w, slice(0, TOK * PAGES)) for w in range(2)], 0)


def mlp_step(
    x_in, o_in, proj_w, fc1_w, fc2_w, pb, g2, b2, f1b, f2b, frame_out, dy_out, do_out,
    tf, fc1_acc, fc2_acc, proj_acc, fc1_sum, small_sum,
):
    d = x_in.shape[1]
    ff = fc1_w.shape[1] // d
    tokens = TOK * PAGES
    o = both_windows(o_in).astype(BF16)
    y = x_in[...].astype(F32) + dot(o, proj_w[...]) + pb[...]
    normed2, inv2 = normalize(y)
    c = (normed2 * g2[...] + b2[...]).astype(BF16)
    dr = both_windows(tf)
    drb = dr.astype(BF16)
    r = y + f2b[...]
    dc = None
    for j in range(ff):
        at = slice(j * d, (j + 1) * d)
        h = dot(c, fc1_w[:, at]) + f1b[:, at]
        phi = 0.5 * (1.0 + lax.erf(h * math.sqrt(0.5)))
        slope = phi + h * (jnp.exp(h * h * -0.5) * (1.0 / math.sqrt(2.0 * math.pi)))
        gelu = (h * phi).astype(BF16)
        dh_wide = dot_bt(drb, fc2_w[at, :]) * slope
        dh = dh_wide.astype(BF16)
        r = r + dot(gelu, fc2_w[at, :])
        fc2_acc[at, :] = dot_at(gelu, drb)
        fc1_acc[:, at] = dot_at(c, dh)
        fc1_sum[:, at] = fold(dh.astype(F32))
        more = dot_bt(dh, fc1_w[:, at])
        dc = more if dc is None else dc + more
    for w in range(2):
        frame_out[:, w * WIN : (w + 1) * WIN] = (
            r[w * tokens : (w + 1) * tokens].reshape(WIN, WIN, PAGES, d).astype(BF16)
        )
    dy = dr + norm_back(dc * g2[...], normed2, inv2)
    dz = dy.astype(BF16)
    proj_acc[...] = dot_at(o, dz)
    do = dot_bt(dz, proj_w[...])
    for w in range(2):
        rows = slice(w * tokens, (w + 1) * tokens)
        store_rows(do_out, w, slice(0, tokens), do[rows])
        store_rows(dy_out, w, slice(0, tokens), dy[rows])
    small_sum[0] = fold(dc * normed2)
    small_sum[1] = fold(dc)
    small_sum[2] = fold(dr)
    small_sum[3] = fold(dz.astype(F32))


def backward_kernel(
    xw, qkv, p_in, dy_in, do_in, qkv_w, g1, b1, out_side, mlp_rows,
    stays, side, corner, up, mine, other,
    dx, qkv_acc, rel_acc, col_sum, small_sum, mixed, sums_out, joined_all,
):
    rel_acc[...] = jnp.zeros_like(rel_acc)
    for page in range(0, PAGES, BACK_AT_ONCE):
        backward_pages(range(page, page + BACK_AT_ONCE), qkv, p_in, do_in, joined_all, rel_acc)

    d = g1.shape[-1]
    heads = d // (KEYS // GROUP)
    joined = joined_all[...]
    normed, inv = normalize(xw[...].astype(F32))
    attn_in = (normed * g1[...] + b1[...]).astype(BF16)
    qkv_acc[...] = dot_at(attn_in, joined)
    col_sum[...] = fold(joined.astype(F32))
    da = dot_bt(joined, qkv_w[...])
    small_sum[0] = fold(da * normed)
    small_sum[1] = fold(da)
    back = norm_back(da * g1[...], normed, inv)
    for page in range(PAGES):
        rows = page_rows(page, TOK)
        for w in range(2):
            at = (2 * page + w) * ROWS
            store_rows(dx, w, rows, load_rows(dy_in, w, rows) + back[at : at + TOK])
    right = load_rows(dx, 1, slice(None)).reshape(WIN, WIN, PAGES, d)
    left = load_rows(dx, 0, slice(None)).reshape(WIN, WIN, PAGES, d)
    stays[:, :WIN] = left[:SHIFT]
    stays[:, WIN:] = right[:SHIFT, :SHIFT]
    side[:SHIFT] = out_side[...]
    side[SHIFT:] = right[:SHIFT, SHIFT:].astype(BF16)
    corner[...] = right[SHIFT:, SHIFT:].astype(BF16)
    up[:, :WIN] = left[SHIFT:].astype(BF16)
    up[:, WIN:] = right[SHIFT:, :SHIFT].astype(BF16)
    for j in range(3):
        sums_out[j * d : (j + 1) * d, :] = qkv_acc[:, j * d : (j + 1) * d].astype(BF16)
    rel = table_gradient(
        [rel_acc[:, h * KEYS : (h + 1) * KEYS] for h in range(heads)], mixed
    )
    rows = [jnp.sum(small_sum[k], 0, keepdims=True) for k in range(2)]
    rows.append(jnp.sum(col_sum[:, :d], 0, keepdims=True))
    rows.append(jnp.sum(col_sum[:, 2 * d :], 0, keepdims=True))
    rows.append(mlp_rows[:12])
    rows.append(rel[:, :d])
    rows.append(jnp.concatenate([rel[:, d:], jnp.zeros((heads, 2 * d - RELS), F32)], 1))
    high, rest = split_rows(jnp.concatenate(rows, 0))
    at = 3 * d
    sums_out[at : at + 32, :] = high
    sums_out[at + 32 : at + 64, :] = rest
    if sums_out.shape[0] > at + 64:
        sums_out[at + 64 :, :] = jnp.zeros((sums_out.shape[0] - at - 64, d), BF16)
    split_halves(sums_out, mine, other)


def backward_pages(pages, qkv, p_in, do_in, joined_all, rel_acc):
    d = qkv.shape[-1] // 3
    heads = d // (KEYS // GROUP)
    groups = heads // GROUP
    scale = (d // heads) ** (-0.5)
    masks = head_masks(ROWS, F32)
    chains = [(page, w, g) for page in pages for w in range(2) for g in range(groups)]
    queries, keys, dos, dps = [], [], [], []
    filler = jnp.zeros((KEYS - ROWS, KEYS), F32)
    for page, w, g in chains:
        lanes = slice(g * KEYS, (g + 1) * KEYS)
        queries.append(qkv[w, page, :, lanes])
        k = qkv[w, page, :, d + g * KEYS : d + (g + 1) * KEYS]
        v = qkv[w, page, :, 2 * d + g * KEYS : 2 * d + (g + 1) * KEYS]
        keys.append(head_rows(k.astype(F32)[:ROWS], masks))
        do = only_tokens(do_in[g, w, page_rows(page, ROWS), :])
        dos.append(jnp.concatenate([do, filler], 0).astype(BF16))
        dps.append(dot_bt(head_rows(v.astype(F32)[:ROWS], masks), dos[-1]))
    dts = []
    rel_sum = [None] * heads
    for c, (page, w, g) in enumerate(chains):
        p = p_in[w, page, g * GROUP * ROWS : (g + 1) * GROUP * ROWS, :].astype(F32)
        t = p * dps[c]
        ds = []
        for h in range(GROUP):
            at = slice(h * ROWS, (h + 1) * ROWS)
            part = t[at] - p[at] * jnp.sum(t[at], 0, keepdims=True)
            head = g * GROUP + h
            rel_sum[head] = part if rel_sum[head] is None else rel_sum[head] + part
            ds.append(part * scale)
        dts.append(jnp.concatenate(ds, 0).astype(BF16))
    for h in range(heads):
        rel_acc[:, h * KEYS : (h + 1) * KEYS] += rel_sum[h]
    parts = {}
    for c, (page, w, g) in enumerate(chains):
        p = p_in[w, page, g * GROUP * ROWS : (g + 1) * GROUP * ROWS, :]
        parts[0, page, w, g] = dot_at(dts[c], keys[c])[:ROWS]
        parts[1, page, w, g] = own_lanes(dot(dts[c], queries[c]))
        parts[2, page, w, g] = own_lanes(dot(p, dos[c]))
    for page in pages:
        for k in range(3):
            for g in range(groups):
                joined = jnp.concatenate([parts[k, page, w, g] for w in range(2)], 0)
                at = k * d + g * KEYS
                joined_all[2 * page * ROWS : 2 * (page + 1) * ROWS, at : at + KEYS] = joined.astype(
                    BF16
                )


def table_gradient(by_head, mixed):
    heads = len(by_head)
    for h in range(heads):
        mixed[pl.ds(h, ROWS, stride=heads), :] = by_head[h]
    wide = None
    for r in range(WIN):
        part = mixed[r * WIN * heads : (r + 1) * WIN * heads, :]
        part = jnp.concatenate([part, jnp.zeros_like(part)], 1)
        shift = (WIN - 1 - r) * WIN
        part = pltpu.roll(part, shift, 1) if shift else part
        wide = part if wide is None else wide + part
    high, rest = split_rows(wide)
    squeeze = squeeze_matrix()
    moved = dot_bt(high, squeeze) + dot_bt(rest, squeeze)
    total = None
    for c in range(WIN):
        part = moved[c * heads : (c + 1) * heads]
        shift = WIN - 1 - c
        part = pltpu.roll(part, shift, 1) if shift else part
        total = part if total is None else total + part
    return total


def collect(buf, mine, other, planes, first, size):
    core, spot = core_and_spot()
    stride = mine.shape[0] // planes
    for c, pieces in ((core, mine), (1 - core, other)):
        for k in range(planes):
            at = pl.multiple_of((c * planes + (spot ^ k)) * size, 16)
            buf[pl.ds(at, size), :] = pieces[k * stride + first : k * stride + first + size, :].astype(
                F32
            )


def finish_kernel(
    total, planes, sizes, mine, other, up, side, corner, stays,
    grad, fc1, fc2, proj, fc1_b, g2, b2, fc2_b, proj_b, qkv, g1, b1, q_b, v_b, rel, buf1, buf2,
):
    collect(buf1, mine, other, planes, 0, sizes[0])
    collect(buf2, mine, other, planes, sizes[0], sizes[1])
    d = proj.shape[0]
    ff = fc1.shape[1] // d
    at = 3 * d
    rows = buf2[at : at + 32, :] + buf2[at + 32 : at + 64, :]
    scale = total / rows[ff + 8 : ff + 9, :]
    rows = rows * scale
    wide = scale.reshape(1, 1, 1, d)
    rest = up.shape[0]
    grad[:rest, :SHIFT] = corner[...].astype(F32) * wide
    grad[:rest, SHIFT:] = up[...].astype(F32) * wide
    grad[rest:, :SHIFT] = side[SHIFT:].astype(F32) * wide
    grad[rest:, SHIFT:] = stays[...] * wide
    for j in range(ff):
        fc1[:, j * d : (j + 1) * d] = buf1[j * d : (j + 1) * d, :] * scale
        fc2[j * d : (j + 1) * d, :] = buf1[(ff + j) * d : (ff + j + 1) * d, :] * scale
        fc1_b[:, j * d : (j + 1) * d] = rows[4 + j : 5 + j]
    proj[...] = buf1[2 * ff * d : (2 * ff + 1) * d, :] * scale
    for k, ref in enumerate((g2, b2, fc2_b, proj_b)):
        ref[...] = rows[ff + 4 + k : ff + 5 + k]
    for j in range(3):
        qkv[:, j * d : (j + 1) * d] = buf2[j * d : (j + 1) * d, :] * scale
    for k, ref in enumerate((g1, b1, q_b, v_b)):
        ref[...] = rows[k : k + 1]
    heads = rel.shape[0]
    rel[:, :d] = rows[16 : 16 + heads]
    rel[:, d:] = rows[16 + heads : 16 + 2 * heads, : rel.shape[1] - d]


def permute(block, target):
    rows, cols = lax.axis_size("rows"), lax.axis_size("cols")
    route = []
    for r in range(rows):
        for c in range(cols):
            tr, tc = target(r, c)
            route.append((r * cols + c, (tr % rows) * cols + tc % cols))
    return lax.ppermute(block, ("rows", "cols"), route)


def after(values, done):
    return lax.optimization_barrier((values, done))[0]


def core_hop(r, c):
    return r ^ 1, c


def plane_hop(k):
    cols = lax.axis_size("cols")
    return lambda r, c: (r ^ (2 * (k // cols)), c ^ (k % cols))


def plane_share(pieces):
    return [pieces[0]] + [permute(p, plane_hop(k)) for k, p in enumerate(pieces) if k]


def depth_sum(piece):
    hop = 4
    while hop < lax.axis_size("rows"):
        piece = sum_call([piece, permute(piece, lambda r, c, hop=hop: (r ^ hop, c))])
        hop *= 2
    return piece


def strip_hops():
    return [lambda r, c: (r - 1, c), lambda r, c: (r, c - 1), lambda r, c: (r - 1, c - 1)]


def in_vmem():
    return pl.BlockSpec(memory_space=pltpu.VMEM)


def to_vmem(a):
    return pltpu.with_memory_space_constraint(a, pltpu.VMEM)


def limit(mib):
    return pltpu.CompilerParams(vmem_limit_bytes=mib * 1024 * 1024)


def strip_shapes(field):
    rows, cols, pages, d = field.shape
    return [
        pltpu.VMEM(s, BF16)
        for s in (
            (SHIFT, cols, pages, d), (rows - SHIFT, SHIFT, pages, d), (SHIFT, SHIFT, pages, d)
        )
    ]


def in_hbm():
    return pl.BlockSpec(memory_space=pltpu.HBM)


def to_hbm(a):
    return pltpu.with_memory_space_constraint(a, pltpu.HBM)


def strips_call(field):
    return pl.pallas_call(
        strips_kernel,
        in_specs=[in_hbm()],
        out_specs=[in_vmem()] * 3,
        out_shape=strip_shapes(field),
        scratch_shapes=[pltpu.SemaphoreType.DMA((3,))],
        compiler_params=limit(4),
        name="input_strips",
    )(to_hbm(field))


def target_call(target, kept, table):
    return pl.pallas_call(
        target_kernel,
        in_specs=[in_hbm()] * 3,
        out_specs=[in_vmem()] * 6,
        out_shape=[
            pltpu.VMEM(target.shape, BF16), *strip_shapes(target),
            pltpu.VMEM((1, target.shape[-1]), F32), pltpu.VMEM(table.shape, F32),
        ],
        scratch_shapes=[
            pltpu.VMEM(target.shape, BF16), pltpu.VMEM(kept.shape, kept.dtype),
            pltpu.SemaphoreType.DMA((3,)),
        ],
        compiler_params=limit(8),
        name="masked_target",
    )(*map(to_hbm, (target, kept, table)))


def split_call(mine, other):
    planes = 2 * lax.axis_size("cols")
    n, d = mine.shape
    return pl.pallas_call(
        split_kernel,
        in_specs=[in_vmem()] * 2,
        out_specs=[in_vmem()] * planes,
        out_shape=[pltpu.VMEM((n // planes, d), BF16)] * planes,
        compiler_params=limit(4),
        name="split_sums",
    )(*map(to_vmem, (mine, other)))


def local_call(kernel, rows, parts, name):
    return pl.pallas_call(
        kernel,
        in_specs=[in_vmem()] * len(parts),
        out_specs=in_vmem(),
        out_shape=pltpu.VMEM((rows,) + parts[-1].shape[1:], BF16),
        compiler_params=limit(4),
        name=name,
    )(*map(to_vmem, parts))


def sum_call(parts):
    return local_call(sum_kernel, parts[0].shape[0], parts, "add_pieces")


def join_call(parts):
    return local_call(join_kernel, sum(a.shape[0] for a in parts), parts, "join_pieces")


def bias_call(rel_table):
    heads = rel_table.shape[0]
    return pl.pallas_call(
        bias_kernel,
        in_specs=[in_vmem()],
        out_specs=in_vmem(),
        out_shape=pltpu.VMEM((2, ROWS * heads, KEYS), F32),
        scratch_shapes=[pltpu.VMEM((heads, RELS), F32)],
        compiler_params=limit(VMEM_LIMIT),
        name="attention_bias",
    )(to_vmem(rel_table))


def cost(flops):
    return pl.CostEstimate(flops=flops, bytes_accessed=10**7, transcendentals=10**6)


def attention_call(patches, p_strips, qkv_w, bias, g1, b1, q_b, v_b):
    pages, d = patches.shape[2:]
    heads = bias.shape[1] // ROWS
    tokens = 2 * TOK * pages
    shape = pltpu.VMEM
    inputs = [patches, *p_strips, qkv_w, bias, g1, b1, q_b, v_b]
    outs = [
        shape((tokens, d), BF16),
        shape((2 * pages * ROWS, d), BF16),
        shape((2, pages, KEYS, 3 * d), BF16),
        shape((2, pages, heads * ROWS, KEYS), BF16),
        shape((d // KEYS, 2, TOK * pages, KEYS), F32),
    ]
    return pl.pallas_call(
        attention_kernel,
        in_specs=[in_vmem()] * len(inputs),
        out_specs=[in_vmem()] * len(outs),
        out_shape=outs,
        scratch_shapes=[pltpu.VMEM((d // KEYS, 2, ROWS * pages, KEYS), F32)],
        compiler_params=limit(VMEM_LIMIT),
        cost_estimate=cost(10**10),
        name="attention_forward",
    )(*map(to_vmem, inputs))


def mlp_call(size, x, mixed, masked, t_strips, count, *weights):
    height, width, pages, d = masked.shape
    ff = weights[1].shape[1]
    shape = pltpu.VMEM
    inputs = [x, mixed, masked, *t_strips, count, *weights]
    rest = WIN - SHIFT
    outs = [
        shape((SHIFT, width - SHIFT, pages, d), BF16), shape((rest, width - SHIFT, pages, d), BF16),
        shape((SHIFT, SHIFT, pages, d), BF16), shape((rest, SHIFT, pages, d), BF16),
        shape((d // KEYS, 2, ROWS * pages, KEYS), F32),
        shape((d // KEYS, 2, ROWS * pages, KEYS), F32),
        shape((16, d), F32), shape((size // 2, d), BF16), shape((size // 2, d), BF16),
    ]
    return pl.pallas_call(
        mlp_kernel,
        in_specs=[in_vmem()] * len(inputs),
        out_specs=[in_vmem()] * len(outs),
        out_shape=outs,
        scratch_shapes=[
            pltpu.VMEM((height, width, pages, d), BF16),
            pltpu.VMEM((size, d), BF16),
            pltpu.VMEM((d // KEYS, 2, TOK * pages, KEYS), F32),
            pltpu.VMEM((d, ff), F32),
            pltpu.VMEM((ff, d), F32),
            pltpu.VMEM((d, d), F32),
            pltpu.VMEM((8, ff), F32),
            pltpu.VMEM((4, 8, d), F32),
        ],
        compiler_params=limit(VMEM_LIMIT),
        cost_estimate=cost(10**10),
        name="mlp_forward_backward",
    )(*map(to_vmem, inputs))


def backward_call(size, xw, qkv, probs, dy, do, *more):
    pages, d = probs.shape[1], xw.shape[1]
    heads = probs.shape[2] // ROWS
    shape = pltpu.VMEM
    inputs = [xw, qkv, probs, dy, do, *more]
    rest = WIN - SHIFT
    outs = [
        shape((SHIFT, 2 * WIN - SHIFT, pages, d), F32), shape((2 * SHIFT, SHIFT, pages, d), BF16),
        shape((rest, SHIFT, pages, d), BF16),
        shape((rest, 2 * WIN - SHIFT, pages, d), BF16), shape((size // 2, d), BF16),
        shape((size // 2, d), BF16),
    ]
    return pl.pallas_call(
        backward_kernel,
        in_specs=[in_vmem()] * len(inputs),
        out_specs=[in_vmem()] * len(outs),
        out_shape=outs,
        scratch_shapes=[
            shape((d // KEYS, 2, TOK * pages, KEYS), F32),
            shape((d, 3 * d), F32),
            shape((ROWS, heads * KEYS), F32),
            shape((8, 3 * d), F32),
            shape((2, 8, d), F32),
            shape((ROWS * heads, KEYS), F32),
            shape((size, d), BF16),
            shape((2 * pages * ROWS, 3 * d), BF16),
        ],
        compiler_params=limit(VMEM_LIMIT),
        cost_estimate=cost(10**10),
        name="attention_backward",
    )(*map(to_vmem, inputs))


def finish_call(total, planes, ff, n1, n2, rel_shape, *inputs):
    d = inputs[0].shape[1]
    row = (1, d)
    field = (WIN, 2 * WIN) + inputs[2].shape[2:]
    shapes = [field, (d, ff), (ff, d), (d, d), (1, ff), row, row, row, row, (d, 3 * d)]
    shapes += [row, row, row, row, rel_shape]
    sizes = (n1 // (2 * planes), n2 // (2 * planes))
    return pl.pallas_call(
        lambda *refs: finish_kernel(total, planes, sizes, *refs),
        in_specs=[in_vmem()] * len(inputs),
        out_shape=[jax.ShapeDtypeStruct(s, F32) for s in shapes],
        scratch_shapes=[pltpu.VMEM((n1, d), F32), pltpu.VMEM((n2, d), F32)],
        compiler_params=limit(VMEM_LIMIT),
        name="finish_sums",
    )(*map(to_vmem, inputs))


def shards(
    patches, target, kept_mask, ln1_gain, ln1_bias, qkv_weight, query_bias, value_bias, rel_table,
    proj_weight, proj_bias, ln2_gain, ln2_bias, fc1_weight, fc1_bias, fc2_weight, fc2_bias,
):
    pages, height, width, d = patches.shape
    ff = fc1_weight.shape[1]
    rows, cols = lax.axis_size("rows"), lax.axis_size("cols")
    planes = 2 * cols
    step = 32 * planes
    tokens = pages * height * width
    vec = lambda a: a.reshape(1, -1)
    n1 = -(-(2 * ff + d) // step) * step
    n2 = -(-(3 * d + 64) // step) * step

    patches = patches.transpose(1, 2, 0, 3)
    p_strips = [permute(a, hop) for a, hop in zip(strips_call(patches), strip_hops())]
    masked, *t_strips, count, table = target_call(
        target.transpose(1, 2, 0, 3), kept_mask.transpose(1, 0, 2), rel_table
    )
    t_strips = [permute(a, hop) for a, hop in zip(t_strips, strip_hops())]
    bias = bias_call(table)

    g1, b1 = vec(ln1_gain), vec(ln1_bias)
    x, xw, qkv, probs, mixed = attention_call(
        patches, p_strips, qkv_weight, bias, g1, b1, vec(query_bias), vec(value_bias)
    )
    out_stays, out_up, out_side, out_corner, dy, do, mlp_rows, mine, other = mlp_call(
        n1, x, mixed, masked, t_strips, count, proj_weight, fc1_weight, fc2_weight,
        vec(proj_bias), vec(ln2_gain), vec(ln2_bias), vec(fc1_bias), vec(fc2_bias),
    )

    to_right, to_below = (lambda r, c: (r, c + 1)), (lambda r, c: (r + 1, c))
    across = lambda r, c: (r + 1, c + 1)
    out_up, out_corner = permute(out_up, to_below), permute(out_corner, across)

    pieces = split_call(mine, permute(other, core_hop))
    got = plane_share(pieces)
    do = after(do, pieces)
    stays, side, corner, up, mine2, other2 = backward_call(
        n2, xw, qkv, probs, dy, do, qkv_weight, g1, b1, out_side, mlp_rows
    )
    got, out_up, out_corner = after((got, out_up, out_corner), mine2)
    piece = sum_call(got)
    mine2, other2, up, out_up, out_corner = after(
        (mine2, other2, up, out_up, out_corner), piece
    )

    pieces2 = split_call(mine2, permute(other2, core_hop))
    piece2 = sum_call(plane_share(pieces2))
    up, side, corner = after((up, side, corner), piece2)
    piece = join_call([piece, piece2])
    up, side, corner = permute(up, to_below), permute(side, to_right), permute(corner, across)
    piece = depth_sum(piece)
    piece, up, side, corner = after((piece, up, side, corner), up)
    mine = join_call(plane_share([piece] * planes))
    other = permute(mine, core_hop)
    top = jnp.concatenate([out_corner, out_up], 1)
    bottom = jnp.concatenate([side[:SHIFT], out_stays], 1)
    output = jnp.concatenate([top, bottom], 0)
    mine, output = after((mine, output), output)
    total = float(tokens * rows * cols)
    (
        grad, fc1_g, fc2_g, proj_g, fc1_bg, g2_g, b2_g, fc2_bg, proj_bg, qkv_g, g1_g, b1_g, q_bg,
        v_bg, rel_g,
    ) = finish_call(
        total, planes, ff, n1, n2, rel_table.shape, mine, other, up, side, corner, stays
    )
    flat = lambda a: a.reshape(-1)
    return (
        output.transpose(2, 0, 1, 3),
        grad.transpose(2, 0, 1, 3),
        flat(g1_g),
        flat(b1_g),
        qkv_g,
        flat(q_bg),
        flat(v_bg),
        rel_g,
        proj_g,
        flat(proj_bg),
        flat(g2_g),
        flat(b2_g),
        fc1_g,
        flat(fc1_bg),
        fc2_g,
        flat(fc2_bg),
    )


def solution(mesh):
    field = P(None, "rows", "cols", None)
    return jax.shard_map(
        shards,
        mesh=mesh,
        in_specs=(field, field, P(None, "rows", "cols")) + (P(),) * 14,
        out_specs=(field, field) + (P(),) * 14,
        check_vma=False,
    )
```

```python
import math

import jax
import jax.numpy as jnp
from jax import lax
from jax.experimental import pallas as pl
from jax.experimental.pallas import tpu as pltpu
from jax.sharding import PartitionSpec as P

WIN = 10
SHIFT = 5
EPS = 1e-05
F32 = jnp.float32
BF16 = jnp.bfloat16

SPAN = 2 * WIN - 1
TOK = WIN * WIN
ROWS = 104
KEYS = 128
GROUP = 4
RELS = 384
NEVER = -1e30
PAGES = 8
VECTORS = 32
BACK_AT_ONCE = 1
AT_ONCE = 4
VMEM_LIMIT = 20


def dot(a, b):
    return lax.dot_general(a, b, (((1,), (0,)), ((), ())), preferred_element_type=F32)


def dot_bt(a, b):
    return lax.dot_general(a, b, (((1,), (1,)), ((), ())), preferred_element_type=F32)


def dot_at(a, b):
    return lax.dot_general(a, b, (((0,), (0,)), ((), ())), preferred_element_type=F32)


def normalize(x):
    center = x - jnp.sum(x, -1, keepdims=True) * (1.0 / x.shape[-1])
    inv = lax.rsqrt(jnp.sum(center * center, -1, keepdims=True) * (1.0 / x.shape[-1]) + EPS)
    return center * inv, inv


def norm_back(up, normed, inv):
    scale = 1.0 / up.shape[-1]
    mean_up = jnp.sum(up, -1, keepdims=True) * scale
    mean_un = jnp.sum(up * normed, -1, keepdims=True) * scale
    return inv * (up - mean_up - normed * mean_un)


def fold(x):
    return jnp.sum(x.reshape(x.shape[0] // 8, 8, x.shape[1]), 0)


def head_masks(rows, dtype):
    lane = lax.broadcasted_iota(jnp.int32, (rows, KEYS), 1)
    width = KEYS // GROUP
    return [
        ((lane >= k * width) & (lane < (k + 1) * width)).astype(F32).astype(dtype)
        for k in range(GROUP)
    ]


def head_rows(x, masks):
    return jnp.concatenate([x * m for m in masks], 0).astype(BF16)


def own_lanes(stacked):
    lane = lax.broadcasted_iota(jnp.int32, (ROWS, KEYS), 1)
    out = stacked[(GROUP - 1) * ROWS :]
    for h in reversed(range(GROUP - 1)):
        out = jnp.where(lane < (h + 1) * (KEYS // GROUP), stacked[h * ROWS : (h + 1) * ROWS], out)
    return out


def split_rows(x):
    high = x.astype(BF16)
    return high, (x - high.astype(F32)).astype(BF16)


def page_rows(page, count):
    return pl.ds(page, count, stride=PAGES)


def load_rows(ref, w, rows):
    return jnp.concatenate([ref[t, w, rows, :] for t in range(ref.shape[0])], 1)


def store_rows(ref, w, rows, value):
    for t in range(ref.shape[0]):
        ref[t, w, rows, :] = value[:, t * KEYS : (t + 1) * KEYS]


def only_tokens(x):
    return jnp.where(lax.broadcasted_iota(jnp.int32, x.shape, 0) < TOK, x, 0.0)


def gather_frame(out, own, low, right, corner):
    for w in range(2):
        for r in range(WIN):
            if r < WIN - SHIFT:
                main, side, mr, sr = own, right, r + SHIFT, r
            else:
                main, side, mr, sr = low, corner, r - SHIFT, r - SHIFT
            if w == 0:
                block = main[mr, SHIFT : SHIFT + WIN].astype(F32)
            else:
                block = jnp.concatenate(
                    [main[mr, SHIFT + WIN :].astype(F32), side[sr].astype(F32)], 0
                )
            at = r * WIN * PAGES
            store_rows(
                out, w, slice(at, at + WIN * PAGES), block.reshape(WIN * PAGES, block.shape[-1])
            )


def tenth(n):
    return (n * 205) >> 11


def squeeze_matrix():
    at = lax.broadcasted_iota(jnp.int32, (RELS, 2 * KEYS), 0)
    to = lax.broadcasted_iota(jnp.int32, (RELS, 2 * KEYS), 1)
    hit = (at == to + (SPAN - WIN) * tenth(to)) & (to < SPAN * WIN)
    return hit.astype(F32).astype(BF16)


def copy_all(pairs, sems):
    copies = [pltpu.make_async_copy(a, b, sems.at[k]) for k, (a, b) in enumerate(pairs)]
    for copy in copies:
        copy.start()
    for copy in copies:
        copy.wait()


def strips_kernel(field, low, right, corner, sems):
    copy_all(
        (
            (field.at[:SHIFT], low), (field.at[SHIFT:, :SHIFT], right),
            (field.at[:SHIFT, :SHIFT], corner),
        ),
        sems,
    )


def target_kernel(
    target_in, kept_in, table_in, masked, low, right, corner, count, table, target, kept, sems
):
    copy_all(((target_in, target), (kept_in, kept), (table_in, table)), sems)
    rows, cols = target.shape[:2]
    total = jnp.zeros(kept.shape[1:], F32)
    for r in range(rows):
        kept_row = kept[r].astype(F32)
        total = total + kept_row
        for c in range(cols):
            masked[r, c] = (target[r, c].astype(F32) * kept_row[:, c : c + 1]).astype(BF16)
    low[...] = masked[:SHIFT]
    right[...] = masked[SHIFT:, :SHIFT]
    corner[...] = masked[:SHIFT, :SHIFT]
    total = jnp.sum(jnp.sum(total, 1, keepdims=True), 0, keepdims=True)
    count[...] = jnp.broadcast_to(total, count.shape)


def core_and_spot():
    r, c = lax.axis_index("rows"), lax.axis_index("cols")
    return r & 1, ((r >> 1) & 1) * lax.axis_size("cols") + c


def split_halves(sums, mine, other):
    size = mine.shape[0]
    core, _ = core_and_spot()
    mine[...] = sums[pl.ds(pl.multiple_of(core * size, 16), size), :]
    other[...] = sums[pl.ds(pl.multiple_of((1 - core) * size, 16), size), :]


def split_kernel(mine, other, *outs):
    size = outs[0].shape[0]
    _, spot = core_and_spot()
    for k, out in enumerate(outs):
        at = pl.ds(pl.multiple_of((spot ^ k) * size, 16), size)
        out[...] = (mine[at, :].astype(F32) + other[at, :].astype(F32)).astype(BF16)


def tree_sum(parts):
    while len(parts) > 1:
        parts = [parts[i] + parts[i + 1] for i in range(0, len(parts), 2)]
    return parts[0]


def sum_kernel(*refs):
    refs[-1][...] = tree_sum([ref[...].astype(F32) for ref in refs[:-1]]).astype(BF16)


def join_kernel(*refs):
    out, at = refs[-1], 0
    for ref in refs[:-1]:
        out[at : at + ref.shape[0]] = ref[...]
        at += ref.shape[0]


def split_three(x):
    high = x.astype(BF16)
    rest = x - high.astype(F32)
    middle = rest.astype(BF16)
    return high, middle, (rest - middle.astype(F32)).astype(BF16)


def bias_kernel(table, out, padded):
    heads = table.shape[0]
    last_row = lax.axis_index("rows") == lax.axis_size("rows") - 1
    last_col = lax.axis_index("cols") == lax.axis_size("cols") - 1
    padded[...] = jnp.zeros_like(padded)
    padded[:, : table.shape[1]] = table[...]
    offsets = padded[...]
    moved = []
    for c in range(WIN):
        shift = WIN - 1 - c
        moved.append(pltpu.roll(offsets, RELS - shift, 1) if shift else offsets)
    stack = jnp.concatenate(moved, 0)
    high, middle, least = split_three(stack)
    squeeze = squeeze_matrix()
    wide = dot(high, squeeze) + dot(middle, squeeze) + dot(least, squeeze)
    count = WIN * heads
    for r in range(WIN):
        shift = (WIN - 1 - r) * WIN
        rel = pltpu.roll(wide, 2 * KEYS - shift, 1) if shift else wide
        rel = rel[:, :KEYS]
        query = lax.broadcasted_iota(jnp.int32, (count, KEYS), 1)
        row = lax.broadcasted_iota(jnp.int32, (count, KEYS), 0)
        across = (query < TOK // 2) if r >= SHIFT else (query >= TOK // 2)
        query_left = query - WIN * tenth(query) < SHIFT
        own_left = row < SHIFT * heads
        beside = query_left != own_left
        for w in range(2):
            cut_off = across & last_row
            if w == 1:
                cut_off = cut_off | (beside & last_col)
            value = rel + jnp.where(cut_off, -100.0, 0.0)
            out[w, r * count : (r + 1) * count, :] = value
    for w in range(2):
        out[w, TOK * heads :, :] = jnp.full((out.shape[1] - TOK * heads, KEYS), NEVER, F32)


def attention_kernel(
    own, low, right, corner, qkv_w, bias, g1, b1, qb, vb,
    x_out, xw_out, qkv_out, p_out, o_out,
    xf,
):
    gather_frame(xf, own, low, right, corner)
    for t in range(xf.shape[0]):
        for w in range(2):
            xf[t, w, TOK * PAGES :, :] = jnp.zeros((xf.shape[2] - TOK * PAGES, KEYS), F32)
            x_out[w * TOK * PAGES : (w + 1) * TOK * PAGES, t * KEYS : (t + 1) * KEYS] = xf[
                t, w, : TOK * PAGES, :
            ].astype(BF16)

    d = g1.shape[-1]
    heads = d // (KEYS // GROUP)
    scale = (d // heads) ** (-0.5)
    windows = [(page, w) for page in range(PAGES) for w in range(2)]
    x = jnp.concatenate(
        [only_tokens(load_rows(xf, w, page_rows(page, ROWS))) for page, w in windows], 0
    )
    xw_out[...] = x.astype(BF16)
    normed, _ = normalize(x)
    attn_in = (normed * g1[...] + b1[...]).astype(BF16)
    proj = dot(attn_in, qkv_w[...])
    q_all = proj[:, :d] + qb[...]
    k_all = proj[:, d : 2 * d]
    v_all = proj[:, 2 * d :] + vb[...]
    masks = head_masks(ROWS, F32)
    filler = jnp.zeros((KEYS - ROWS, d), F32)
    groups = heads // GROUP
    for start in range(0, len(windows), AT_ONCE):
        scores, values = [], []
        some = windows[start : start + AT_ONCE]
        for n, (page, w) in enumerate(some):
            rows = slice((start + n) * ROWS, (start + n + 1) * ROWS)
            q = jnp.concatenate([q_all[rows], filler], 0).astype(BF16)
            k = jnp.concatenate([k_all[rows], filler], 0).astype(BF16)
            v = jnp.concatenate([v_all[rows], filler], 0).astype(BF16)
            qkv_out[w, page, :, :d] = q
            qkv_out[w, page, :, d : 2 * d] = k
            qkv_out[w, page, :, 2 * d :] = v
            for g in range(groups):
                lanes = slice(g * KEYS, (g + 1) * KEYS)
                scores.append(dot_bt(head_rows(k_all[rows, lanes], masks), q[:, lanes]))
                values.append(head_rows(v_all[rows, lanes], masks))
        probs = []
        for n, s in enumerate(scores):
            page, w = some[n // groups]
            g = n % groups
            es = []
            for h in range(GROUP):
                rel = bias[w, pl.ds(g * GROUP + h, ROWS, stride=heads), :]
                sh = s[h * ROWS : (h + 1) * ROWS] * scale + rel
                e = jnp.exp(sh - jnp.max(sh, 0, keepdims=True))
                es.append(e * (1.0 / jnp.sum(e, 0, keepdims=True)))
            p = jnp.concatenate(es, 0).astype(BF16)
            p_out[w, page, g * GROUP * ROWS : (g + 1) * GROUP * ROWS, :] = p
            probs.append(p)
        parts = [dot_at(p, v)[:ROWS] for p, v in zip(probs, values)]
        for n, (page, w) in enumerate(some):
            joined = jnp.concatenate(parts[n * groups : (n + 1) * groups], 1)
            store_rows(o_out, w, page_rows(page, TOK), joined[:TOK])


def mlp_kernel(
    x_in, o_in, t_own, t_low, t_right, t_corner, count,
    proj_w, fc1_w, fc2_w, pb, g2, b2, f1b, f2b,
    stays, up, side, corner, dy_out, do_out, rows_out, mine, other,
    frame_out, sums_out, tf, fc1_acc, fc2_acc, proj_acc, fc1_sum, small_sum,
):
    gather_frame(tf, t_own, t_low, t_right, t_corner)

    mlp_step(
        x_in, o_in, proj_w, fc1_w, fc2_w, pb, g2, b2, f1b, f2b, frame_out, dy_out, do_out,
        tf, fc1_acc, fc2_acc, proj_acc, fc1_sum, small_sum,
    )

    d = proj_w.shape[0]
    ff = fc1_w.shape[1] // d
    for j in range(ff):
        sums_out[j * d : (j + 1) * d, :] = fc1_acc[:, j * d : (j + 1) * d].astype(BF16)
        sums_out[(ff + j) * d : (ff + j + 1) * d, :] = fc2_acc[j * d : (j + 1) * d, :].astype(BF16)
    at = 2 * ff * d
    sums_out[at : at + d, :] = proj_acc[...].astype(BF16)
    rows = [jnp.sum(fc1_sum[:, j * d : (j + 1) * d], 0, keepdims=True) for j in range(ff)]
    rows += [jnp.sum(small_sum[k], 0, keepdims=True) for k in range(4)]
    rows.append(count[...])
    rows.append(jnp.zeros((16 - len(rows), d), F32))
    rows_out[...] = jnp.concatenate(rows, 0)
    at += d
    if sums_out.shape[0] > at:
        sums_out[at:, :] = jnp.zeros((sums_out.shape[0] - at, d), BF16)
    split_halves(sums_out, mine, other)
    stays[...] = frame_out[:SHIFT, :-SHIFT]
    up[...] = frame_out[SHIFT:, :-SHIFT]
    side[...] = frame_out[:SHIFT, -SHIFT:]
    corner[...] = frame_out[SHIFT:, -SHIFT:]


def both_windows(ref):
    return jnp.concatenate([load_rows(ref, w, slice(0, TOK * PAGES)) for w in range(2)], 0)


def mlp_step(
    x_in, o_in, proj_w, fc1_w, fc2_w, pb, g2, b2, f1b, f2b, frame_out, dy_out, do_out,
    tf, fc1_acc, fc2_acc, proj_acc, fc1_sum, small_sum,
):
    d = x_in.shape[1]
    ff = fc1_w.shape[1] // d
    tokens = TOK * PAGES
    o = both_windows(o_in).astype(BF16)
    y = x_in[...].astype(F32) + dot(o, proj_w[...]) + pb[...]
    normed2, inv2 = normalize(y)
    c = (normed2 * g2[...] + b2[...]).astype(BF16)
    dr = both_windows(tf)
    drb = dr.astype(BF16)
    r = y + f2b[...]
    dc = None
    for j in range(ff):
        at = slice(j * d, (j + 1) * d)
        h = dot(c, fc1_w[:, at]) + f1b[:, at]
        phi = 0.5 * (1.0 + lax.erf(h * math.sqrt(0.5)))
        slope = phi + h * (jnp.exp(h * h * -0.5) * (1.0 / math.sqrt(2.0 * math.pi)))
        gelu = (h * phi).astype(BF16)
        dh_wide = dot_bt(drb, fc2_w[at, :]) * slope
        dh = dh_wide.astype(BF16)
        r = r + dot(gelu, fc2_w[at, :])
        fc2_acc[at, :] = dot_at(gelu, drb)
        fc1_acc[:, at] = dot_at(c, dh)
        fc1_sum[:, at] = fold(dh.astype(F32))
        more = dot_bt(dh, fc1_w[:, at])
        dc = more if dc is None else dc + more
    for w in range(2):
        frame_out[:, w * WIN : (w + 1) * WIN] = (
            r[w * tokens : (w + 1) * tokens].reshape(WIN, WIN, PAGES, d).astype(BF16)
        )
    dy = dr + norm_back(dc * g2[...], normed2, inv2)
    dz = dy.astype(BF16)
    proj_acc[...] = dot_at(o, dz)
    do = dot_bt(dz, proj_w[...])
    for w in range(2):
        rows = slice(w * tokens, (w + 1) * tokens)
        store_rows(do_out, w, slice(0, tokens), do[rows])
        store_rows(dy_out, w, slice(0, tokens), dy[rows])
    small_sum[0] = fold(dc * normed2)
    small_sum[1] = fold(dc)
    small_sum[2] = fold(dr)
    small_sum[3] = fold(dz.astype(F32))


def backward_kernel(
    xw, qkv, p_in, dy_in, do_in, qkv_w, g1, b1, out_side, mlp_rows,
    stays, side, corner, up, mine, other,
    dx, qkv_acc, rel_acc, col_sum, small_sum, mixed, sums_out, joined_all,
):
    rel_acc[...] = jnp.zeros_like(rel_acc)
    for page in range(0, PAGES, BACK_AT_ONCE):
        backward_pages(range(page, page + BACK_AT_ONCE), qkv, p_in, do_in, joined_all, rel_acc)

    d = g1.shape[-1]
    heads = d // (KEYS // GROUP)
    joined = joined_all[...]
    normed, inv = normalize(xw[...].astype(F32))
    attn_in = (normed * g1[...] + b1[...]).astype(BF16)
    qkv_acc[...] = dot_at(attn_in, joined)
    col_sum[...] = fold(joined.astype(F32))
    da = dot_bt(joined, qkv_w[...])
    small_sum[0] = fold(da * normed)
    small_sum[1] = fold(da)
    back = norm_back(da * g1[...], normed, inv)
    for page in range(PAGES):
        rows = page_rows(page, TOK)
        for w in range(2):
            at = (2 * page + w) * ROWS
            store_rows(dx, w, rows, load_rows(dy_in, w, rows) + back[at : at + TOK])
    right = load_rows(dx, 1, slice(None)).reshape(WIN, WIN, PAGES, d)
    left = load_rows(dx, 0, slice(None)).reshape(WIN, WIN, PAGES, d)
    stays[:, :WIN] = left[:SHIFT]
    stays[:, WIN:] = right[:SHIFT, :SHIFT]
    side[:SHIFT] = out_side[...]
    side[SHIFT:] = right[:SHIFT, SHIFT:].astype(BF16)
    corner[...] = right[SHIFT:, SHIFT:].astype(BF16)
    up[:, :WIN] = left[SHIFT:].astype(BF16)
    up[:, WIN:] = right[SHIFT:, :SHIFT].astype(BF16)
    half = sums_out.shape[0] // 2
    part = 3 * d // 2
    for j in range(6):
        at = j // 3 * half + j % 3 * (d // 2)
        rows = slice(j % 2 * (d // 2), (j % 2 + 1) * (d // 2))
        sums_out[at : at + d // 2, :] = qkv_acc[rows, j // 2 * d : (j // 2 + 1) * d].astype(BF16)
    rel = table_gradient(
        [rel_acc[:, h * KEYS : (h + 1) * KEYS] for h in range(heads)], mixed
    )
    rows = [jnp.sum(small_sum[k], 0, keepdims=True) for k in range(2)]
    rows.append(jnp.sum(col_sum[:, :d], 0, keepdims=True))
    rows.append(jnp.sum(col_sum[:, 2 * d :], 0, keepdims=True))
    rows.append(mlp_rows[:12])
    rows.append(rel[:, :d])
    rows.append(jnp.concatenate([rel[:, d:], jnp.zeros((heads, 2 * d - RELS), F32)], 1))
    high, rest = split_rows(jnp.concatenate(rows, 0))
    for start in (0, half):
        at = start + part
        sums_out[at : at + VECTORS, :] = high
        sums_out[at + VECTORS : at + 2 * VECTORS, :] = rest
        at += 2 * VECTORS
        if at < start + half:
            sums_out[at : start + half, :] = jnp.zeros((start + half - at, d), BF16)
    split_halves(sums_out, mine, other)


def backward_pages(pages, qkv, p_in, do_in, joined_all, rel_acc):
    d = qkv.shape[-1] // 3
    heads = d // (KEYS // GROUP)
    groups = heads // GROUP
    scale = (d // heads) ** (-0.5)
    masks = head_masks(ROWS, F32)
    chains = [(page, w, g) for page in pages for w in range(2) for g in range(groups)]
    queries, keys, dos, dps = [], [], [], []
    filler = jnp.zeros((KEYS - ROWS, KEYS), F32)
    for page, w, g in chains:
        lanes = slice(g * KEYS, (g + 1) * KEYS)
        queries.append(qkv[w, page, :, lanes])
        k = qkv[w, page, :, d + g * KEYS : d + (g + 1) * KEYS]
        v = qkv[w, page, :, 2 * d + g * KEYS : 2 * d + (g + 1) * KEYS]
        keys.append(head_rows(k.astype(F32)[:ROWS], masks))
        do = only_tokens(do_in[g, w, page_rows(page, ROWS), :])
        dos.append(jnp.concatenate([do, filler], 0).astype(BF16))
        dps.append(dot_bt(head_rows(v.astype(F32)[:ROWS], masks), dos[-1]))
    dts = []
    rel_sum = [None] * heads
    for c, (page, w, g) in enumerate(chains):
        p = p_in[w, page, g * GROUP * ROWS : (g + 1) * GROUP * ROWS, :].astype(F32)
        t = p * dps[c]
        ds = []
        for h in range(GROUP):
            at = slice(h * ROWS, (h + 1) * ROWS)
            part = t[at] - p[at] * jnp.sum(t[at], 0, keepdims=True)
            head = g * GROUP + h
            rel_sum[head] = part if rel_sum[head] is None else rel_sum[head] + part
            ds.append(part * scale)
        dts.append(jnp.concatenate(ds, 0).astype(BF16))
    for h in range(heads):
        rel_acc[:, h * KEYS : (h + 1) * KEYS] += rel_sum[h]
    parts = {}
    for c, (page, w, g) in enumerate(chains):
        p = p_in[w, page, g * GROUP * ROWS : (g + 1) * GROUP * ROWS, :]
        parts[0, page, w, g] = dot_at(dts[c], keys[c])[:ROWS]
        parts[1, page, w, g] = own_lanes(dot(dts[c], queries[c]))
        parts[2, page, w, g] = own_lanes(dot(p, dos[c]))
    for page in pages:
        for k in range(3):
            for g in range(groups):
                joined = jnp.concatenate([parts[k, page, w, g] for w in range(2)], 0)
                at = k * d + g * KEYS
                joined_all[2 * page * ROWS : 2 * (page + 1) * ROWS, at : at + KEYS] = joined.astype(
                    BF16
                )


def table_gradient(by_head, mixed):
    heads = len(by_head)
    for h in range(heads):
        mixed[pl.ds(h, ROWS, stride=heads), :] = by_head[h]
    wide = None
    for r in range(WIN):
        part = mixed[r * WIN * heads : (r + 1) * WIN * heads, :]
        part = jnp.concatenate([part, jnp.zeros_like(part)], 1)
        shift = (WIN - 1 - r) * WIN
        part = pltpu.roll(part, shift, 1) if shift else part
        wide = part if wide is None else wide + part
    high, rest = split_rows(wide)
    squeeze = squeeze_matrix()
    moved = dot_bt(high, squeeze) + dot_bt(rest, squeeze)
    total = None
    for c in range(WIN):
        part = moved[c * heads : (c + 1) * heads]
        shift = WIN - 1 - c
        part = pltpu.roll(part, shift, 1) if shift else part
        total = part if total is None else total + part
    return total


def collect(buf, mine, other, planes, first, size):
    core, spot = core_and_spot()
    stride = mine.shape[0] // planes
    for c, pieces in ((core, mine), (1 - core, other)):
        for k in range(planes):
            at = pl.multiple_of((c * planes + (spot ^ k)) * size, 16)
            buf[pl.ds(at, size), :] = pieces[k * stride + first : k * stride + first + size, :].astype(
                F32
            )


def gradient_kernel(total, planes, count_row, first, size, mine, up, side, corner, stays, grad):
    _, spot = core_and_spot()
    stride = mine.shape[0] // planes
    count = 0.0
    for row in (count_row, count_row + VECTORS):
        piece, at = row // size, row % size
        start = (spot ^ piece) * stride + first + at // 16 * 16
        block = mine[pl.ds(pl.multiple_of(start, 16), 16), :].astype(F32)
        count = count + block[at % 16 : at % 16 + 1]
    wide = (total / count).reshape(1, 1, 1, count.shape[1])
    rest = up.shape[0]
    grad[:rest, :SHIFT] = corner[...].astype(F32) * wide
    grad[:rest, SHIFT:] = up[...].astype(F32) * wide
    grad[rest:, :SHIFT] = side[SHIFT:].astype(F32) * wide
    grad[rest:, SHIFT:] = stays[...] * wide


def finish_kernel(
    total, planes, sizes, mine, other,
    fc1, fc2, proj, fc1_b, g2, b2, fc2_b, proj_b, qkv, g1, b1, q_b, v_b, rel, buf1, buf2,
):
    collect(buf1, mine, other, planes, 0, sizes[0])
    collect(buf2, mine, other, planes, sizes[0], sizes[1])
    d = proj.shape[0]
    ff = fc1.shape[1] // d
    half, at = buf2.shape[0] // 2, 3 * d // 2
    rows = buf2[at : at + VECTORS, :] + buf2[at + VECTORS : at + 2 * VECTORS, :]
    scale = total / rows[ff + 8 : ff + 9, :]
    rows = rows * scale
    for j in range(ff):
        fc1[:, j * d : (j + 1) * d] = buf1[j * d : (j + 1) * d, :] * scale
        fc2[j * d : (j + 1) * d, :] = buf1[(ff + j) * d : (ff + j + 1) * d, :] * scale
        fc1_b[:, j * d : (j + 1) * d] = rows[4 + j : 5 + j]
    proj[...] = buf1[2 * ff * d : (2 * ff + 1) * d, :] * scale
    for k, ref in enumerate((g2, b2, fc2_b, proj_b)):
        ref[...] = rows[ff + 4 + k : ff + 5 + k]
    for j in range(6):
        at = j // 3 * half + j % 3 * (d // 2)
        part = slice(j % 2 * (d // 2), (j % 2 + 1) * (d // 2))
        qkv[part, j // 2 * d : (j // 2 + 1) * d] = buf2[at : at + d // 2, :] * scale
    for k, ref in enumerate((g1, b1, q_b, v_b)):
        ref[...] = rows[k : k + 1]
    heads = rel.shape[0]
    rel[:, :d] = rows[16 : 16 + heads]
    rel[:, d:] = rows[16 + heads : 16 + 2 * heads, : rel.shape[1] - d]


def permute(block, target):
    rows, cols = lax.axis_size("rows"), lax.axis_size("cols")
    route = []
    for r in range(rows):
        for c in range(cols):
            tr, tc = target(r, c)
            route.append((r * cols + c, (tr % rows) * cols + tc % cols))
    return lax.ppermute(block, ("rows", "cols"), route)


def after(values, done):
    return lax.optimization_barrier((values, done))[0]


def core_hop(r, c):
    return r ^ 1, c


def plane_hop(k):
    cols = lax.axis_size("cols")
    return lambda r, c: (r ^ (2 * (k // cols)), c ^ (k % cols))


def plane_share(pieces):
    return [pieces[0]] + [permute(p, plane_hop(k)) for k, p in enumerate(pieces) if k]


def depth_sum(piece):
    hop = 4
    while hop < lax.axis_size("rows"):
        piece = sum_call([piece, permute(piece, lambda r, c, hop=hop: (r ^ hop, c))])
        hop *= 2
    return piece


def strip_hops():
    return [lambda r, c: (r - 1, c), lambda r, c: (r, c - 1), lambda r, c: (r - 1, c - 1)]


def in_vmem():
    return pl.BlockSpec(memory_space=pltpu.VMEM)


def to_vmem(a):
    return pltpu.with_memory_space_constraint(a, pltpu.VMEM)


def limit(mib):
    return pltpu.CompilerParams(vmem_limit_bytes=mib * 1024 * 1024)


def strip_shapes(field):
    rows, cols, pages, d = field.shape
    return [
        pltpu.VMEM(s, BF16)
        for s in (
            (SHIFT, cols, pages, d), (rows - SHIFT, SHIFT, pages, d), (SHIFT, SHIFT, pages, d)
        )
    ]


def in_hbm():
    return pl.BlockSpec(memory_space=pltpu.HBM)


def to_hbm(a):
    return pltpu.with_memory_space_constraint(a, pltpu.HBM)


def strips_call(field):
    return pl.pallas_call(
        strips_kernel,
        in_specs=[in_hbm()],
        out_specs=[in_vmem()] * 3,
        out_shape=strip_shapes(field),
        scratch_shapes=[pltpu.SemaphoreType.DMA((3,))],
        compiler_params=limit(4),
        name="input_strips",
    )(to_hbm(field))


def target_call(target, kept, table):
    return pl.pallas_call(
        target_kernel,
        in_specs=[in_hbm()] * 3,
        out_specs=[in_vmem()] * 6,
        out_shape=[
            pltpu.VMEM(target.shape, BF16), *strip_shapes(target),
            pltpu.VMEM((1, target.shape[-1]), F32), pltpu.VMEM(table.shape, F32),
        ],
        scratch_shapes=[
            pltpu.VMEM(target.shape, BF16), pltpu.VMEM(kept.shape, kept.dtype),
            pltpu.SemaphoreType.DMA((3,)),
        ],
        compiler_params=limit(8),
        name="masked_target",
    )(*map(to_hbm, (target, kept, table)))


def split_call(mine, other):
    planes = 2 * lax.axis_size("cols")
    n, d = mine.shape
    return pl.pallas_call(
        split_kernel,
        in_specs=[in_vmem()] * 2,
        out_specs=[in_vmem()] * planes,
        out_shape=[pltpu.VMEM((n // planes, d), BF16)] * planes,
        compiler_params=limit(4),
        name="split_sums",
    )(*map(to_vmem, (mine, other)))


def local_call(kernel, rows, parts, name):
    return pl.pallas_call(
        kernel,
        in_specs=[in_vmem()] * len(parts),
        out_specs=in_vmem(),
        out_shape=pltpu.VMEM((rows,) + parts[-1].shape[1:], BF16),
        compiler_params=limit(4),
        name=name,
    )(*map(to_vmem, parts))


def sum_call(parts):
    return local_call(sum_kernel, parts[0].shape[0], parts, "add_pieces")


def join_call(parts):
    return local_call(join_kernel, sum(a.shape[0] for a in parts), parts, "join_pieces")


def bias_call(rel_table):
    heads = rel_table.shape[0]
    return pl.pallas_call(
        bias_kernel,
        in_specs=[in_vmem()],
        out_specs=in_vmem(),
        out_shape=pltpu.VMEM((2, ROWS * heads, KEYS), F32),
        scratch_shapes=[pltpu.VMEM((heads, RELS), F32)],
        compiler_params=limit(VMEM_LIMIT),
        name="attention_bias",
    )(to_vmem(rel_table))


def cost(flops):
    return pl.CostEstimate(flops=flops, bytes_accessed=10**7, transcendentals=10**6)


def attention_call(patches, p_strips, qkv_w, bias, g1, b1, q_b, v_b):
    pages, d = patches.shape[2:]
    heads = bias.shape[1] // ROWS
    tokens = 2 * TOK * pages
    shape = pltpu.VMEM
    inputs = [patches, *p_strips, qkv_w, bias, g1, b1, q_b, v_b]
    outs = [
        shape((tokens, d), BF16),
        shape((2 * pages * ROWS, d), BF16),
        shape((2, pages, KEYS, 3 * d), BF16),
        shape((2, pages, heads * ROWS, KEYS), BF16),
        shape((d // KEYS, 2, TOK * pages, KEYS), F32),
    ]
    return pl.pallas_call(
        attention_kernel,
        in_specs=[in_vmem()] * len(inputs),
        out_specs=[in_vmem()] * len(outs),
        out_shape=outs,
        scratch_shapes=[pltpu.VMEM((d // KEYS, 2, ROWS * pages, KEYS), F32)],
        compiler_params=limit(VMEM_LIMIT),
        cost_estimate=cost(10**10),
        name="attention_forward",
    )(*map(to_vmem, inputs))


def mlp_call(size, x, mixed, masked, t_strips, count, *weights):
    height, width, pages, d = masked.shape
    ff = weights[1].shape[1]
    shape = pltpu.VMEM
    inputs = [x, mixed, masked, *t_strips, count, *weights]
    rest = WIN - SHIFT
    outs = [
        shape((SHIFT, width - SHIFT, pages, d), BF16), shape((rest, width - SHIFT, pages, d), BF16),
        shape((SHIFT, SHIFT, pages, d), BF16), shape((rest, SHIFT, pages, d), BF16),
        shape((d // KEYS, 2, ROWS * pages, KEYS), F32),
        shape((d // KEYS, 2, ROWS * pages, KEYS), F32),
        shape((16, d), F32), shape((size // 2, d), BF16), shape((size // 2, d), BF16),
    ]
    return pl.pallas_call(
        mlp_kernel,
        in_specs=[in_vmem()] * len(inputs),
        out_specs=[in_vmem()] * len(outs),
        out_shape=outs,
        scratch_shapes=[
            pltpu.VMEM((height, width, pages, d), BF16),
            pltpu.VMEM((size, d), BF16),
            pltpu.VMEM((d // KEYS, 2, TOK * pages, KEYS), F32),
            pltpu.VMEM((d, ff), F32),
            pltpu.VMEM((ff, d), F32),
            pltpu.VMEM((d, d), F32),
            pltpu.VMEM((8, ff), F32),
            pltpu.VMEM((4, 8, d), F32),
        ],
        compiler_params=limit(VMEM_LIMIT),
        cost_estimate=cost(10**10),
        name="mlp_forward_backward",
    )(*map(to_vmem, inputs))


def backward_call(size, xw, qkv, probs, dy, do, *more):
    pages, d = probs.shape[1], xw.shape[1]
    heads = probs.shape[2] // ROWS
    shape = pltpu.VMEM
    inputs = [xw, qkv, probs, dy, do, *more]
    rest = WIN - SHIFT
    outs = [
        shape((SHIFT, 2 * WIN - SHIFT, pages, d), F32), shape((2 * SHIFT, SHIFT, pages, d), BF16),
        shape((rest, SHIFT, pages, d), BF16),
        shape((rest, 2 * WIN - SHIFT, pages, d), BF16), shape((size // 2, d), BF16),
        shape((size // 2, d), BF16),
    ]
    return pl.pallas_call(
        backward_kernel,
        in_specs=[in_vmem()] * len(inputs),
        out_specs=[in_vmem()] * len(outs),
        out_shape=outs,
        scratch_shapes=[
            shape((d // KEYS, 2, TOK * pages, KEYS), F32),
            shape((d, 3 * d), F32),
            shape((ROWS, heads * KEYS), F32),
            shape((8, 3 * d), F32),
            shape((2, 8, d), F32),
            shape((ROWS * heads, KEYS), F32),
            shape((size, d), BF16),
            shape((2 * pages * ROWS, 3 * d), BF16),
        ],
        compiler_params=limit(VMEM_LIMIT),
        cost_estimate=cost(10**10),
        name="attention_backward",
    )(*map(to_vmem, inputs))


def gradient_call(total, planes, ff, n1, n2, *inputs):
    d = inputs[0].shape[1]
    first, size = n1 // (2 * planes), n2 // (2 * planes)
    count_row = 3 * d // 2 + ff // d + 8
    return pl.pallas_call(
        lambda *refs: gradient_kernel(total, planes, count_row, first, size, *refs),
        in_specs=[in_vmem()] * len(inputs),
        out_shape=jax.ShapeDtypeStruct((WIN, 2 * WIN) + inputs[1].shape[2:], F32),
        compiler_params=limit(VMEM_LIMIT),
        name="input_gradient",
    )(*map(to_vmem, inputs))


def finish_call(total, planes, ff, n1, n2, rel_shape, *inputs):
    d = inputs[0].shape[1]
    row = (1, d)
    shapes = [(d, ff), (ff, d), (d, d), (1, ff), row, row, row, row, (d, 3 * d)]
    shapes += [row, row, row, row, rel_shape]
    sizes = (n1 // (2 * planes), n2 // (2 * planes))
    return pl.pallas_call(
        lambda *refs: finish_kernel(total, planes, sizes, *refs),
        in_specs=[in_vmem()] * len(inputs),
        out_shape=[jax.ShapeDtypeStruct(s, F32) for s in shapes],
        scratch_shapes=[pltpu.VMEM((n1, d), F32), pltpu.VMEM((n2, d), F32)],
        compiler_params=limit(VMEM_LIMIT),
        name="finish_sums",
    )(*map(to_vmem, inputs))


def shards(
    patches, target, kept_mask, ln1_gain, ln1_bias, qkv_weight, query_bias, value_bias, rel_table,
    proj_weight, proj_bias, ln2_gain, ln2_bias, fc1_weight, fc1_bias, fc2_weight, fc2_bias,
):
    pages, height, width, d = patches.shape
    ff = fc1_weight.shape[1]
    rows, cols = lax.axis_size("rows"), lax.axis_size("cols")
    planes = 2 * cols
    step = 32 * planes
    tokens = pages * height * width
    vec = lambda a: a.reshape(1, -1)
    n1 = -(-(2 * ff + d) // step) * step
    n2 = -(-(3 * d + 4 * VECTORS) // step) * step

    patches = patches.transpose(1, 2, 0, 3)
    p_strips = [permute(a, hop) for a, hop in zip(strips_call(patches), strip_hops())]
    masked, *t_strips, count, table = target_call(
        target.transpose(1, 2, 0, 3), kept_mask.transpose(1, 0, 2), rel_table
    )
    t_strips = [permute(a, hop) for a, hop in zip(t_strips, strip_hops())]
    bias = bias_call(table)

    g1, b1 = vec(ln1_gain), vec(ln1_bias)
    x, xw, qkv, probs, mixed = attention_call(
        patches, p_strips, qkv_weight, bias, g1, b1, vec(query_bias), vec(value_bias)
    )
    out_stays, out_up, out_side, out_corner, dy, do, mlp_rows, mine, other = mlp_call(
        n1, x, mixed, masked, t_strips, count, proj_weight, fc1_weight, fc2_weight,
        vec(proj_bias), vec(ln2_gain), vec(ln2_bias), vec(fc1_bias), vec(fc2_bias),
    )

    to_right, to_below = (lambda r, c: (r, c + 1)), (lambda r, c: (r + 1, c))
    across = lambda r, c: (r + 1, c + 1)
    out_up, out_corner = permute(out_up, to_below), permute(out_corner, across)

    pieces = split_call(mine, permute(other, core_hop))
    got = plane_share(pieces)
    do = after(do, pieces)
    stays, side, corner, up, mine2, other2 = backward_call(
        n2, xw, qkv, probs, dy, do, qkv_weight, g1, b1, out_side, mlp_rows
    )
    got, out_up, out_corner = after((got, out_up, out_corner), mine2)
    piece = sum_call(got)
    mine2, other2, up, out_up, out_corner = after(
        (mine2, other2, up, out_up, out_corner), piece
    )

    pieces2 = split_call(mine2, permute(other2, core_hop))
    piece2 = sum_call(plane_share(pieces2))
    up, side, corner = after((up, side, corner), piece2)
    piece = join_call([piece, piece2])
    up, side, corner = permute(up, to_below), permute(side, to_right), permute(corner, across)
    piece = depth_sum(piece)
    piece, up, side, corner = after((piece, up, side, corner), up)
    mine = join_call(plane_share([piece] * planes))
    other = permute(mine, core_hop)
    top = jnp.concatenate([out_corner, out_up], 1)
    bottom = jnp.concatenate([side[:SHIFT], out_stays], 1)
    output = jnp.concatenate([top, bottom], 0)
    mine, output = after((mine, output), output)
    total = float(tokens * rows * cols)
    grad = gradient_call(total, planes, ff, n1, n2, mine, up, side, corner, stays)
    other, grad = after((other, grad), grad)
    (
        fc1_g, fc2_g, proj_g, fc1_bg, g2_g, b2_g, fc2_bg, proj_bg, qkv_g, g1_g, b1_g, q_bg,
        v_bg, rel_g,
    ) = finish_call(
        total, planes, ff, n1, n2, rel_table.shape, mine, other
    )
    flat = lambda a: a.reshape(-1)
    return (
        output.transpose(2, 0, 1, 3),
        grad.transpose(2, 0, 1, 3),
        flat(g1_g),
        flat(b1_g),
        qkv_g,
        flat(q_bg),
        flat(v_bg),
        rel_g,
        proj_g,
        flat(proj_bg),
        flat(g2_g),
        flat(b2_g),
        fc1_g,
        flat(fc1_bg),
        fc2_g,
        flat(fc2_bg),
    )


def solution(mesh):
    field = P(None, "rows", "cols", None)
    return jax.shard_map(
        shards,
        mesh=mesh,
        in_specs=(field, field, P(None, "rows", "cols")) + (P(),) * 14,
        out_specs=(field, field) + (P(),) * 14,
        check_vma=False,
    )
```

```python
import math

import jax
import jax.numpy as jnp
from jax import lax
from jax.experimental import pallas as pl
from jax.experimental.pallas import tpu as pltpu
from jax.sharding import PartitionSpec as P

WIN = 10
SHIFT = 5
EPS = 1e-05
F32 = jnp.float32
BF16 = jnp.bfloat16

SPAN = 2 * WIN - 1
TOK = WIN * WIN
ROWS = 104
PAD_ROWS = ROWS + 1
KEYS = 128
GROUP = 4
RELS = 384
NEVER = -1e30
PAGES = 8
VECTORS = 32
BACK_AT_ONCE = 1
AT_ONCE = 4
VMEM_LIMIT = 20


def dot(a, b):
    return lax.dot_general(a, b, (((1,), (0,)), ((), ())), preferred_element_type=F32)


def dot_bt(a, b):
    return lax.dot_general(a, b, (((1,), (1,)), ((), ())), preferred_element_type=F32)


def dot_at(a, b):
    return lax.dot_general(a, b, (((0,), (0,)), ((), ())), preferred_element_type=F32)


def normalize(x):
    center = x - jnp.sum(x, -1, keepdims=True) * (1.0 / x.shape[-1])
    inv = lax.rsqrt(jnp.sum(center * center, -1, keepdims=True) * (1.0 / x.shape[-1]) + EPS)
    return center * inv, inv


def norm_back(up, normed, inv):
    scale = 1.0 / up.shape[-1]
    mean_up = jnp.sum(up, -1, keepdims=True) * scale
    mean_un = jnp.sum(up * normed, -1, keepdims=True) * scale
    return inv * (up - mean_up - normed * mean_un)


def fold(x):
    return jnp.sum(x.reshape(x.shape[0] // 8, 8, x.shape[1]), 0)


def head_masks(rows, dtype):
    lane = lax.broadcasted_iota(jnp.int32, (rows, KEYS), 1)
    width = KEYS // GROUP
    return [
        ((lane >= k * width) & (lane < (k + 1) * width)).astype(F32).astype(dtype)
        for k in range(GROUP)
    ]


def head_rows(x, masks):
    return jnp.concatenate([x * m for m in masks], 0).astype(BF16)


def own_lanes(stacked):
    lane = lax.broadcasted_iota(jnp.int32, (ROWS, KEYS), 1)
    out = stacked[(GROUP - 1) * ROWS :]
    for h in reversed(range(GROUP - 1)):
        out = jnp.where(lane < (h + 1) * (KEYS // GROUP), stacked[h * ROWS : (h + 1) * ROWS], out)
    return out


def split_rows(x):
    high = x.astype(BF16)
    return high, (x - high.astype(F32)).astype(BF16)


def page_rows(page, count):
    return pl.ds(page, count, stride=PAGES)


def load_rows(ref, w, rows):
    return jnp.concatenate([ref[t, w, rows, :] for t in range(ref.shape[0])], 1)


def store_rows(ref, w, rows, value):
    for t in range(ref.shape[0]):
        ref[t, w, rows, :] = value[:, t * KEYS : (t + 1) * KEYS]


def only_tokens(x):
    return jnp.where(lax.broadcasted_iota(jnp.int32, x.shape, 0) < TOK, x, 0.0)


def gather_frame(out, own, low, right, corner):
    for w in range(2):
        for r in range(WIN):
            if r < WIN - SHIFT:
                main, side, mr, sr = own, right, r + SHIFT, r
            else:
                main, side, mr, sr = low, corner, r - SHIFT, r - SHIFT
            if w == 0:
                block = main[mr, SHIFT : SHIFT + WIN].astype(F32)
            else:
                block = jnp.concatenate(
                    [main[mr, SHIFT + WIN :].astype(F32), side[sr].astype(F32)], 0
                )
            at = r * WIN * PAGES
            store_rows(
                out, w, slice(at, at + WIN * PAGES), block.reshape(WIN * PAGES, block.shape[-1])
            )


def tenth(n):
    return (n * 205) >> 11


def squeeze_matrix():
    at = lax.broadcasted_iota(jnp.int32, (RELS, 2 * KEYS), 0)
    to = lax.broadcasted_iota(jnp.int32, (RELS, 2 * KEYS), 1)
    hit = (at == to + (SPAN - WIN) * tenth(to)) & (to < SPAN * WIN)
    return hit.astype(F32).astype(BF16)


def copy_all(pairs, sems):
    copies = [pltpu.make_async_copy(a, b, sems.at[k]) for k, (a, b) in enumerate(pairs)]
    for copy in copies:
        copy.start()
    for copy in copies:
        copy.wait()


def strips_kernel(field, low, right, corner, sems):
    copy_all(
        (
            (field.at[:SHIFT], low), (field.at[SHIFT:, :SHIFT], right),
            (field.at[:SHIFT, :SHIFT], corner),
        ),
        sems,
    )


def target_kernel(
    target_in, kept_in, table_in, masked, low, right, corner, count, table, target, kept, sems
):
    copy_all(((target_in, target), (kept_in, kept), (table_in, table)), sems)
    rows, cols = target.shape[:2]
    total = jnp.zeros(kept.shape[1:], F32)
    for r in range(rows):
        kept_row = kept[r].astype(F32)
        total = total + kept_row
        for c in range(cols):
            masked[r, c] = (target[r, c].astype(F32) * kept_row[:, c : c + 1]).astype(BF16)
    low[...] = masked[:SHIFT]
    right[...] = masked[SHIFT:, :SHIFT]
    corner[...] = masked[:SHIFT, :SHIFT]
    total = jnp.sum(jnp.sum(total, 1, keepdims=True), 0, keepdims=True)
    count[...] = jnp.broadcast_to(total, count.shape)


def core_and_spot():
    r, c = lax.axis_index("rows"), lax.axis_index("cols")
    return r & 1, ((r >> 1) & 1) * lax.axis_size("cols") + c


def split_halves(sums, mine, other):
    size = mine.shape[0]
    core, _ = core_and_spot()
    mine[...] = sums[pl.ds(pl.multiple_of(core * size, 16), size), :]
    other[...] = sums[pl.ds(pl.multiple_of((1 - core) * size, 16), size), :]


def split_kernel(mine, other, *outs):
    size = outs[0].shape[0]
    _, spot = core_and_spot()
    for k, out in enumerate(outs):
        at = pl.ds(pl.multiple_of((spot ^ k) * size, 16), size)
        out[...] = (mine[at, :].astype(F32) + other[at, :].astype(F32)).astype(BF16)


def tree_sum(parts):
    while len(parts) > 1:
        parts = [parts[i] + parts[i + 1] for i in range(0, len(parts), 2)]
    return parts[0]


def sum_kernel(*refs):
    refs[-1][...] = tree_sum([ref[...].astype(F32) for ref in refs[:-1]]).astype(BF16)


def join_kernel(*refs):
    out, at = refs[-1], 0
    for ref in refs[:-1]:
        out[at : at + ref.shape[0]] = ref[...]
        at += ref.shape[0]


def split_three(x):
    high = x.astype(BF16)
    rest = x - high.astype(F32)
    middle = rest.astype(BF16)
    return high, middle, (rest - middle.astype(F32)).astype(BF16)


def bias_kernel(table, out, padded):
    heads = table.shape[0]
    last_row = lax.axis_index("rows") == lax.axis_size("rows") - 1
    last_col = lax.axis_index("cols") == lax.axis_size("cols") - 1
    padded[...] = jnp.zeros_like(padded)
    padded[:, : table.shape[1]] = table[...]
    offsets = padded[...]
    moved = []
    for c in range(WIN):
        shift = WIN - 1 - c
        moved.append(pltpu.roll(offsets, RELS - shift, 1) if shift else offsets)
    stack = jnp.concatenate(moved, 0)
    high, middle, least = split_three(stack)
    squeeze = squeeze_matrix()
    wide = dot(high, squeeze) + dot(middle, squeeze) + dot(least, squeeze)
    count = WIN * heads
    for r in range(WIN):
        shift = (WIN - 1 - r) * WIN
        rel = pltpu.roll(wide, 2 * KEYS - shift, 1) if shift else wide
        rel = rel[:, :KEYS]
        query = lax.broadcasted_iota(jnp.int32, (count, KEYS), 1)
        row = lax.broadcasted_iota(jnp.int32, (count, KEYS), 0)
        across = (query < TOK // 2) if r >= SHIFT else (query >= TOK // 2)
        query_left = query - WIN * tenth(query) < SHIFT
        own_left = row < SHIFT * heads
        beside = query_left != own_left
        for w in range(2):
            cut_off = across & last_row
            if w == 1:
                cut_off = cut_off | (beside & last_col)
            value = rel + jnp.where(cut_off, -100.0, 0.0)
            out[w, r * count : (r + 1) * count, :] = value
    for w in range(2):
        out[w, TOK * heads :, :] = jnp.full((out.shape[1] - TOK * heads, KEYS), NEVER, F32)


def attention_kernel(
    own, low, right, corner, qkv_w, bias, g1, b1, qb, vb,
    x_out, xw_out, qkv_out, p_out, o_out,
    xf,
):
    gather_frame(xf, own, low, right, corner)
    for t in range(xf.shape[0]):
        for w in range(2):
            xf[t, w, TOK * PAGES :, :] = jnp.zeros((xf.shape[2] - TOK * PAGES, KEYS), F32)
            x_out[w * TOK * PAGES : (w + 1) * TOK * PAGES, t * KEYS : (t + 1) * KEYS] = xf[
                t, w, : TOK * PAGES, :
            ].astype(BF16)

    d = g1.shape[-1]
    heads = d // (KEYS // GROUP)
    scale = (d // heads) ** (-0.5)
    windows = [(page, w) for page in range(PAGES) for w in range(2)]
    x = jnp.concatenate(
        [only_tokens(load_rows(xf, w, page_rows(page, ROWS))) for page, w in windows], 0
    )
    xw_out[...] = x.astype(BF16)
    normed, _ = normalize(x)
    attn_in = (normed * g1[...] + b1[...]).astype(BF16)
    proj = dot(attn_in, qkv_w[...])
    q_all = proj[:, :d] + qb[...]
    k_all = proj[:, d : 2 * d]
    v_all = proj[:, 2 * d :] + vb[...]
    masks = head_masks(ROWS, F32)
    filler = jnp.zeros((KEYS - ROWS, d), F32)
    groups = heads // GROUP
    for start in range(0, len(windows), AT_ONCE):
        scores, values = [], []
        some = windows[start : start + AT_ONCE]
        for n, (page, w) in enumerate(some):
            rows = slice((start + n) * ROWS, (start + n + 1) * ROWS)
            q = jnp.concatenate([q_all[rows], filler], 0).astype(BF16)
            k = jnp.concatenate([k_all[rows], filler], 0).astype(BF16)
            v = jnp.concatenate([v_all[rows], filler], 0).astype(BF16)
            qkv_out[w, page, :, :d] = q
            qkv_out[w, page, :, d : 2 * d] = k
            qkv_out[w, page, :, 2 * d :] = v
            for g in range(groups):
                lanes = slice(g * KEYS, (g + 1) * KEYS)
                scores.append(dot_bt(head_rows(k_all[rows, lanes], masks), q[:, lanes]))
                values.append(head_rows(v_all[rows, lanes], masks))
        probs = []
        for n, s in enumerate(scores):
            page, w = some[n // groups]
            g = n % groups
            es = []
            for h in range(GROUP):
                rel = bias[w, pl.ds(g * GROUP + h, ROWS, stride=heads), :]
                sh = s[h * ROWS : (h + 1) * ROWS] * scale + rel
                e = jnp.exp(sh - jnp.max(sh, 0, keepdims=True))
                es.append(e * (1.0 / jnp.sum(e, 0, keepdims=True)))
            p = jnp.concatenate(es, 0).astype(BF16)
            p_out[w, page, g * GROUP * ROWS : (g + 1) * GROUP * ROWS, :] = p
            probs.append(p)
        parts = [dot_at(p, v)[:ROWS] for p, v in zip(probs, values)]
        for n, (page, w) in enumerate(some):
            joined = jnp.concatenate(parts[n * groups : (n + 1) * groups], 1)
            store_rows(o_out, w, page_rows(page, TOK), joined[:TOK])


def mlp_kernel(
    x_in, o_in, t_own, t_low, t_right, t_corner, count,
    proj_w, fc1_w, fc2_w, pb, g2, b2, f1b, f2b,
    stays, up, side, corner, dy_out, do_out, rows_out, mine, other,
    frame_out, sums_out, tf, fc1_acc, fc2_acc, proj_acc, fc1_sum, small_sum,
):
    gather_frame(tf, t_own, t_low, t_right, t_corner)

    mlp_step(
        x_in, o_in, proj_w, fc1_w, fc2_w, pb, g2, b2, f1b, f2b, frame_out, dy_out, do_out,
        tf, fc1_acc, fc2_acc, proj_acc, fc1_sum, small_sum,
    )

    d = proj_w.shape[0]
    ff = fc1_w.shape[1] // d
    for j in range(ff):
        sums_out[j * d : (j + 1) * d, :] = fc1_acc[:, j * d : (j + 1) * d].astype(BF16)
        sums_out[(ff + j) * d : (ff + j + 1) * d, :] = fc2_acc[j * d : (j + 1) * d, :].astype(BF16)
    at = 2 * ff * d
    sums_out[at : at + d, :] = proj_acc[...].astype(BF16)
    rows = [jnp.sum(fc1_sum[:, j * d : (j + 1) * d], 0, keepdims=True) for j in range(ff)]
    rows += [jnp.sum(small_sum[k], 0, keepdims=True) for k in range(4)]
    rows.append(count[...])
    rows.append(jnp.zeros((16 - len(rows), d), F32))
    rows_out[...] = jnp.concatenate(rows, 0)
    at += d
    if sums_out.shape[0] > at:
        sums_out[at:, :] = jnp.zeros((sums_out.shape[0] - at, d), BF16)
    split_halves(sums_out, mine, other)
    stays[...] = frame_out[:SHIFT, :-SHIFT]
    up[...] = frame_out[SHIFT:, :-SHIFT]
    side[...] = frame_out[:SHIFT, -SHIFT:]
    corner[...] = frame_out[SHIFT:, -SHIFT:]


def both_windows(ref):
    return jnp.concatenate([load_rows(ref, w, slice(0, TOK * PAGES)) for w in range(2)], 0)


def mlp_step(
    x_in, o_in, proj_w, fc1_w, fc2_w, pb, g2, b2, f1b, f2b, frame_out, dy_out, do_out,
    tf, fc1_acc, fc2_acc, proj_acc, fc1_sum, small_sum,
):
    d = x_in.shape[1]
    ff = fc1_w.shape[1] // d
    tokens = TOK * PAGES
    o = both_windows(o_in).astype(BF16)
    y = x_in[...].astype(F32) + dot(o, proj_w[...]) + pb[...]
    normed2, inv2 = normalize(y)
    c = (normed2 * g2[...] + b2[...]).astype(BF16)
    dr = both_windows(tf)
    drb = dr.astype(BF16)
    r = y + f2b[...]
    dc = None
    for j in range(ff):
        at = slice(j * d, (j + 1) * d)
        h = dot(c, fc1_w[:, at]) + f1b[:, at]
        phi = 0.5 * (1.0 + lax.erf(h * math.sqrt(0.5)))
        slope = phi + h * (jnp.exp(h * h * -0.5) * (1.0 / math.sqrt(2.0 * math.pi)))
        gelu = (h * phi).astype(BF16)
        dh_wide = dot_bt(drb, fc2_w[at, :]) * slope
        dh = dh_wide.astype(BF16)
        r = r + dot(gelu, fc2_w[at, :])
        fc2_acc[at, :] = dot_at(gelu, drb)
        fc1_acc[:, at] = dot_at(c, dh)
        fc1_sum[:, at] = fold(dh.astype(F32))
        more = dot_bt(dh, fc1_w[:, at])
        dc = more if dc is None else dc + more
    for w in range(2):
        frame_out[:, w * WIN : (w + 1) * WIN] = (
            r[w * tokens : (w + 1) * tokens].reshape(WIN, WIN, PAGES, d).astype(BF16)
        )
    dy = dr + norm_back(dc * g2[...], normed2, inv2)
    dz = dy.astype(BF16)
    proj_acc[...] = dot_at(o, dz)
    do = dot_bt(dz, proj_w[...])
    for w in range(2):
        rows = slice(w * tokens, (w + 1) * tokens)
        store_rows(do_out, w, slice(0, tokens), do[rows])
        store_rows(dy_out, w, slice(0, tokens), dy[rows])
    small_sum[0] = fold(dc * normed2)
    small_sum[1] = fold(dc)
    small_sum[2] = fold(dr)
    small_sum[3] = fold(dz.astype(F32))


def backward_kernel(
    xw, qkv, p_in, dy_in, do_in, qkv_w, g1, b1, out_side, mlp_rows,
    stays, side, corner, up, mine, other,
    dx, qkv_acc, rel_acc, col_sum, small_sum, mixed, sums_out, joined_all,
):
    rel_acc[...] = jnp.zeros_like(rel_acc)
    for page in range(0, PAGES, BACK_AT_ONCE):
        backward_pages(range(page, page + BACK_AT_ONCE), qkv, p_in, do_in, joined_all, rel_acc)

    d = g1.shape[-1]
    heads = d // (KEYS // GROUP)
    joined = joined_all[...]
    normed, inv = normalize(xw[...].astype(F32))
    attn_in = (normed * g1[...] + b1[...]).astype(BF16)
    qkv_acc[...] = dot_at(attn_in, joined)
    col_sum[...] = fold(joined.astype(F32))
    da = dot_bt(joined, qkv_w[...])
    small_sum[0] = fold(da * normed)
    small_sum[1] = fold(da)
    back = norm_back(da * g1[...], normed, inv)
    for page in range(PAGES):
        rows = page_rows(page, TOK)
        for w in range(2):
            at = (2 * page + w) * ROWS
            store_rows(dx, w, rows, load_rows(dy_in, w, rows) + back[at : at + TOK])
    right = load_rows(dx, 1, slice(0, TOK * PAGES)).reshape(WIN, WIN, PAGES, d)
    left = load_rows(dx, 0, slice(0, TOK * PAGES)).reshape(WIN, WIN, PAGES, d)
    stays[:, :WIN] = left[:SHIFT]
    stays[:, WIN:] = right[:SHIFT, :SHIFT]
    side[:SHIFT] = out_side[...]
    side[SHIFT:] = right[:SHIFT, SHIFT:].astype(BF16)
    corner[...] = right[SHIFT:, SHIFT:].astype(BF16)
    up[:, :WIN] = left[SHIFT:].astype(BF16)
    up[:, WIN:] = right[SHIFT:, :SHIFT].astype(BF16)
    half = sums_out.shape[0] // 2
    part = 3 * d // 2
    for j in range(6):
        at = j // 3 * half + j % 3 * (d // 2)
        rows = slice(j % 2 * (d // 2), (j % 2 + 1) * (d // 2))
        sums_out[at : at + d // 2, :] = qkv_acc[rows, j // 2 * d : (j // 2 + 1) * d].astype(BF16)
    rel = table_gradient(
        [rel_acc[:, h * KEYS : (h + 1) * KEYS] for h in range(heads)], mixed
    )
    rows = [jnp.sum(small_sum[k], 0, keepdims=True) for k in range(2)]
    rows.append(jnp.sum(col_sum[:, :d], 0, keepdims=True))
    rows.append(jnp.sum(col_sum[:, 2 * d :], 0, keepdims=True))
    rows.append(mlp_rows[:12])
    rows.append(rel[:, :d])
    rows.append(jnp.concatenate([rel[:, d:], jnp.zeros((heads, 2 * d - RELS), F32)], 1))
    high, rest = split_rows(jnp.concatenate(rows, 0))
    for start in (0, half):
        at = start + part
        sums_out[at : at + VECTORS, :] = high
        sums_out[at + VECTORS : at + 2 * VECTORS, :] = rest
        at += 2 * VECTORS
        if at < start + half:
            sums_out[at : start + half, :] = jnp.zeros((start + half - at, d), BF16)
    split_halves(sums_out, mine, other)


def backward_pages(pages, qkv, p_in, do_in, joined_all, rel_acc):
    d = qkv.shape[-1] // 3
    heads = d // (KEYS // GROUP)
    groups = heads // GROUP
    scale = (d // heads) ** (-0.5)
    masks = head_masks(ROWS, F32)
    chains = [(page, w, g) for page in pages for w in range(2) for g in range(groups)]
    queries, keys, dos, dps = [], [], [], []
    filler = jnp.zeros((KEYS - ROWS, KEYS), F32)
    for page, w, g in chains:
        lanes = slice(g * KEYS, (g + 1) * KEYS)
        queries.append(qkv[w, page, :, lanes])
        k = qkv[w, page, :, d + g * KEYS : d + (g + 1) * KEYS]
        v = qkv[w, page, :, 2 * d + g * KEYS : 2 * d + (g + 1) * KEYS]
        keys.append(head_rows(k.astype(F32)[:ROWS], masks))
        do = only_tokens(do_in[g, w, page_rows(page, ROWS), :])
        dos.append(jnp.concatenate([do, filler], 0).astype(BF16))
        dps.append(dot_bt(head_rows(v.astype(F32)[:ROWS], masks), dos[-1]))
    dts = []
    rel_sum = [None] * heads
    for c, (page, w, g) in enumerate(chains):
        p = p_in[w, page, g * GROUP * ROWS : (g + 1) * GROUP * ROWS, :].astype(F32)
        t = p * dps[c]
        ds = []
        for h in range(GROUP):
            at = slice(h * ROWS, (h + 1) * ROWS)
            part = t[at] - p[at] * jnp.sum(t[at], 0, keepdims=True)
            head = g * GROUP + h
            rel_sum[head] = part if rel_sum[head] is None else rel_sum[head] + part
            ds.append(part * scale)
        dts.append(jnp.concatenate(ds, 0).astype(BF16))
    for h in range(heads):
        rel_acc[:, h * KEYS : (h + 1) * KEYS] += rel_sum[h]
    parts = {}
    for c, (page, w, g) in enumerate(chains):
        p = p_in[w, page, g * GROUP * ROWS : (g + 1) * GROUP * ROWS, :]
        parts[0, page, w, g] = dot_at(dts[c], keys[c])[:ROWS]
        parts[1, page, w, g] = own_lanes(dot(dts[c], queries[c]))
        parts[2, page, w, g] = own_lanes(dot(p, dos[c]))
    for page in pages:
        for k in range(3):
            for g in range(groups):
                joined = jnp.concatenate([parts[k, page, w, g] for w in range(2)], 0)
                at = k * d + g * KEYS
                joined_all[2 * page * ROWS : 2 * (page + 1) * ROWS, at : at + KEYS] = joined.astype(
                    BF16
                )


def table_gradient(by_head, mixed):
    heads = len(by_head)
    for h in range(heads):
        mixed[pl.ds(h, ROWS, stride=heads), :] = by_head[h]
    wide = None
    for r in range(WIN):
        part = mixed[r * WIN * heads : (r + 1) * WIN * heads, :]
        part = jnp.concatenate([part, jnp.zeros_like(part)], 1)
        shift = (WIN - 1 - r) * WIN
        part = pltpu.roll(part, shift, 1) if shift else part
        wide = part if wide is None else wide + part
    high, rest = split_rows(wide)
    squeeze = squeeze_matrix()
    moved = dot_bt(high, squeeze) + dot_bt(rest, squeeze)
    total = None
    for c in range(WIN):
        part = moved[c * heads : (c + 1) * heads]
        shift = WIN - 1 - c
        part = pltpu.roll(part, shift, 1) if shift else part
        total = part if total is None else total + part
    return total


def collect(buf, mine, other, planes, first, size):
    core, spot = core_and_spot()
    stride = mine.shape[0] // planes
    for c, pieces in ((core, mine), (1 - core, other)):
        for k in range(planes):
            at = pl.multiple_of((c * planes + (spot ^ k)) * size, 16)
            buf[pl.ds(at, size), :] = pieces[k * stride + first : k * stride + first + size, :].astype(
                F32
            )


def gradient_kernel(total, planes, count_row, first, size, mine, up, side, corner, stays, grad):
    _, spot = core_and_spot()
    stride = mine.shape[0] // planes
    count = 0.0
    for row in (count_row, count_row + VECTORS):
        piece, at = row // size, row % size
        start = (spot ^ piece) * stride + first + at // 16 * 16
        block = mine[pl.ds(pl.multiple_of(start, 16), 16), :].astype(F32)
        count = count + block[at % 16 : at % 16 + 1]
    wide = (total / count).reshape(1, 1, 1, count.shape[1])
    rest = up.shape[0]
    grad[:rest, :SHIFT] = corner[...].astype(F32) * wide
    grad[:rest, SHIFT:] = up[...].astype(F32) * wide
    grad[rest:, :SHIFT] = side[SHIFT:].astype(F32) * wide
    grad[rest:, SHIFT:] = stays[...] * wide


def finish_kernel(
    total, planes, sizes, mine, other,
    fc1, fc2, proj, fc1_b, g2, b2, fc2_b, proj_b, qkv, g1, b1, q_b, v_b, rel, buf1, buf2,
):
    collect(buf1, mine, other, planes, 0, sizes[0])
    collect(buf2, mine, other, planes, sizes[0], sizes[1])
    d = proj.shape[0]
    ff = fc1.shape[1] // d
    half, at = buf2.shape[0] // 2, 3 * d // 2
    rows = buf2[at : at + VECTORS, :] + buf2[at + VECTORS : at + 2 * VECTORS, :]
    scale = total / rows[ff + 8 : ff + 9, :]
    rows = rows * scale
    for j in range(ff):
        fc1[:, j * d : (j + 1) * d] = buf1[j * d : (j + 1) * d, :] * scale
        fc2[j * d : (j + 1) * d, :] = buf1[(ff + j) * d : (ff + j + 1) * d, :] * scale
        fc1_b[:, j * d : (j + 1) * d] = rows[4 + j : 5 + j]
    proj[...] = buf1[2 * ff * d : (2 * ff + 1) * d, :] * scale
    for k, ref in enumerate((g2, b2, fc2_b, proj_b)):
        ref[...] = rows[ff + 4 + k : ff + 5 + k]
    for j in range(6):
        at = j // 3 * half + j % 3 * (d // 2)
        part = slice(j % 2 * (d // 2), (j % 2 + 1) * (d // 2))
        qkv[part, j // 2 * d : (j // 2 + 1) * d] = buf2[at : at + d // 2, :] * scale
    for k, ref in enumerate((g1, b1, q_b, v_b)):
        ref[...] = rows[k : k + 1]
    heads = rel.shape[0]
    rel[:, :d] = rows[16 : 16 + heads]
    rel[:, d:] = rows[16 + heads : 16 + 2 * heads, : rel.shape[1] - d]


def permute(block, target):
    rows, cols = lax.axis_size("rows"), lax.axis_size("cols")
    route = []
    for r in range(rows):
        for c in range(cols):
            tr, tc = target(r, c)
            route.append((r * cols + c, (tr % rows) * cols + tc % cols))
    return lax.ppermute(block, ("rows", "cols"), route)


def after(values, done):
    return lax.optimization_barrier((values, done))[0]


def core_hop(r, c):
    return r ^ 1, c


def plane_hop(k):
    cols = lax.axis_size("cols")
    return lambda r, c: (r ^ (2 * (k // cols)), c ^ (k % cols))


def plane_share(pieces):
    return [pieces[0]] + [permute(p, plane_hop(k)) for k, p in enumerate(pieces) if k]


def depth_sum(piece):
    hop = 4
    while hop < lax.axis_size("rows"):
        piece = sum_call([piece, permute(piece, lambda r, c, hop=hop: (r ^ hop, c))])
        hop *= 2
    return piece


def strip_hops():
    return [lambda r, c: (r - 1, c), lambda r, c: (r, c - 1), lambda r, c: (r - 1, c - 1)]


def in_vmem():
    return pl.BlockSpec(memory_space=pltpu.VMEM)


def to_vmem(a):
    return pltpu.with_memory_space_constraint(a, pltpu.VMEM)


def limit(mib):
    return pltpu.CompilerParams(vmem_limit_bytes=mib * 1024 * 1024)


def strip_shapes(field):
    rows, cols, pages, d = field.shape
    return [
        pltpu.VMEM(s, BF16)
        for s in (
            (SHIFT, cols, pages, d), (rows - SHIFT, SHIFT, pages, d), (SHIFT, SHIFT, pages, d)
        )
    ]


def in_hbm():
    return pl.BlockSpec(memory_space=pltpu.HBM)


def to_hbm(a):
    return pltpu.with_memory_space_constraint(a, pltpu.HBM)


def strips_call(field):
    return pl.pallas_call(
        strips_kernel,
        in_specs=[in_hbm()],
        out_specs=[in_vmem()] * 3,
        out_shape=strip_shapes(field),
        scratch_shapes=[pltpu.SemaphoreType.DMA((3,))],
        compiler_params=limit(4),
        name="input_strips",
    )(to_hbm(field))


def target_call(target, kept, table):
    return pl.pallas_call(
        target_kernel,
        in_specs=[in_hbm()] * 3,
        out_specs=[in_vmem()] * 6,
        out_shape=[
            pltpu.VMEM(target.shape, BF16), *strip_shapes(target),
            pltpu.VMEM((1, target.shape[-1]), F32), pltpu.VMEM(table.shape, F32),
        ],
        scratch_shapes=[
            pltpu.VMEM(target.shape, BF16), pltpu.VMEM(kept.shape, kept.dtype),
            pltpu.SemaphoreType.DMA((3,)),
        ],
        compiler_params=limit(8),
        name="masked_target",
    )(*map(to_hbm, (target, kept, table)))


def split_call(mine, other):
    planes = 2 * lax.axis_size("cols")
    n, d = mine.shape
    return pl.pallas_call(
        split_kernel,
        in_specs=[in_vmem()] * 2,
        out_specs=[in_vmem()] * planes,
        out_shape=[pltpu.VMEM((n // planes, d), BF16)] * planes,
        compiler_params=limit(4),
        name="split_sums",
    )(*map(to_vmem, (mine, other)))


def local_call(kernel, rows, parts, name):
    return pl.pallas_call(
        kernel,
        in_specs=[in_vmem()] * len(parts),
        out_specs=in_vmem(),
        out_shape=pltpu.VMEM((rows,) + parts[-1].shape[1:], BF16),
        compiler_params=limit(4),
        name=name,
    )(*map(to_vmem, parts))


def sum_call(parts):
    return local_call(sum_kernel, parts[0].shape[0], parts, "add_pieces")


def join_call(parts):
    return local_call(join_kernel, sum(a.shape[0] for a in parts), parts, "join_pieces")


def bias_call(rel_table):
    heads = rel_table.shape[0]
    return pl.pallas_call(
        bias_kernel,
        in_specs=[in_vmem()],
        out_specs=in_vmem(),
        out_shape=pltpu.VMEM((2, PAD_ROWS * heads, KEYS), F32),
        scratch_shapes=[pltpu.VMEM((heads, RELS), F32)],
        compiler_params=limit(VMEM_LIMIT),
        name="attention_bias",
    )(to_vmem(rel_table))


def cost(flops):
    return pl.CostEstimate(flops=flops, bytes_accessed=10**7, transcendentals=10**6)


def attention_call(patches, p_strips, qkv_w, bias, g1, b1, q_b, v_b):
    pages, d = patches.shape[2:]
    heads = bias.shape[1] // ROWS
    tokens = 2 * TOK * pages
    shape = pltpu.VMEM
    inputs = [patches, *p_strips, qkv_w, bias, g1, b1, q_b, v_b]
    outs = [
        shape((tokens, d), BF16),
        shape((2 * pages * ROWS, d), BF16),
        shape((2, pages, KEYS, 3 * d), BF16),
        shape((2, pages, heads * ROWS, KEYS), BF16),
        shape((d // KEYS, 2, PAD_ROWS * pages, KEYS), F32),
    ]
    return pl.pallas_call(
        attention_kernel,
        in_specs=[in_vmem()] * len(inputs),
        out_specs=[in_vmem()] * len(outs),
        out_shape=outs,
        scratch_shapes=[pltpu.VMEM((d // KEYS, 2, PAD_ROWS * pages, KEYS), F32)],
        compiler_params=limit(VMEM_LIMIT),
        cost_estimate=cost(10**10),
        name="attention_forward",
    )(*map(to_vmem, inputs))


def mlp_call(size, x, mixed, masked, t_strips, count, *weights):
    height, width, pages, d = masked.shape
    ff = weights[1].shape[1]
    shape = pltpu.VMEM
    inputs = [x, mixed, masked, *t_strips, count, *weights]
    rest = WIN - SHIFT
    outs = [
        shape((SHIFT, width - SHIFT, pages, d), BF16), shape((rest, width - SHIFT, pages, d), BF16),
        shape((SHIFT, SHIFT, pages, d), BF16), shape((rest, SHIFT, pages, d), BF16),
        shape((d // KEYS, 2, PAD_ROWS * pages, KEYS), F32),
        shape((d // KEYS, 2, PAD_ROWS * pages, KEYS), F32),
        shape((16, d), F32), shape((size // 2, d), BF16), shape((size // 2, d), BF16),
    ]
    return pl.pallas_call(
        mlp_kernel,
        in_specs=[in_vmem()] * len(inputs),
        out_specs=[in_vmem()] * len(outs),
        out_shape=outs,
        scratch_shapes=[
            pltpu.VMEM((height, width, pages, d), BF16),
            pltpu.VMEM((size, d), BF16),
            pltpu.VMEM((d // KEYS, 2, PAD_ROWS * pages, KEYS), F32),
            pltpu.VMEM((d, ff), F32),
            pltpu.VMEM((ff, d), F32),
            pltpu.VMEM((d, d), F32),
            pltpu.VMEM((8, ff), F32),
            pltpu.VMEM((4, 8, d), F32),
        ],
        compiler_params=limit(VMEM_LIMIT),
        cost_estimate=cost(10**10),
        name="mlp_forward_backward",
    )(*map(to_vmem, inputs))


def backward_call(size, xw, qkv, probs, dy, do, *more):
    pages, d = probs.shape[1], xw.shape[1]
    heads = probs.shape[2] // ROWS
    shape = pltpu.VMEM
    inputs = [xw, qkv, probs, dy, do, *more]
    rest = WIN - SHIFT
    outs = [
        shape((SHIFT, 2 * WIN - SHIFT, pages, d), F32), shape((2 * SHIFT, SHIFT, pages, d), BF16),
        shape((rest, SHIFT, pages, d), BF16),
        shape((rest, 2 * WIN - SHIFT, pages, d), BF16), shape((size // 2, d), BF16),
        shape((size // 2, d), BF16),
    ]
    return pl.pallas_call(
        backward_kernel,
        in_specs=[in_vmem()] * len(inputs),
        out_specs=[in_vmem()] * len(outs),
        out_shape=outs,
        scratch_shapes=[
            shape((d // KEYS, 2, PAD_ROWS * pages, KEYS), F32),
            shape((d, 3 * d), F32),
            shape((ROWS, heads * KEYS), F32),
            shape((8, 3 * d), F32),
            shape((2, 8, d), F32),
            shape((PAD_ROWS * heads, KEYS), F32),
            shape((size, d), BF16),
            shape((2 * pages * ROWS, 3 * d), BF16),
        ],
        compiler_params=limit(VMEM_LIMIT),
        cost_estimate=cost(10**10),
        name="attention_backward",
    )(*map(to_vmem, inputs))


def gradient_call(total, planes, ff, n1, n2, *inputs):
    d = inputs[0].shape[1]
    first, size = n1 // (2 * planes), n2 // (2 * planes)
    count_row = 3 * d // 2 + ff // d + 8
    return pl.pallas_call(
        lambda *refs: gradient_kernel(total, planes, count_row, first, size, *refs),
        in_specs=[in_vmem()] * len(inputs),
        out_shape=jax.ShapeDtypeStruct((WIN, 2 * WIN) + inputs[1].shape[2:], F32),
        compiler_params=limit(VMEM_LIMIT),
        name="input_gradient",
    )(*map(to_vmem, inputs))


def finish_call(total, planes, ff, n1, n2, rel_shape, *inputs):
    d = inputs[0].shape[1]
    row = (1, d)
    shapes = [(d, ff), (ff, d), (d, d), (1, ff), row, row, row, row, (d, 3 * d)]
    shapes += [row, row, row, row, rel_shape]
    sizes = (n1 // (2 * planes), n2 // (2 * planes))
    return pl.pallas_call(
        lambda *refs: finish_kernel(total, planes, sizes, *refs),
        in_specs=[in_vmem()] * len(inputs),
        out_shape=[jax.ShapeDtypeStruct(s, F32) for s in shapes],
        scratch_shapes=[pltpu.VMEM((n1, d), F32), pltpu.VMEM((n2, d), F32)],
        compiler_params=limit(VMEM_LIMIT),
        name="finish_sums",
    )(*map(to_vmem, inputs))


def shards(
    patches, target, kept_mask, ln1_gain, ln1_bias, qkv_weight, query_bias, value_bias, rel_table,
    proj_weight, proj_bias, ln2_gain, ln2_bias, fc1_weight, fc1_bias, fc2_weight, fc2_bias,
):
    pages, height, width, d = patches.shape
    ff = fc1_weight.shape[1]
    rows, cols = lax.axis_size("rows"), lax.axis_size("cols")
    planes = 2 * cols
    step = 32 * planes
    tokens = pages * height * width
    vec = lambda a: a.reshape(1, -1)
    n1 = -(-(2 * ff + d) // step) * step
    n2 = -(-(3 * d + 4 * VECTORS) // step) * step

    patches = patches.transpose(1, 2, 0, 3)
    p_strips = [permute(a, hop) for a, hop in zip(strips_call(patches), strip_hops())]
    masked, *t_strips, count, table = target_call(
        target.transpose(1, 2, 0, 3), kept_mask.transpose(1, 0, 2), rel_table
    )
    t_strips = [permute(a, hop) for a, hop in zip(t_strips, strip_hops())]
    bias = bias_call(table)

    g1, b1 = vec(ln1_gain), vec(ln1_bias)
    x, xw, qkv, probs, mixed = attention_call(
        patches, p_strips, qkv_weight, bias, g1, b1, vec(query_bias), vec(value_bias)
    )
    out_stays, out_up, out_side, out_corner, dy, do, mlp_rows, mine, other = mlp_call(
        n1, x, mixed, masked, t_strips, count, proj_weight, fc1_weight, fc2_weight,
        vec(proj_bias), vec(ln2_gain), vec(ln2_bias), vec(fc1_bias), vec(fc2_bias),
    )

    to_right, to_below = (lambda r, c: (r, c + 1)), (lambda r, c: (r + 1, c))
    across = lambda r, c: (r + 1, c + 1)
    out_up, out_corner = permute(out_up, to_below), permute(out_corner, across)

    pieces = split_call(mine, permute(other, core_hop))
    got = plane_share(pieces)
    do = after(do, pieces)
    stays, side, corner, up, mine2, other2 = backward_call(
        n2, xw, qkv, probs, dy, do, qkv_weight, g1, b1, out_side, mlp_rows
    )
    got, out_up, out_corner = after((got, out_up, out_corner), mine2)
    piece = sum_call(got)
    mine2, other2, up, out_up, out_corner = after(
        (mine2, other2, up, out_up, out_corner), piece
    )

    pieces2 = split_call(mine2, permute(other2, core_hop))
    piece2 = sum_call(plane_share(pieces2))
    up, side, corner = after((up, side, corner), piece2)
    piece = join_call([piece, piece2])
    up, side, corner = permute(up, to_below), permute(side, to_right), permute(corner, across)
    piece = depth_sum(piece)
    piece, up, side, corner = after((piece, up, side, corner), up)
    mine = join_call(plane_share([piece] * planes))
    other = permute(mine, core_hop)
    top = jnp.concatenate([out_corner, out_up], 1)
    bottom = jnp.concatenate([side[:SHIFT], out_stays], 1)
    output = jnp.concatenate([top, bottom], 0)
    mine, output = after((mine, output), output)
    total = float(tokens * rows * cols)
    grad = gradient_call(total, planes, ff, n1, n2, mine, up, side, corner, stays)
    other, grad = after((other, grad), grad)
    (
        fc1_g, fc2_g, proj_g, fc1_bg, g2_g, b2_g, fc2_bg, proj_bg, qkv_g, g1_g, b1_g, q_bg,
        v_bg, rel_g,
    ) = finish_call(
        total, planes, ff, n1, n2, rel_table.shape, mine, other
    )
    flat = lambda a: a.reshape(-1)
    return (
        output.transpose(2, 0, 1, 3),
        grad.transpose(2, 0, 1, 3),
        flat(g1_g),
        flat(b1_g),
        qkv_g,
        flat(q_bg),
        flat(v_bg),
        rel_g,
        proj_g,
        flat(proj_bg),
        flat(g2_g),
        flat(b2_g),
        fc1_g,
        flat(fc1_bg),
        fc2_g,
        flat(fc2_bg),
    )


def solution(mesh):
    field = P(None, "rows", "cols", None)
    return jax.shard_map(
        shards,
        mesh=mesh,
        in_specs=(field, field, P(None, "rows", "cols")) + (P(),) * 14,
        out_specs=(field, field) + (P(),) * 14,
        check_vma=False,
    )
```
